128 devices in a mesh: fsdp: 4 (over x), ctx: 16 (over z, y), tp: 2 (over core).
Axes of the slice: x: 4, y: 4, z: 4, core: 2. Of those that a mesh axis runs over, the one named last changes fastest.
Arguments:
- block_input: float32 [16384, 1024], P(('fsdp', 'ctx')), may hold values from -6 to 6
- cotangent: float32 [16384, 1024], P(('fsdp', 'ctx')), may hold values from -6 to 6
- lengths: int32 [4, 8], P('fsdp'), may hold values from 1 to 3968, 4096 in all within a row
- w_in: float32 [2, 1024, 2, 2060], P(None, ('fsdp', 'ctx'), 'tp'), may hold values from -0.1875 to 0.1875
- w_out: float32 [2, 2, 1024, 1024], P(None, 'tp', None, ('fsdp', 'ctx'))
- w_gu: float32 [2, 1024, 2, 2048], P(None, ('fsdp', 'ctx'), 'tp'), may hold values from -0.1875 to 0.1875
- w_down: float32 [2, 2, 1024, 1024], P(None, 'tp', None, ('fsdp', 'ctx')), may hold values from -0.125 to 0.125
- vectors: float32 [2, 2, 5284], P(None, 'tp')
- norm_gains: float32 [2, 2, 1024], replicated, may hold values from 0.5 to 1.5
- first_in: float32 [2, 1024, 2, 2060], P(None, ('fsdp', 'ctx'), 'tp')
- first_out: float32 [2, 2, 1024, 1024], P(None, 'tp', None, ('fsdp', 'ctx'))
- first_gu: float32 [2, 1024, 2, 2048], P(None, ('fsdp', 'ctx'), 'tp')
- first_down: float32 [2, 2, 1024, 1024], P(None, 'tp', None, ('fsdp', 'ctx'))
- first_vectors: float32 [2, 2, 5284], P(None, 'tp')
- first_gains: float32 [2, 2, 1024], replicated
- second_in: float32 [2, 1024, 2, 2060], P(None, ('fsdp', 'ctx'), 'tp')
- second_out: float32 [2, 2, 1024, 1024], P(None, 'tp', None, ('fsdp', 'ctx'))
- second_gu: float32 [2, 1024, 2, 2048], P(None, ('fsdp', 'ctx'), 'tp')
- second_down: float32 [2, 2, 1024, 1024], P(None, 'tp', None, ('fsdp', 'ctx'))
- second_vectors: float32 [2, 2, 5284], P(None, 'tp')
- second_gains: float32 [2, 2, 1024], replicated
Outputs:
- block_output: float32 [16384, 1024], P(('fsdp', 'ctx'))
- input_grad: float32 [16384, 1024], P(('fsdp', 'ctx'))
- new_first_in: float32 [2, 1024, 2, 2060], P(None, ('fsdp', 'ctx'), 'tp')
- new_second_in: float32 [2, 1024, 2, 2060], P(None, ('fsdp', 'ctx'), 'tp')
- new_w_in: float32 [2, 1024, 2, 2060], P(None, ('fsdp', 'ctx'), 'tp')
- new_first_out: float32 [2, 2, 1024, 1024], P(None, 'tp', None, ('fsdp', 'ctx'))
- new_second_out: float32 [2, 2, 1024, 1024], P(None, 'tp', None, ('fsdp', 'ctx'))
- new_w_out: float32 [2, 2, 1024, 1024], P(None, 'tp', None, ('fsdp', 'ctx'))
- new_first_gu: float32 [2, 1024, 2, 2048], P(None, ('fsdp', 'ctx'), 'tp')
- new_second_gu: float32 [2, 1024, 2, 2048], P(None, ('fsdp', 'ctx'), 'tp')
- new_w_gu: float32 [2, 1024, 2, 2048], P(None, ('fsdp', 'ctx'), 'tp')
- new_first_down: float32 [2, 2, 1024, 1024], P(None, 'tp', None, ('fsdp', 'ctx'))
- new_second_down: float32 [2, 2, 1024, 1024], P(None, 'tp', None, ('fsdp', 'ctx'))
- new_w_down: float32 [2, 2, 1024, 1024], P(None, 'tp', None, ('fsdp', 'ctx'))
- new_first_vectors: float32 [2, 2, 5284], P(None, 'tp')
- new_second_vectors: float32 [2, 2, 5284], P(None, 'tp')
- new_vectors: float32 [2, 2, 5284], P(None, 'tp')
- new_first_gains: float32 [2, 2, 1024], replicated
- new_second_gains: float32 [2, 2, 1024], replicated
- new_norm_gains: float32 [2, 2, 1024], replicated
The draws below stay inside these ranges and needn't reach their ends.
Inputs may be any that keep to these rules, and one draw needn't show every extreme that they name: Row f holds the lengths of the 8 documents of sequence f in order; they sum to 4096.
All inputs are finite; a program needn't handle non-finite values.
Results may differ from the reference program's by a relative error of at most 0.03.
Values may be sent and summed in bfloat16 or wider, within the bound.
A program may use at most 384 MiB of HBM per device.

```python
import math
import jax
import jax.numpy as jnp
import numpy as np
from jax import lax

D = 1024
KV_HEADS = 2
HD = 64
MAMBA_HEAD_SIZE = 64
MAMBA_STATE_SIZE = 128
CONV = 4
FF = 2048
LAYERS = 2
DOCS = 8
STEP = 10
SPAN = 256
RANKS = 2
QR = 256
DSR = 768
BCR = 128
MHR = 12
CH_RANK = 896
IN_RANK = 2060
OUT_RANK = 1024
FFR = 1024
VEC = 5284
SEQ = 4096
TOKENS = 16384
N_FSDP = 4


def first_moment(key, array_shape, scale):
    return jax.random.truncated_normal(key, -4.0, 4.0, array_shape, jnp.float32) * (scale / 9.0)


def second_moment(key, array_shape, scale):
    level_key, spread_key = jax.random.split(key)
    levels = jax.random.uniform(level_key, array_shape, jnp.float32, 1.0, 4.0)
    spread = jnp.exp(jax.random.uniform(spread_key, array_shape, jnp.float32, -0.69, 0.69))
    return levels * spread * (scale * scale / 19.0)


def matrix_scale():
    return 0.5 * TOKENS ** 0.5


def vector_scale():
    return TOKENS ** 0.5


def draw_w_out(key, part):
    key = jax.random.fold_in(key, 1)
    values = jax.random.truncated_normal(key, -6.0, 6.0, (LAYERS, RANKS, OUT_RANK, D), jnp.float32)
    row_index = jnp.arange(OUT_RANK)
    factor = jnp.where(row_index < OUT_RANK - DSR, 8.0, 1.0)
    return values * factor[None, None, :, None] / (RANKS * OUT_RANK) ** 0.5


def draw_vectors(key, part):
    key = jax.random.fold_in(key, 2)
    keys_all = jax.random.split(key, 6)
    leading = (LAYERS, RANKS)
    conv_taps = jax.random.truncated_normal(keys_all[0], -3.0, 3.0, leading + (CONV * CH_RANK,), jnp.float32) * 0.5
    conv_bias = jax.random.uniform(keys_all[1], leading + (CH_RANK,), jnp.float32, -0.5, 0.5)
    gated_gain = jax.random.uniform(keys_all[2], leading + (DSR,), jnp.float32, 0.6, 1.4)
    fraction = jax.random.uniform(keys_all[3], leading + (MHR,), jnp.float32, 0.0, 1.0)
    rising = 0.75
    floor_log = math.log(20.0 / SEQ)
    a_log = floor_log + fraction * (math.log(0.5) - floor_log)
    dt_bias = jax.random.uniform(keys_all[4], leading + (MHR,), jnp.float32, -3.5, -2.5)
    rank_factor = 1.0 + rising * jnp.arange(RANKS, dtype=jnp.float32) / max(RANKS - 1, 1)
    d_skip = jax.random.uniform(keys_all[5], leading + (MHR,), jnp.float32, 1.0, 2.0) * rank_factor[None, :, None]
    return jnp.concatenate([conv_taps, conv_bias, gated_gain, a_log, dt_bias, d_skip], axis=2)


def draw_first_in(key, part):
    key = jax.random.fold_in(key, 11)
    return first_moment(key, (LAYERS, D, RANKS, IN_RANK), matrix_scale())


def draw_first_out(key, part):
    key = jax.random.fold_in(key, 12)
    return first_moment(key, (LAYERS, RANKS, OUT_RANK, D), matrix_scale())


def draw_first_gu(key, part):
    key = jax.random.fold_in(key, 13)
    return first_moment(key, (LAYERS, D, RANKS, 2 * FFR), matrix_scale())


def draw_first_down(key, part):
    key = jax.random.fold_in(key, 14)
    return first_moment(key, (LAYERS, RANKS, FFR, D), matrix_scale())


def draw_first_vectors(key, part):
    key = jax.random.fold_in(key, 15)
    return first_moment(key, (LAYERS, RANKS, VEC), vector_scale())


def draw_first_gains(key, part):
    key = jax.random.fold_in(key, 16)
    return first_moment(key, (LAYERS, 2, D), vector_scale())


def draw_second_in(key, part):
    key = jax.random.fold_in(key, 21)
    return second_moment(key, (LAYERS, D, RANKS, IN_RANK), matrix_scale())


def draw_second_out(key, part):
    key = jax.random.fold_in(key, 22)
    return second_moment(key, (LAYERS, RANKS, OUT_RANK, D), matrix_scale())


def draw_second_gu(key, part):
    key = jax.random.fold_in(key, 23)
    return second_moment(key, (LAYERS, D, RANKS, 2 * FFR), matrix_scale())


def draw_second_down(key, part):
    key = jax.random.fold_in(key, 24)
    return second_moment(key, (LAYERS, RANKS, FFR, D), matrix_scale())


def draw_second_vectors(key, part):
    key = jax.random.fold_in(key, 25)
    return second_moment(key, (LAYERS, RANKS, VEC), vector_scale())


def draw_second_gains(key, part):
    key = jax.random.fold_in(key, 26)
    return second_moment(key, (LAYERS, 2, D), vector_scale())


def block_levels(rng, dims, shards, smallest, high):
    factor_of, own = 1.0, jax.random.fold_in(rng, 6)
    for axis_at, shards_of in shards:
        draws = jnp.exp(jax.random.uniform(jax.random.fold_in(own, axis_at), (shards_of,), jnp.float32, smallest / len(shards), high / len(shards)))
        factor_of = factor_of * jnp.repeat(draws, dims[axis_at] // shards_of).reshape([-1 if axis == axis_at else 1 for axis in range(len(dims))])
    return factor_of


def length_profile(amount, total, bound, skew):
    loads = [(1 << 20) // math.isqrt(grade ** skew) + 1 for grade in range(2, amount + 1)]
    spare, given = total - bound - (amount - 1), [1] * (amount - 1)
    while spare > 0:
        movable = [i for i in range(amount - 1) if given[i] < bound]
        whole, remaining = sum([loads[i] for i in movable]), spare
        for i in movable:
            extra = min(bound - given[i], max(1, remaining * loads[i] // whole), spare)
            given[i] = given[i] + extra
            spare = spare - extra
    return np.array([bound] + given)


def uneven(rng, count, total, bound, skew):
    if count == 2:
        one = jax.random.randint(rng, (), max(1, total - bound), min(bound, total - 1) + 1)
        return jnp.stack([one, total - one])
    sizes = jnp.asarray(length_profile(count, total, bound, skew), jnp.int32)
    twos = (count - 1) // 2
    donor, taker = sizes[1:1 + 2 * twos:2], sizes[2:2 + 2 * twos:2]
    slack = jnp.minimum(donor - 1, bound - taker)
    passed = jax.random.randint(jax.random.fold_in(rng, 1), (twos,), 0, 1 << 20) % (slack + 1)
    sizes = sizes.at[1:1 + 2 * twos:2].set(donor - passed).at[2:2 + 2 * twos:2].set(taker + passed)
    return sizes[jax.random.permutation(jax.random.fold_in(rng, 2), count)]


def bell_draw(rng, extent, scale, reach, shards=(), kind=jnp.bfloat16):
    array = scale * jax.random.normal(rng, extent, jnp.float32)
    if shards:
        array = array * block_levels(rng, extent, shards, -0.22, 0.18)
    return jnp.clip(array, -reach, reach).astype(kind)


def setup_inputs(seed: int = 0) -> dict:
    key_of = jax.random.split(jax.random.key(seed), 22)
    block_input = bell_draw(key_of[0], (TOKENS, D), 1.0, 6.0, ((0, 64),), jnp.float32)
    cotangent = bell_draw(key_of[1], (TOKENS, D), 1.0, 6.0, ((0, 64),), jnp.float32)
    lengths = jax.vmap(lambda own: uneven(own, DOCS, SEQ, SEQ - SPAN // 2, 0))(jax.random.split(key_of[2], N_FSDP)).reshape((N_FSDP, DOCS)).astype(jnp.int32)
    w_in = bell_draw(key_of[3], (LAYERS, D, RANKS, IN_RANK), D ** -0.5, 0.1875, ((1, 64), (2, 2)), jnp.float32)
    w_out = draw_w_out(jax.random.fold_in(key_of[21], 71), 0)
    w_gu = bell_draw(key_of[5], (LAYERS, D, RANKS, 2 * FFR), D ** -0.5, 0.1875, ((1, 64), (2, 2)), jnp.float32)
    w_down = bell_draw(key_of[6], (LAYERS, RANKS, FFR, D), FF ** -0.5, 0.125, ((1, 2), (3, 64)), jnp.float32)
    vectors = draw_vectors(jax.random.fold_in(key_of[21], 71), 0)
    norm_gains = jnp.clip(1.0 + 0.1 * jax.random.normal(key_of[8], (LAYERS, 2, D), jnp.float32), 0.5, 1.5)
    first_in = draw_first_in(jax.random.fold_in(key_of[21], 71), 0)
    first_out = draw_first_out(jax.random.fold_in(key_of[21], 71), 0)
    first_gu = draw_first_gu(jax.random.fold_in(key_of[21], 71), 0)
    first_down = draw_first_down(jax.random.fold_in(key_of[21], 71), 0)
    first_vectors = draw_first_vectors(jax.random.fold_in(key_of[21], 71), 0)
    first_gains = draw_first_gains(jax.random.fold_in(key_of[21], 71), 0)
    second_in = draw_second_in(jax.random.fold_in(key_of[21], 71), 0)
    second_out = draw_second_out(jax.random.fold_in(key_of[21], 71), 0)
    second_gu = draw_second_gu(jax.random.fold_in(key_of[21], 71), 0)
    second_down = draw_second_down(jax.random.fold_in(key_of[21], 71), 0)
    second_vectors = draw_second_vectors(jax.random.fold_in(key_of[21], 71), 0)
    second_gains = draw_second_gains(jax.random.fold_in(key_of[21], 71), 0)
    return dict(block_input=block_input, cotangent=cotangent, lengths=lengths, w_in=w_in, w_out=w_out, w_gu=w_gu, w_down=w_down, vectors=vectors, norm_gains=norm_gains, first_in=first_in, first_out=first_out, first_gu=first_gu, first_down=first_down, first_vectors=first_vectors, first_gains=first_gains, second_in=second_in, second_out=second_out, second_gu=second_gu, second_down=second_down, second_vectors=second_vectors, second_gains=second_gains)


highest = lax.Precision.HIGHEST
norm_eps = 1e-05
rope_base = 100000000000.0
masked_value = -1e+30
beta_one = 0.9
beta_two = 0.95
adam_eps = 1e-08
decay_rate = 0.1
rate_matrix = 0.05
rate_vector = 0.5

@jax.custom_vjp
def low(v):
    return lax.optimization_barrier(v.astype(jnp.bfloat16)).astype(jnp.float32)

@jax.custom_vjp
def low_back(v):
    return v

def low_keep(v):
    return (low(v), None)

def low_pass(kept, grad):
    return (grad,)

def back_keep(v):
    return (v, None)

def back_low(kept, grad):
    return (low(grad),)
low.defvjp(low_keep, low_pass)
low_back.defvjp(back_keep, back_low)

def rms_norm(value, gain):
    return value * lax.rsqrt(lax.optimization_barrier(jnp.mean(value * value, axis=-1, keepdims=True)) + norm_eps) * gain

def doc_layout(doc_row, start_row, item_count):
    ends = jnp.cumsum(doc_row).astype(jnp.int32)
    starts = ends - doc_row
    token_index = start_row + jnp.arange(item_count, dtype=jnp.int32)
    segment = lax.optimization_barrier(jnp.sum((token_index[:, None] >= ends[None, :]).astype(jnp.int32), axis=1))
    picked = segment[:, None] == jnp.arange(doc_row.shape[0], dtype=jnp.int32)[None, :]
    begin = lax.optimization_barrier(jnp.sum(jnp.where(picked, starts[None, :], 0), axis=1)).astype(jnp.int32)
    return (segment, token_index - begin)

def rope_tables(position):
    freq = rope_base ** (-2.0 * jnp.arange(HD // 2, dtype=jnp.float32) / HD)
    angle = position.astype(jnp.float32)[:, None] * freq[None, :]
    return (jnp.cos(angle), jnp.sin(angle))

def rotate(value, cosine, sine):
    shaped = value.reshape(value.shape[0], -1, 2, HD // 2)
    first_half = shaped[:, :, 0]
    second_half = shaped[:, :, 1]
    cos_part = cosine[:, None, :]
    sin_part = sine[:, None, :]
    turned = jnp.stack([first_half * cos_part - second_half * sin_part, second_half * cos_part + first_half * sin_part], axis=2)
    return turned.reshape(value.shape)

def conv_act(extended, conv_taps, conv_bias, seg_ext):
    item_count = extended.shape[0] - (CONV - 1)
    own_seg = seg_ext[CONV - 1:]
    total = conv_bias[None, :] + conv_taps[CONV - 1][None, :] * extended[CONV - 1:]
    for back in range(1, CONV):
        begin = CONV - 1 - back
        same = seg_ext[begin:begin + item_count] == own_seg
        total = total + conv_taps[CONV - 1 - back][None, :] * jnp.where(same[:, None], extended[begin:begin + item_count], 0.0)
    return jax.nn.silu(total)

def decay_terms(drive_input, dt_bias, a_log):
    dt_step = jax.nn.softplus(drive_input + dt_bias)
    return (dt_step, jnp.cumsum(-dt_step * jnp.exp(a_log), axis=0))

def ssd_output(inner_input, b_mat, c_mat, drive_input, dt_bias, a_log, d_skip, segment, position, state_in):
    item_count = inner_input.shape[0]
    head_total = drive_input.shape[1]
    grouped_heads = inner_input.reshape(item_count, head_total, MAMBA_HEAD_SIZE)
    dt_step, log_cum = decay_terms(drive_input, dt_bias, a_log)
    token_order = jnp.arange(item_count, dtype=jnp.int32)
    causal = (token_order[None, :] <= token_order[:, None]) & (segment[None, :] == segment[:, None])
    spread = log_cum.T[:, :, None] - log_cum.T[:, None, :]
    kernel = jnp.where(causal[None], jnp.exp(jnp.where(causal[None], spread, 0.0)), 0.0)
    inner_prod = jnp.dot(c_mat, b_mat.T, precision=highest)
    mixing = kernel * inner_prod[None] * dt_step.T[:, None, :]
    final_result = jnp.einsum('hts,shp->thp', mixing, grouped_heads, precision=highest)
    carry_on = ((segment == segment[0]) & (position[0] != 0)).astype(jnp.float32)
    carried = jnp.einsum('tn,hpn->thp', c_mat, state_in, precision=highest)
    final_result = final_result + carried * (jnp.exp(log_cum) * carry_on[:, None])[:, :, None] + d_skip[None, :, None] * grouped_heads
    return final_result.reshape(item_count, head_total * MAMBA_HEAD_SIZE)

def ssd_summary(inner_input, b_mat, drive_input, dt_bias, a_log, segment, position):
    item_count = inner_input.shape[0]
    head_total = drive_input.shape[1]
    grouped_heads = inner_input.reshape(item_count, head_total, MAMBA_HEAD_SIZE)
    dt_step, log_cum = decay_terms(drive_input, dt_bias, a_log)
    in_last = (segment == segment[item_count - 1]).astype(jnp.float32)
    weight_last = jnp.exp(log_cum[item_count - 1][None, :] - log_cum) * dt_step * in_last[:, None]
    state = jnp.einsum('sh,shp,sn->hpn', weight_last, grouped_heads, b_mat, precision=highest)
    live = ((segment[item_count - 1] == segment[0]) & (position[0] != 0)).astype(jnp.float32)
    return (live * jnp.exp(log_cum[item_count - 1]), state)

def split_vector(vector, widths):
    q_width, k_width, s_width, b_width, h_width = widths
    channels = s_width + b_width
    conv_taps = vector[:CONV * channels].reshape(CONV, channels)
    offset = CONV * channels
    conv_bias = vector[offset:offset + channels]
    offset = offset + channels
    gated_gain = vector[offset:offset + s_width]
    offset = offset + s_width
    return (conv_taps, conv_bias, gated_gain, vector[offset:offset + h_width], vector[offset + h_width:offset + 2 * h_width], vector[offset + 2 * h_width:offset + 3 * h_width])

def attend(queries, keys, values, allowed):
    length = queries.shape[0]
    blocks = length // SPAN
    grouped_heads = queries.reshape(blocks, SPAN, -1, HD)
    masks = allowed.reshape(blocks, SPAN, length)

    def one_block(item):
        query_block, mask_block = item
        raw = low_back(jnp.einsum('tgd,sd->gts', query_block, keys, precision=highest))
        logits = jnp.where(mask_block[None], raw * HD ** (-0.5), masked_value)
        top = lax.optimization_barrier(jnp.max(logits, axis=2, keepdims=True))
        log_total = top + jnp.log(lax.optimization_barrier(jnp.sum(jnp.exp(logits - top), axis=2, keepdims=True)))
        prob = low(jnp.exp(logits - log_total))
        return jnp.einsum('gts,sd->tgd', prob, values, precision=highest)
    final_result = lax.map(jax.checkpoint(one_block), (grouped_heads, masks))
    return final_result.reshape(length, -1)

def ssd_sequence(inner_input, b_mat, c_mat, drive_input, dt_bias, a_log, d_skip, segment, position):
    length = inner_input.shape[0]
    blocks = length // SPAN

    def split_blocks(value):
        return value.reshape((blocks, SPAN) + value.shape[1:])

    def advance(carry, item):
        x_part, b_part, c_part, drive_part, seg_part, pos_part = item
        final_result = ssd_output(x_part, b_part, c_part, drive_part, dt_bias, a_log, d_skip, seg_part, pos_part, carry)
        decay, state = ssd_summary(x_part, b_part, drive_part, dt_bias, a_log, seg_part, pos_part)
        return (decay[:, None, None] * carry + state, final_result)
    initial_state = jnp.zeros((drive_input.shape[1], MAMBA_HEAD_SIZE, MAMBA_STATE_SIZE), jnp.float32)
    items = (split_blocks(inner_input), split_blocks(b_mat), split_blocks(c_mat), split_blocks(drive_input), split_blocks(segment), split_blocks(position))
    final_state, outputs = lax.scan(jax.checkpoint(advance), initial_state, items)
    return outputs.reshape(length, -1)

def layer_forward(state, layer_params, segment, position, cosine, sine):
    w_in, w_out, w_gu, w_down, vectors, gains = layer_params
    length = state.shape[0]
    k_width = KV_HEADS * HD // RANKS
    widths = (QR, k_width, DSR, BCR, MHR)
    at_v = QR + k_width
    at_z = at_v + k_width
    at_x = at_z + DSR
    at_t = at_x + CH_RANK
    hidden = low(rms_norm(state, gains[0]))
    proj = low_back(jnp.dot(hidden, low(w_in.reshape(D, RANKS * IN_RANK)), precision=highest)).reshape(length, RANKS, IN_RANK)
    token_index = jnp.arange(length, dtype=jnp.int32)
    allowed = (token_index[None, :] <= token_index[:, None]) & (segment[None, :] == segment[:, None])
    seg_ext = jnp.concatenate([jnp.full((CONV - 1,), -1, jnp.int32), segment])
    attn_parts = []
    x_parts = []
    bc_parts = []
    z_parts = []
    drive_parts = []
    gain_parts = []
    log_parts = []
    bias_parts = []
    skip_parts = []
    for rank in range(RANKS):
        piece = proj[:, rank]
        conv_taps, conv_bias, gated_gain, a_log, dt_bias, d_skip = split_vector(vectors[rank], widths)
        queries = low(rotate(piece[:, :QR], cosine, sine))
        keys = low(rotate(piece[:, QR:at_v], cosine, sine))
        values = low(piece[:, at_v:at_z])
        attn_parts.append(low_back(attend(queries, keys, values, allowed)))
        extended = jnp.concatenate([jnp.zeros((CONV - 1, CH_RANK), jnp.float32), piece[:, at_x:at_t]], axis=0)
        active = conv_act(extended, conv_taps, conv_bias, seg_ext)
        x_parts.append(active[:, :DSR])
        bc_parts.append(active[:, DSR:])
        z_parts.append(piece[:, at_z:at_x])
        drive_parts.append(piece[:, at_t:])
        gain_parts.append(gated_gain)
        log_parts.append(a_log)
        bias_parts.append(dt_bias)
        skip_parts.append(d_skip)
    both = jnp.concatenate(bc_parts, axis=1)
    ssm = ssd_sequence(jnp.concatenate(x_parts, axis=1), both[:, :MAMBA_STATE_SIZE], both[:, MAMBA_STATE_SIZE:], jnp.concatenate(drive_parts, axis=1), jnp.concatenate(bias_parts), jnp.concatenate(log_parts), jnp.concatenate(skip_parts), segment, position)
    gated = ssm * jax.nn.silu(jnp.concatenate(z_parts, axis=1))
    normed = gated * lax.rsqrt(lax.optimization_barrier(jnp.mean(gated * gated, axis=1, keepdims=True)) + norm_eps) * jnp.concatenate(gain_parts)
    pieces = []
    for rank in range(RANKS):
        pieces.append(attn_parts[rank])
        pieces.append(normed[:, rank * DSR:(rank + 1) * DSR])
    features = low(jnp.concatenate(pieces, axis=1))
    middle = state + low_back(jnp.dot(features, low(w_out.reshape(RANKS * OUT_RANK, D)), precision=highest))
    hidden2 = low(rms_norm(middle, gains[1]))
    upgate = low_back(jnp.dot(hidden2, low(w_gu.reshape(D, RANKS * 2 * FFR)), precision=highest)).reshape(length, RANKS, 2, FFR)
    inner = low(jax.nn.silu(upgate[:, :, 0]) * upgate[:, :, 1]).reshape(length, RANKS * FFR)
    return middle + low_back(jnp.dot(inner, low(w_down.reshape(RANKS * FFR, D)), precision=highest))

def adamw(weight, first_m, second_m, grad, rate, decay):
    first_new = beta_one * first_m + (1.0 - beta_one) * grad
    second_new = beta_two * second_m + (1.0 - beta_two) * grad * grad
    ratio = first_new / (1.0 - beta_one ** STEP) / (jnp.sqrt(second_new / (1.0 - beta_two ** STEP)) + adam_eps)
    return (first_new, second_new, weight - rate * (ratio + decay * weight))

def reference(block_input, cotangent, lengths, w_in, w_out, w_gu, w_down, vectors, norm_gains, first_in, first_out, first_gu, first_down, first_vectors, first_gains, second_in, second_out, second_gu, second_down, second_vectors, second_gains):
    params = (w_in, w_out, w_gu, w_down, vectors, norm_gains)

    def one_sequence(totals, item):
        x_seq, cot_seq, doc_row = item
        segment, position = doc_layout(doc_row, 0, SEQ)
        cosine, sine = rope_tables(position)

        def forward(x_start, weights):
            state = x_start
            for layer_at in range(LAYERS):
                state = layer_forward(state, tuple((weight[layer_at] for weight in weights)), segment, position, cosine, sine)
            return state
        final_result, pull = jax.vjp(forward, x_seq, params)
        d_input, d_params = pull(cot_seq)
        return (jax.tree.map(jnp.add, totals, d_params), (final_result, d_input))
    start_totals = jax.tree.map(jnp.zeros_like, params)
    grads, (outputs, input_grads) = lax.scan(one_sequence, start_totals, (block_input.reshape(N_FSDP, SEQ, D), cotangent.reshape(N_FSDP, SEQ, D), lengths))
    up_in = adamw(w_in, first_in, second_in, grads[0], rate_matrix, decay_rate)
    up_out = adamw(w_out, first_out, second_out, grads[1], rate_matrix, decay_rate)
    up_gu = adamw(w_gu, first_gu, second_gu, grads[2], rate_matrix, decay_rate)
    up_down = adamw(w_down, first_down, second_down, grads[3], rate_matrix, decay_rate)
    up_vec = adamw(vectors, first_vectors, second_vectors, grads[4], rate_vector, 0.0)
    up_gain = adamw(norm_gains, first_gains, second_gains, grads[5], rate_vector, 0.0)
    return (outputs.reshape(TOKENS, D), input_grads.reshape(TOKENS, D), up_in[0], up_in[1], up_in[2], up_out[0], up_out[1], up_out[2], up_gu[0], up_gu[1], up_gu[2], up_down[0], up_down[1], up_down[2], up_vec[0], up_vec[1], up_vec[2], up_gain[0], up_gain[1], up_gain[2])
```

```python
import functools

import jax
import jax.numpy as jnp
from jax import lax
from jax.experimental import pallas as pl
from jax.experimental.pallas import tpu as pltpu
from jax.sharding import Mesh
from jax.sharding import PartitionSpec as P

HEADS = 8
KV_HEADS = 2
HD = 64
MAMBA_HEADS = 24
MAMBA_HEAD_SIZE = 64
MAMBA_STATE_SIZE = 128
CONV = 4
LAYERS = 2
STEP = 10
DSSM = 1536
FSDP_CTX = ("fsdp", "ctx_0", "ctx_1")
CTX = ("ctx_0", "ctx_1")


highest = lax.Precision.HIGHEST
state_precision = lax.Precision.DEFAULT
D = 1024
IN_COLS = 2060
IN_PAD = 2176
AXES = ("fsdp", "ctx_0", "ctx_1")
SIDE = 4
ROWS = 16
STREAMS = (
    (0, 0, 1152, (0, 1, 2), 1),
    (0, 1152, 1024, (0, 1, 2), -1),
    (1, 0, 1024, (1, 2, 0), 1),
    (1, 1024, 1024, (1, 2, 0), -1),
    (2, 0, 1024, (2, 0, 1), 1),
    (3, 0, 1024, (2, 0, 1), -1),
)
WIDTHS = (IN_PAD, 2048, 1024, 1024)
norm_eps = 1e-05
rope_base = 100000000000.0
masked_value = -1e30
beta_one = 0.9
beta_two = 0.95
adam_eps = 1e-08
decay_rate = 0.1
rate_matrix = 0.05
rate_vector = 0.5


def ring_places():
    return tuple(lax.axis_index(a) for a in AXES)


def ring_step(places, axis, by):
    return {AXES[axis]: lax.rem(places[axis] + (by + SIDE), SIDE)}


def greet_neighbours(places):
    barrier = pltpu.get_barrier_semaphore()
    for axis in range(3):
        for by in (1, -1):
            pl.semaphore_signal(
                barrier,
                inc=1,
                device_id=ring_step(places, axis, by),
                device_id_type=pl.DeviceIdType.MESH,
            )
    pl.semaphore_wait(barrier, 6)


def remote(src, dst, send, recv, device):
    return pltpu.make_async_remote_copy(
        src_ref=src,
        dst_ref=dst,
        send_sem=send,
        recv_sem=recv,
        device_id=device,
        device_id_type=pl.DeviceIdType.MESH,
    )


def gather_kernel(*refs):
    shards, full = refs[:4], refs[4:8]
    send, recv, own_sem = refs[8:]
    places = ring_places()
    greet_neighbours(places)
    own = []
    for k in range(4):
        copy = pltpu.make_async_copy(
            shards[k], full[k].at[places[0], places[1], places[2]], own_sem.at[k]
        )
        copy.start()
        own.append(copy)
    started = []

    def region(number, stage, place):
        at, first, width, order, _ = STREAMS[number]
        order = order[::-1]
        index = list(places)
        for axis in order[:stage]:
            index[axis] = slice(None)
        index[order[stage]] = place
        return full[at].at[(*index, slice(None), pl.ds(first, width))]

    def launch(number, stage, kind):
        at, first, width, order, way = STREAMS[number]
        axis = order[::-1][stage]
        here = places[axis]
        if kind == 2:
            source = target = region(number, stage, lax.rem(here + (SIDE - way), SIDE))
        else:
            source = target = region(number, stage, here)
            if stage == 0:
                source = shards[at].at[:, pl.ds(first, width)]
        copy = remote(
            source,
            target,
            send.at[number, stage, kind],
            recv.at[number, stage, kind],
            ring_step(places, axis, -way if kind == 1 else way),
        )
        copy.start()
        started.append(copy)
        return copy

    for stage in range(3):
        if stage == 1:
            for copy in own:
                copy.wait()
        first, back = [], []
        for n in range(6):
            first.append(launch(n, stage, 0))
            back.append(launch(n, stage, 1))
        onward = []
        for n in range(6):
            first[n].wait_recv()
            onward.append(launch(n, stage, 2))
        for n in range(6):
            back[n].wait_recv()
            onward[n].wait_recv()
    for copy in started:
        copy.wait_send()


def gather_weights(parts):
    shapes = [jax.ShapeDtypeStruct((4, 4, 4, ROWS, w), jnp.bfloat16) for w in WIDTHS]
    outs = pl.pallas_call(
        gather_kernel,
        out_shape=shapes,
        in_specs=[pl.BlockSpec(memory_space=pl.ANY)] * 4,
        out_specs=[pl.BlockSpec(memory_space=pl.ANY)] * 4,
        scratch_shapes=[
            pltpu.SemaphoreType.DMA((6, 3, 3)),
            pltpu.SemaphoreType.DMA((6, 3, 3)),
            pltpu.SemaphoreType.DMA((4,)),
        ],
        compiler_params=pltpu.CompilerParams(collective_id=0, has_side_effects=True),
        cost_estimate=pl.CostEstimate(flops=0, bytes_accessed=180000000, transcendentals=0),
        name="gather_weights",
    )(*parts)
    return tuple(o.reshape(D, o.shape[-1]) for o in outs)


def scatter_kernel(*refs):
    grads, small = refs[:4], refs[4]
    outs, small_out = refs[5:11], refs[11]
    ahead, mine = refs[12:18], refs[18:24]
    arrived = (refs[24:30], refs[30:36], refs[36:42])
    small_in, send, recv, own_sem, small_send, small_recv = refs[42:]
    places = ring_places()
    greet_neighbours(places)
    started = []

    def near(axis, by):
        return lax.rem(places[axis] + (by + SIDE), SIDE)

    def block(number, stage, place):
        at, first, width, order, _ = STREAMS[number]
        axis = order[stage]
        if stage == 0:
            index = [slice(None)] * 3
            index[axis] = place
            return grads[at].at[(*index, slice(None), pl.ds(first, width))]
        left = [a for a in range(3) if a != order[0]]
        index = [slice(None)] * 2
        if stage == 2:
            index[left.index(order[1])] = places[order[1]]
        index[left.index(axis)] = place
        return mine[number].at[tuple(index)]

    def launch(number, stage, kind, source):
        axis, way = STREAMS[number][3][stage], STREAMS[number][4]
        copy = remote(
            source,
            arrived[stage][number].at[kind],
            send.at[number, stage, kind],
            recv.at[number, stage, kind],
            ring_step(places, axis, -way if kind == 2 else way),
        )
        copy.start()
        started.append(copy)
        return copy

    def add_into(target, source, stage):
        def one(total, part):
            total[...] = total[...] + part[...]

        if stage == 0:

            def body(k, carry):
                one(target.at[k // 4, k % 4], source.at[k // 4, k % 4])
                return carry

            lax.fori_loop(0, 16, body, 0)
        elif stage == 1:

            def body(k, carry):
                one(target.at[k], source.at[k])
                return carry

            lax.fori_loop(0, 4, body, 0)
        else:
            one(target, source)

    def small_exchange(step):
        axis, odd = step // 2, step % 2
        here = places[axis]
        partner = 3 - here if odd else here + 1 - 2 * lax.rem(here, 2)
        copy = remote(
            small_out,
            small_in.at[step],
            small_send.at[step],
            small_recv.at[step],
            {AXES[axis]: partner},
        )
        copy.start()
        return copy

    def small_finish(copy, step):
        copy.wait_send()
        copy.wait_recv()
        small_out[...] = small_out[...] + small_in[step]

    first, back, local = [], [], []
    for n in range(6):
        axis, way = STREAMS[n][3][0], STREAMS[n][4]
        first.append(launch(n, 0, 0, block(n, 0, near(axis, 2))))
    for n in range(6):
        axis, way = STREAMS[n][3][0], STREAMS[n][4]
        pair = (
            pltpu.make_async_copy(block(n, 0, near(axis, way)), ahead[n], own_sem.at[n, 0]),
            pltpu.make_async_copy(block(n, 0, places[axis]), mine[n], own_sem.at[n, 1]),
        )
        for copy in pair:
            copy.start()
        local.append(pair)
        back.append(launch(n, 0, 2, block(n, 0, near(axis, -way))))
    small_out[...] = small[...]
    for stage in range(3):
        if stage:
            first, back = [], []
            for n in range(6):
                axis, way = STREAMS[n][3][stage], STREAMS[n][4]
                first.append(launch(n, stage, 0, block(n, stage, near(axis, 2))))
                back.append(launch(n, stage, 2, block(n, stage, near(axis, -way))))
        step = small_exchange(2 * stage)
        onward = []
        for n in range(6):
            axis, way = STREAMS[n][3][stage], STREAMS[n][4]
            if stage == 0:
                local[n][0].wait()
                local[n][1].wait()
                target = ahead[n]
            else:
                target = block(n, stage, near(axis, way))
            first[n].wait_recv()
            add_into(target, arrived[stage][n].at[0], stage)
            onward.append(launch(n, stage, 1, target))
        small_finish(step, 2 * stage)
        step = small_exchange(2 * stage + 1)
        for n in range(6):
            axis = STREAMS[n][3][stage]
            target = mine[n] if stage == 0 else block(n, stage, places[axis])
            back[n].wait_recv()
            if stage < 2:
                add_into(target, arrived[stage][n].at[2], stage)
            onward[n].wait_recv()
            if stage < 2:
                add_into(target, arrived[stage][n].at[1], stage)
            else:
                outs[n][...] = target[...].astype(jnp.float32) + (
                    arrived[2][n][1].astype(jnp.float32) + arrived[2][n][2].astype(jnp.float32)
                )
        small_finish(step, 2 * stage + 1)
    for copy in started:
        copy.wait_send()


def scatter_gradients(grads, small):
    widths = [s[2] for s in STREAMS]
    vmem = pl.BlockSpec(memory_space=pltpu.VMEM)
    scratch = [pltpu.VMEM((4, 4, ROWS, w), jnp.bfloat16) for w in widths] * 2
    scratch += [pltpu.VMEM((3, 4, 4, ROWS, w), jnp.bfloat16) for w in widths]
    scratch += [pltpu.VMEM((3, 4, ROWS, w), jnp.bfloat16) for w in widths]
    scratch += [pltpu.VMEM((3, ROWS, w), jnp.bfloat16) for w in widths]
    scratch += [
        pltpu.VMEM((6, *small.shape), jnp.float32),
        pltpu.SemaphoreType.DMA((6, 3, 3)),
        pltpu.SemaphoreType.DMA((6, 3, 3)),
        pltpu.SemaphoreType.DMA((6, 2)),
        pltpu.SemaphoreType.DMA((6,)),
        pltpu.SemaphoreType.DMA((6,)),
    ]
    shapes = [jax.ShapeDtypeStruct((ROWS, w), jnp.float32) for w in widths]
    shapes.append(jax.ShapeDtypeStruct(small.shape, jnp.float32))
    views = [g.reshape(4, 4, 4, ROWS, g.shape[-1]) for g in grads]
    outs = pl.pallas_call(
        scatter_kernel,
        out_shape=shapes,
        in_specs=[pl.BlockSpec(memory_space=pl.ANY)] * 4 + [vmem],
        out_specs=[vmem] * 7,
        scratch_shapes=scratch,
        compiler_params=pltpu.CompilerParams(
            collective_id=1, has_side_effects=True, vmem_limit_bytes=44 * 2**20
        ),
        cost_estimate=pl.CostEstimate(flops=0, bytes_accessed=200000000, transcendentals=0),
        name="scatter_gradients",
    )(*views, small)
    return outs


def other_core(value):
    return lax.ppermute(value, "tp", [(0, 1), (1, 0)])


def folded(pieces, reverse):
    decay, state = jnp.ones_like(pieces[0][0]), jnp.zeros_like(pieces[0][1])
    before = [None] * len(pieces)
    order = range(len(pieces))
    for k in reversed(order) if reverse else order:
        before[k] = (decay, state)
        own_decay, own_state = pieces[k]
        decay, state = decay * own_decay, own_decay * state + own_state
    return before, (decay, state)


def entering(decay, state, reverse):
    heads = decay.shape[0]
    chunk = heads // SIDE
    tail = state.shape[1:]

    def packed(some_decay, some_state):
        lead = some_state.shape[:-2]
        rows = jnp.broadcast_to(some_decay, (*lead, 16, tail[1]))
        return jnp.concatenate([some_state, rows], axis=-2).astype(jnp.bfloat16)

    def opened(message):
        wide = message.astype(jnp.float32)
        return wide[:, tail[0] : tail[0] + 1, :], wide[:, : tail[0], :]

    message = packed(decay[:, None, None], state).reshape(SIDE, chunk, tail[0] + 16, tail[1])
    got = lax.all_to_all(message, "ctx_1", split_axis=0, concat_axis=0, tiled=True)
    inside, total = folded([opened(got[k]) for k in range(SIDE)], reverse)
    sums = jnp.broadcast_to(packed(*total)[None], (SIDE, chunk, tail[0] + 16, tail[1]))
    rows = lax.all_to_all(sums, "ctx_0", split_axis=0, concat_axis=0, tiled=True)
    outer = folded([opened(rows[k]) for k in range(SIDE)], reverse)[0]
    here = lax.axis_index("ctx_0")
    before = sum(jnp.where(here == k, outer[k][1], 0.0) for k in range(SIDE))
    answer = jnp.stack([d * before + s for d, s in inside]).astype(jnp.bfloat16)
    back = lax.all_to_all(answer, "ctx_1", split_axis=0, concat_axis=0, tiled=True)
    return back.astype(jnp.float32).reshape(heads, *tail)


def from_everyone(value, axis):
    copies = jnp.broadcast_to(value, (lax.axis_size(axis), *value.shape))
    return lax.all_to_all(copies, axis, split_axis=0, concat_axis=0, tiled=True)


def joined_along(pieces, dim):
    shape = list(pieces.shape[1:])
    shape[dim] *= pieces.shape[0]
    return jnp.moveaxis(pieces, 0, dim).reshape(shape)


def gathered_copies(value, axis, dim):
    pieces = from_everyone(value, axis)
    return joined_along(pieces, dim)


def passed_along(value, axis, by):
    count = lax.axis_size(axis)
    pairs = [(i, i + by) for i in range(count) if 0 <= i + by < count]
    return lax.ppermute(value, axis, pairs)


def split_up(value, dim, count):
    before, after = (value.shape[:dim], value.shape[dim + 1 :])
    return jnp.moveaxis(value.reshape(*before, count, -1, *after), dim, 0)


def summed_on_arrival(value, axis, dim):
    pieces = split_up(value, dim, lax.axis_size(axis))
    arrived = lax.all_to_all(pieces, axis, split_axis=0, concat_axis=0, tiled=True)
    return arrived.astype(jnp.float32).sum(axis=0)


def rms_norm(value, gain):
    return value * lax.rsqrt(jnp.mean(value * value, axis=-1, keepdims=True) + norm_eps) * gain


def silu_slope(value):
    sigma = jax.nn.sigmoid(value)
    return sigma * (1.0 + value * (1.0 - sigma))


def doc_layout(doc_row, start_row, item_count):
    ends = jnp.cumsum(doc_row)
    starts = ends - doc_row
    token_index = start_row + jnp.arange(item_count, dtype=jnp.int32)
    segment = jnp.sum((token_index[:, None] >= ends[None, :]).astype(jnp.int32), axis=1)
    picked = segment[:, None] == jnp.arange(doc_row.shape[0], dtype=jnp.int32)[None, :]
    begin = jnp.sum(jnp.where(picked, starts[None, :], 0), axis=1)
    return (segment, token_index - begin)


def rope_tables(position):
    freq = rope_base ** (-2.0 * jnp.arange(HD // 2, dtype=jnp.float32) / HD)
    angle = position.astype(jnp.float32)[:, None] * freq[None, :]
    return (jnp.cos(angle), jnp.sin(angle))


def rotate(value, cosine, sine):
    shaped = value.reshape(value.shape[0], -1, 2, HD // 2)
    first_half = shaped[:, :, 0]
    second_half = shaped[:, :, 1]
    cos_part = cosine[:, None, :]
    sin_part = sine[:, None, :]
    turned = jnp.stack(
        [
            first_half * cos_part - second_half * sin_part,
            second_half * cos_part + first_half * sin_part,
        ],
        axis=2,
    )
    return turned.reshape(value.shape)


def conv_act(extended, conv_taps, conv_bias, seg_ext):
    item_count = extended.shape[0] - (CONV - 1)
    own_seg = seg_ext[CONV - 1 :]
    total = conv_bias[None, :] + conv_taps[CONV - 1][None, :] * extended[CONV - 1 :]
    for back in range(1, CONV):
        begin = CONV - 1 - back
        same = seg_ext[begin : begin + item_count] == own_seg
        total = total + conv_taps[CONV - 1 - back][None, :] * jnp.where(
            same[:, None], extended[begin : begin + item_count], 0.0
        )
    return jax.nn.silu(total)


def decay_terms(drive_input, dt_bias, a_log):
    dt_step = jax.nn.softplus(drive_input + dt_bias)
    order = jnp.arange(dt_step.shape[0], dtype=jnp.int32)
    upto = (order[None, :] <= order[:, None]).astype(jnp.float32)
    return (dt_step, jnp.dot(upto, -dt_step * jnp.exp(a_log), precision=highest))


def ssd_output(
    inner_input, b_mat, c_mat, drive_input, dt_bias, a_log, d_skip, segment, position, state_in
):
    item_count = inner_input.shape[0]
    head_total = drive_input.shape[1]
    grouped_heads = inner_input.reshape(item_count, head_total, MAMBA_HEAD_SIZE)
    dt_step, log_cum = decay_terms(drive_input, dt_bias, a_log)
    token_order = jnp.arange(item_count, dtype=jnp.int32)
    causal = (token_order[None, :] <= token_order[:, None]) & (segment[None, :] == segment[:, None])
    spread = log_cum.T[:, :, None] - log_cum.T[:, None, :]
    kernel = jnp.where(causal[None], jnp.exp(jnp.where(causal[None], spread, 0.0)), 0.0)
    inner_prod = jnp.dot(c_mat, b_mat.T, precision=state_precision)
    mixing = kernel * inner_prod[None] * dt_step.T[:, None, :]
    final_result = jnp.einsum("hts,shp->thp", mixing, grouped_heads, precision=state_precision)
    carry_on = ((segment == segment[0]) & (position[0] != 0)).astype(jnp.float32)
    carried = jnp.einsum("tn,hpn->thp", c_mat, state_in, precision=state_precision)
    final_result = (
        final_result
        + carried * (jnp.exp(log_cum) * carry_on[:, None])[:, :, None]
        + d_skip[None, :, None] * grouped_heads
    )
    return final_result.reshape(item_count, head_total * MAMBA_HEAD_SIZE)


def ssd_summary(inner_input, b_mat, drive_input, dt_bias, a_log, segment, position):
    item_count = inner_input.shape[0]
    head_total = drive_input.shape[1]
    grouped_heads = inner_input.reshape(item_count, head_total, MAMBA_HEAD_SIZE)
    dt_step, log_cum = decay_terms(drive_input, dt_bias, a_log)
    in_last = (segment == segment[item_count - 1]).astype(jnp.float32)
    weight_last = jnp.exp(log_cum[item_count - 1][None, :] - log_cum) * dt_step * in_last[:, None]
    state = jnp.einsum("sh,shp,sn->hpn", weight_last, grouped_heads, b_mat, precision=state_precision)
    live = ((segment[item_count - 1] == segment[0]) & (position[0] != 0)).astype(jnp.float32)
    return (live * jnp.exp(log_cum[item_count - 1]), state)


def split_vector(vector, widths):
    q_width, k_width, s_width, b_width, h_width = widths
    channels = s_width + b_width
    conv_taps = vector[: CONV * channels].reshape(CONV, channels)
    offset = CONV * channels
    conv_bias = vector[offset : offset + channels]
    offset = offset + channels
    gated_gain = vector[offset : offset + s_width]
    offset = offset + s_width
    return (
        conv_taps,
        conv_bias,
        gated_gain,
        vector[offset : offset + h_width],
        vector[offset + h_width : offset + 2 * h_width],
        vector[offset + 2 * h_width : offset + 3 * h_width],
    )


def feature_sum(value):
    own = value.astype(jnp.bfloat16)
    return own.astype(jnp.float32) + other_core(own).astype(jnp.float32)


def norm_sum(value):
    return value + other_core(value)


def local_matrices(w_in, w_out, w_gu, w_down, layer_at):
    return (
        jnp.pad(w_in[layer_at, :, 0, :], ((0, 0), (0, IN_PAD - IN_COLS))).astype(jnp.bfloat16),
        w_gu[layer_at, :, 0, :].astype(jnp.bfloat16),
        w_out[layer_at, 0].T.astype(jnp.bfloat16),
        w_down[layer_at, 0].T.astype(jnp.bfloat16),
    )


def fetch_layer(w_in, w_out, w_gu, w_down, layer_at):
    parts = local_matrices(w_in, w_out, w_gu, w_down, layer_at)
    if layer_at == 0:
        return gather_weights(parts)
    filled = lax.all_gather(jnp.concatenate(parts, axis=1), FSDP_CTX, axis=0, tiled=True)
    bounds = [sum(WIDTHS[:k]) for k in range(1, len(WIDTHS))]
    return tuple(jnp.split(filled, bounds, axis=1))


def attention_logits(queries_b, key_values, allowed):
    grouped_heads = queries_b.reshape(queries_b.shape[0], -1, HD)
    raw = jnp.einsum(
        "tgd,sd->gts", grouped_heads, key_values[:, :HD], preferred_element_type=jnp.float32
    )
    return jnp.where(allowed[None], raw * HD ** (-0.5), masked_value)


def layer_forward(state, weights, vector, gains, context, widths):
    w_in_b, w_gu_b, w_out_t, w_down_t = weights
    segment, position, seg_ext, allowed, cosine, sine = context
    q_width, k_width, s_width, b_width, h_width = widths
    conv_taps, conv_bias, gated_gain, a_log, dt_bias, d_skip = split_vector(vector, widths)
    item_count = state.shape[0]
    at_v = q_width + k_width
    at_z = at_v + k_width
    at_x = at_z + s_width
    at_t = at_x + s_width + b_width
    hidden_b = rms_norm(state, gains[0]).astype(jnp.bfloat16)
    proj = jnp.dot(hidden_b, w_in_b, preferred_element_type=jnp.float32)
    queries_b = rotate(proj[:, :q_width], cosine, sine).astype(jnp.bfloat16)
    pair = jnp.concatenate(
        [rotate(proj[:, q_width:at_v], cosine, sine), proj[:, at_v:at_z]], axis=1
    ).astype(jnp.bfloat16)
    key_values = gathered_copies(pair, CTX, 0)
    logits = attention_logits(queries_b, key_values, allowed)
    top = jnp.max(logits, axis=2, keepdims=True)
    log_total = top + jnp.log(jnp.sum(jnp.exp(logits - top), axis=2, keepdims=True))
    prob_b = jnp.exp(logits - log_total).astype(jnp.bfloat16)
    attended = jnp.einsum(
        "gts,sd->tgd", prob_b, key_values[:, HD:], preferred_element_type=jnp.float32
    ).reshape(item_count, q_width)
    mixed_in = proj[:, at_x:at_t]
    halo_rows = passed_along(mixed_in[item_count - (CONV - 1) :], CTX, 1)
    extended = jnp.concatenate([halo_rows, mixed_in], axis=0)
    active = conv_act(extended, conv_taps, conv_bias, seg_ext)
    own_part = active[:, s_width:].astype(jnp.bfloat16)
    other_part = other_core(own_part)
    leads = lax.axis_index("tp") == 0
    both = jnp.concatenate(
        [jnp.where(leads, own_part, other_part), jnp.where(leads, other_part, own_part)], axis=1
    ).astype(jnp.float32)
    inner_input = active[:, :s_width]
    drive_input = proj[:, at_t : at_t + h_width]
    decay_own, state_own = ssd_summary(
        inner_input, both[:, :MAMBA_STATE_SIZE], drive_input, dt_bias, a_log, segment, position
    )
    state_in = entering(decay_own, state_own, False)
    ssm = ssd_output(
        inner_input,
        both[:, :MAMBA_STATE_SIZE],
        both[:, MAMBA_STATE_SIZE:],
        drive_input,
        dt_bias,
        a_log,
        d_skip,
        segment,
        position,
        state_in,
    )
    gated = ssm * jax.nn.silu(proj[:, at_z:at_x])
    inverse = lax.rsqrt(norm_sum(jnp.sum(gated * gated, axis=1)) / DSSM + norm_eps)[:, None]
    features = jnp.concatenate([attended, gated * inverse * gated_gain], axis=1).astype(
        jnp.bfloat16
    )
    middle = state + feature_sum(
        jnp.einsum("tc,dc->td", features, w_out_t, preferred_element_type=jnp.float32)
    )
    hidden2_b = rms_norm(middle, gains[1]).astype(jnp.bfloat16)
    upgate = jnp.dot(hidden2_b, w_gu_b, preferred_element_type=jnp.float32)
    half_width = upgate.shape[1] // 2
    inner_b = (jax.nn.silu(upgate[:, :half_width]) * upgate[:, half_width:]).astype(jnp.bfloat16)
    final_result = middle + feature_sum(
        jnp.einsum("tf,df->td", inner_b, w_down_t, preferred_element_type=jnp.float32)
    )
    kept = (
        state,
        hidden_b,
        proj,
        queries_b,
        key_values,
        log_total,
        extended,
        active,
        both,
        state_in,
        decay_own,
        ssm,
        gated,
        inverse,
        features,
        middle,
        hidden2_b,
        upgate,
        inner_b,
    )
    return (final_result, kept)


def layer_backward(grad_out, kept, weights, vector, gains, context, widths):
    w_in_b, w_gu_b, w_out_t, w_down_t = weights
    segment, position, seg_ext, allowed, cosine, sine = context
    q_width, k_width, s_width, b_width, h_width = widths
    conv_taps, conv_bias, gated_gain, a_log, dt_bias, d_skip = split_vector(vector, widths)
    (
        state,
        hidden_b,
        proj,
        queries_b,
        key_values,
        log_total,
        extended,
        active,
        both,
        state_in,
        decay_own,
        ssm,
        gated,
        inverse,
        features,
        middle,
        hidden2_b,
        upgate,
        inner_b,
    ) = kept
    item_count = state.shape[0]
    at_v = q_width + k_width
    at_z = at_v + k_width
    at_x = at_z + s_width
    at_t = at_x + s_width + b_width
    grad_b = grad_out.astype(jnp.bfloat16)
    grad_down = jnp.einsum(
        "td,tf->df", grad_b, inner_b, preferred_element_type=jnp.float32
    ).astype(jnp.bfloat16)
    d_inner = jnp.dot(grad_b, w_down_t, preferred_element_type=jnp.float32)
    half_width = upgate.shape[1] // 2
    gate_part = upgate[:, :half_width]
    d_upgate_b = jnp.concatenate(
        [
            d_inner * upgate[:, half_width:] * silu_slope(gate_part),
            d_inner * jax.nn.silu(gate_part),
        ],
        axis=1,
    ).astype(jnp.bfloat16)
    grad_gu = jnp.einsum(
        "td,tf->df", hidden2_b, d_upgate_b, preferred_element_type=jnp.float32
    ).astype(jnp.bfloat16)
    d_hidden2 = feature_sum(
        jnp.einsum("tf,df->td", d_upgate_b, w_gu_b, preferred_element_type=jnp.float32)
    )
    d_middle_norm, d_gain_mlp = jax.vjp(rms_norm, middle, gains[1])[1](d_hidden2)
    d_middle = grad_out + d_middle_norm
    mix_b = d_middle.astype(jnp.bfloat16)
    grad_out_proj = jnp.einsum(
        "td,tc->dc", mix_b, features, preferred_element_type=jnp.float32
    ).astype(jnp.bfloat16)
    d_features = jnp.dot(mix_b, w_out_t, preferred_element_type=jnp.float32)
    d_normed = d_features[:, q_width:]
    weighted = d_normed * gated_gain
    d_gated_gain = jnp.sum(d_normed * gated * inverse, axis=0)
    across = norm_sum(jnp.sum(weighted * gated, axis=1))[:, None]
    d_gated = weighted * inverse - gated * inverse**3 * across / DSSM
    gate_z = proj[:, at_z:at_x]
    d_ssm = d_gated * jax.nn.silu(gate_z)
    d_gate_z = d_gated * ssm * silu_slope(gate_z)
    inner_input = active[:, :s_width]
    drive_input = proj[:, at_t : at_t + h_width]

    def output_part(x_part, b_part, c_part, drive_part, bias_part, log_part, skip_part, carry_part):
        return ssd_output(
            x_part,
            b_part,
            c_part,
            drive_part,
            bias_part,
            log_part,
            skip_part,
            segment,
            position,
            carry_part,
        )

    output_pull = jax.vjp(
        output_part,
        inner_input,
        both[:, :MAMBA_STATE_SIZE],
        both[:, MAMBA_STATE_SIZE:],
        drive_input,
        dt_bias,
        a_log,
        d_skip,
        state_in,
    )[1]
    dx_one, db_one, dc_one, drive_one, bias_one, log_one, skip_grad, d_carry = output_pull(d_ssm)
    later = entering(decay_own, d_carry, True)

    def summary_part(x_part, b_part, drive_part, bias_part, log_part):
        return ssd_summary(x_part, b_part, drive_part, bias_part, log_part, segment, position)

    summary_pull = jax.vjp(
        summary_part, inner_input, both[:, :MAMBA_STATE_SIZE], drive_input, dt_bias, a_log
    )[1]
    dx_two, db_two, drive_two, bias_two, log_two = summary_pull(
        (jnp.sum(later * state_in, axis=(1, 2)), later)
    )
    d_both = jnp.concatenate([db_one + db_two, dc_one], axis=1)
    d_both_b = d_both.astype(jnp.bfloat16)
    leads = lax.axis_index("tp") == 0
    kept_part = jnp.where(leads, d_both_b[:, :b_width], d_both_b[:, b_width:])
    sent_part = jnp.where(leads, d_both_b[:, b_width:], d_both_b[:, :b_width])
    d_own = kept_part.astype(jnp.float32) + other_core(sent_part).astype(jnp.float32)

    def conv_part(ext_part, taps_part, bias_part):
        return conv_act(ext_part, taps_part, bias_part, seg_ext)

    conv_pull = jax.vjp(conv_part, extended, conv_taps, conv_bias)[1]
    d_extended, d_taps, d_bias = conv_pull(jnp.concatenate([dx_one + dx_two, d_own], axis=1))
    spill = passed_along(d_extended[: CONV - 1], CTX, -1)
    d_mixed = jnp.concatenate(
        [d_extended[CONV - 1 : item_count], d_extended[item_count:] + spill], axis=0
    )
    logits = attention_logits(queries_b, key_values, allowed)
    prob = jnp.exp(logits - log_total)
    prob_b = prob.astype(jnp.bfloat16)
    d_att_b = d_features[:, :q_width].astype(jnp.bfloat16).reshape(item_count, -1, HD)
    d_prob = jnp.einsum(
        "tgd,sd->gts", d_att_b, key_values[:, HD:], preferred_element_type=jnp.float32
    )
    d_raw_b = (
        prob * (d_prob - jnp.sum(prob * d_prob, axis=2, keepdims=True)) * HD ** (-0.5)
    ).astype(jnp.bfloat16)
    d_query = jnp.einsum(
        "gts,sd->tgd", d_raw_b, key_values[:, :HD], preferred_element_type=jnp.float32
    ).reshape(item_count, q_width)
    grouped_q = queries_b.reshape(item_count, -1, HD)
    d_key = jnp.einsum("gts,tgd->sd", d_raw_b, grouped_q, preferred_element_type=jnp.float32)
    d_value = jnp.einsum("gts,tgd->sd", prob_b, d_att_b, preferred_element_type=jnp.float32)
    d_pair = summed_on_arrival(
        jnp.concatenate([d_key, d_value], axis=1).astype(jnp.bfloat16), CTX, 0
    )
    d_proj_b = jnp.concatenate(
        [
            rotate(d_query, cosine, -sine),
            rotate(d_pair[:, :HD], cosine, -sine),
            d_pair[:, HD:],
            d_gate_z,
            d_mixed,
            drive_one + drive_two,
            jnp.zeros((item_count, IN_PAD - IN_COLS), jnp.float32),
        ],
        axis=1,
    ).astype(jnp.bfloat16)
    grad_in = jnp.einsum(
        "td,tc->dc", hidden_b, d_proj_b, preferred_element_type=jnp.float32
    ).astype(jnp.bfloat16)
    d_hidden = feature_sum(
        jnp.einsum("tc,dc->td", d_proj_b, w_in_b, preferred_element_type=jnp.float32)
    )
    d_state_norm, d_gain_mix = jax.vjp(rms_norm, state, gains[0])[1](d_hidden)
    d_vector = jnp.concatenate(
        [
            d_taps.reshape(-1),
            d_bias,
            d_gated_gain,
            log_one + log_two,
            bias_one + bias_two,
            skip_grad,
        ]
    )
    return (
        d_middle + d_state_norm,
        (grad_in, grad_gu, grad_out_proj, grad_down),
        d_vector,
        jnp.stack([d_gain_mix, d_gain_mlp]),
    )


def adamw(weight, first_m, second_m, grad, rate, decay):
    first_new = beta_one * first_m + (1.0 - beta_one) * grad
    second_new = beta_two * second_m + (1.0 - beta_two) * grad * grad
    ratio = (
        first_new
        / (1.0 - beta_one**STEP)
        / (jnp.sqrt(second_new / (1.0 - beta_two**STEP)) + adam_eps)
    )
    return (first_new, second_new, weight - rate * (ratio + decay * weight))


def per_device(
    block_input,
    cotangent,
    lengths,
    w_in,
    w_out,
    w_gu,
    w_down,
    vectors,
    norm_gains,
    first_in,
    first_out,
    first_gu,
    first_down,
    first_vectors,
    first_gains,
    second_in,
    second_out,
    second_gu,
    second_down,
    second_vectors,
    second_gains,
):
    group_count = lax.axis_size("tp")
    widths = (
        HEADS * HD // group_count,
        KV_HEADS * HD // group_count,
        MAMBA_HEADS * MAMBA_HEAD_SIZE // group_count,
        2 * MAMBA_STATE_SIZE // group_count,
        MAMBA_HEADS // group_count,
    )
    item_count = block_input.shape[0]
    start_row = lax.axis_index(CTX) * item_count
    seq_total = item_count * lax.axis_size(CTX)
    doc_row = lengths[0]
    segment, position = doc_layout(doc_row, start_row, item_count)
    seg_ext = doc_layout(doc_row, start_row - (CONV - 1), item_count + CONV - 1)[0]
    key_seg = doc_layout(doc_row, 0, seq_total)[0]
    query_index = start_row + jnp.arange(item_count, dtype=jnp.int32)
    allowed = (jnp.arange(seq_total, dtype=jnp.int32)[None, :] <= query_index[:, None]) & (
        key_seg[None, :] == segment[:, None]
    )
    cosine, sine = rope_tables(position)
    context = (segment, position, seg_ext, allowed, cosine, sine)
    stored = []
    fetched = []
    state = block_input
    for layer_at in range(LAYERS):
        weights = fetch_layer(w_in, w_out, w_gu, w_down, layer_at)
        state, kept = layer_forward(
            state, weights, vectors[layer_at, 0], norm_gains[layer_at], context, widths
        )
        stored.append(kept)
        fetched.append(weights)
    grad_state = cotangent
    shards = [None] * LAYERS
    small_grads = [None] * LAYERS
    vec = vectors.shape[-1]
    for layer_at in reversed(range(LAYERS)):
        grad_state, matrices, d_vector, d_gains = layer_backward(
            grad_state,
            stored[layer_at],
            fetched[layer_at],
            vectors[layer_at, 0],
            norm_gains[layer_at],
            context,
            widths,
        )
        small = jnp.concatenate([d_vector, d_gains.reshape(-1)])
        span = -(-small.shape[0] // 1024) * 8
        small = jnp.pad(small, (0, span * 128 - small.shape[0])).reshape(span, 128)
        *pieces, small = scatter_gradients(matrices, small)
        shards[layer_at] = pieces
        small_grads[layer_at] = small.reshape(-1)
    grad_in_all = jnp.stack(
        [jnp.concatenate([p[0], p[1]], axis=1)[:, :IN_COLS] for p in shards]
    ).reshape(w_in.shape)
    grad_gu_all = jnp.stack([jnp.concatenate([p[2], p[3]], axis=1) for p in shards]).reshape(
        w_gu.shape
    )
    grad_out_all = jnp.stack([p[4].T for p in shards]).reshape(w_out.shape)
    grad_down_all = jnp.stack([p[5].T for p in shards]).reshape(w_down.shape)
    vector_total = jnp.stack([v[:vec] for v in small_grads]).reshape(vectors.shape)
    gain_total = jnp.stack([v[vec : vec + 2 * D] for v in small_grads]).reshape(norm_gains.shape)
    up_in = adamw(w_in, first_in, second_in, grad_in_all, rate_matrix, decay_rate)
    up_out = adamw(w_out, first_out, second_out, grad_out_all, rate_matrix, decay_rate)
    up_gu = adamw(w_gu, first_gu, second_gu, grad_gu_all, rate_matrix, decay_rate)
    up_down = adamw(w_down, first_down, second_down, grad_down_all, rate_matrix, decay_rate)
    up_vec = adamw(vectors, first_vectors, second_vectors, vector_total, rate_vector, 0.0)
    up_gain = adamw(norm_gains, first_gains, second_gains, gain_total, rate_vector, 0.0)
    return (
        state,
        grad_state,
        up_in[0],
        up_in[1],
        up_in[2],
        up_out[0],
        up_out[1],
        up_out[2],
        up_gu[0],
        up_gu[1],
        up_gu[2],
        up_down[0],
        up_down[1],
        up_down[2],
        up_vec[0],
        up_vec[1],
        up_vec[2],
        up_gain[0],
        up_gain[1],
        up_gain[2],
    )


def solution(mesh):
    torus = Mesh(
        mesh.devices.reshape(mesh.shape["fsdp"], 4, 4, mesh.shape["tp"]),
        ("fsdp", "ctx_0", "ctx_1", "tp"),
    )
    in_specs = (
        P(FSDP_CTX, None),
        P(FSDP_CTX, None),
        P("fsdp", None),
        P(None, FSDP_CTX, "tp", None),
        P(None, "tp", None, FSDP_CTX),
        P(None, FSDP_CTX, "tp", None),
        P(None, "tp", None, FSDP_CTX),
        P(None, "tp", None),
        P(),
        P(None, FSDP_CTX, "tp", None),
        P(None, "tp", None, FSDP_CTX),
        P(None, FSDP_CTX, "tp", None),
        P(None, "tp", None, FSDP_CTX),
        P(None, "tp", None),
        P(),
        P(None, FSDP_CTX, "tp", None),
        P(None, "tp", None, FSDP_CTX),
        P(None, FSDP_CTX, "tp", None),
        P(None, "tp", None, FSDP_CTX),
        P(None, "tp", None),
        P(),
    )
    out_specs = (
        P(FSDP_CTX, None),
        P(FSDP_CTX, None),
        P(None, FSDP_CTX, "tp", None),
        P(None, FSDP_CTX, "tp", None),
        P(None, FSDP_CTX, "tp", None),
        P(None, "tp", None, FSDP_CTX),
        P(None, "tp", None, FSDP_CTX),
        P(None, "tp", None, FSDP_CTX),
        P(None, FSDP_CTX, "tp", None),
        P(None, FSDP_CTX, "tp", None),
        P(None, FSDP_CTX, "tp", None),
        P(None, "tp", None, FSDP_CTX),
        P(None, "tp", None, FSDP_CTX),
        P(None, "tp", None, FSDP_CTX),
        P(None, "tp", None),
        P(None, "tp", None),
        P(None, "tp", None),
        P(),
        P(),
        P(),
    )
    return jax.shard_map(
        per_device, mesh=torus, in_specs=in_specs, out_specs=out_specs, check_vma=False
    )
```

```python
import functools

import jax
import jax.numpy as jnp
from jax import lax
from jax.experimental import pallas as pl
from jax.experimental.pallas import tpu as pltpu
from jax.sharding import Mesh
from jax.sharding import PartitionSpec as P

HEADS = 8
KV_HEADS = 2
HD = 64
MAMBA_HEADS = 24
MAMBA_HEAD_SIZE = 64
MAMBA_STATE_SIZE = 128
CONV = 4
LAYERS = 2
STEP = 10
DSSM = 1536
FSDP_CTX = ("fsdp", "ctx_0", "ctx_1")
CTX = ("ctx_0", "ctx_1")


highest = lax.Precision.HIGHEST
state_precision = lax.Precision.DEFAULT
D = 1024
IN_COLS = 2060
IN_PAD = 2176
AXES = ("fsdp", "ctx_0", "ctx_1")
SIDE = 4
ROWS = 16
STREAMS = (
    (0, 0, 1152, (0, 1, 2), 1),
    (0, 1152, 1024, (0, 1, 2), -1),
    (1, 0, 1024, (1, 2, 0), 1),
    (1, 1024, 1024, (1, 2, 0), -1),
    (2, 0, 1024, (2, 0, 1), 1),
    (3, 0, 1024, (2, 0, 1), -1),
)
WIDTHS = (IN_PAD, 2048, 1024, 1024)
GRAD_STREAMS = (
    (0, 0, 640, (0, 1, 2), 1),
    (0, 640, 512, (0, 1, 2), -1),
    (0, 1152, 512, (1, 2, 0), 1),
    (0, 1664, 512, (1, 2, 0), -1),
    (1, 0, 512, (2, 0, 1), 1),
    (1, 512, 512, (2, 0, 1), -1),
)
KEY_BLOCK = 512
norm_eps = 1e-05
rope_base = 100000000000.0
masked_value = -1e30
beta_one = 0.9
beta_two = 0.95
adam_eps = 1e-08
decay_rate = 0.1
rate_matrix = 0.05
rate_vector = 0.5


def ring_places():
    return tuple(lax.axis_index(a) for a in AXES)


def ring_step(places, axis, by):
    return {AXES[axis]: lax.rem(places[axis] + (by + SIDE), SIDE)}


def greet_neighbours(places):
    barrier = pltpu.get_barrier_semaphore()
    for axis in range(3):
        for by in (1, -1):
            pl.semaphore_signal(
                barrier,
                inc=1,
                device_id=ring_step(places, axis, by),
                device_id_type=pl.DeviceIdType.MESH,
            )
    pl.semaphore_wait(barrier, 6)


def remote(src, dst, send, recv, device):
    return pltpu.make_async_remote_copy(
        src_ref=src,
        dst_ref=dst,
        send_sem=send,
        recv_sem=recv,
        device_id=device,
        device_id_type=pl.DeviceIdType.MESH,
    )


def gather_kernel(*refs):
    shards, full = refs[:4], refs[4:8]
    send, recv, own_sem = refs[8:]
    places = ring_places()
    greet_neighbours(places)
    own = []
    for k in range(4):
        copy = pltpu.make_async_copy(
            shards[k], full[k].at[places[0], places[1], places[2]], own_sem.at[k]
        )
        copy.start()
        own.append(copy)
    started = []

    def region(number, stage, place):
        at, first, width, order, _ = STREAMS[number]
        order = order[::-1]
        index = list(places)
        for axis in order[:stage]:
            index[axis] = slice(None)
        index[order[stage]] = place
        return full[at].at[(*index, slice(None), pl.ds(first, width))]

    def launch(number, stage, kind):
        at, first, width, order, way = STREAMS[number]
        axis = order[::-1][stage]
        here = places[axis]
        if kind == 2:
            source = target = region(number, stage, lax.rem(here + (SIDE - way), SIDE))
        else:
            source = target = region(number, stage, here)
            if stage == 0:
                source = shards[at].at[:, pl.ds(first, width)]
        copy = remote(
            source,
            target,
            send.at[number, stage, kind],
            recv.at[number, stage, kind],
            ring_step(places, axis, -way if kind == 1 else way),
        )
        copy.start()
        started.append(copy)
        return copy

    for stage in range(3):
        if stage == 1:
            for copy in own:
                copy.wait()
        first, back = [], []
        for n in range(6):
            first.append(launch(n, stage, 0))
            back.append(launch(n, stage, 1))
        onward = []
        for n in range(6):
            first[n].wait_recv()
            onward.append(launch(n, stage, 2))
        for n in range(6):
            back[n].wait_recv()
            onward[n].wait_recv()
    for copy in started:
        copy.wait_send()


def gather_weights(parts):
    shapes = [jax.ShapeDtypeStruct((4, 4, 4, ROWS, w), jnp.bfloat16) for w in WIDTHS]
    outs = pl.pallas_call(
        gather_kernel,
        out_shape=shapes,
        in_specs=[pl.BlockSpec(memory_space=pl.ANY)] * 4,
        out_specs=[pl.BlockSpec(memory_space=pl.ANY)] * 4,
        scratch_shapes=[
            pltpu.SemaphoreType.DMA((6, 3, 3)),
            pltpu.SemaphoreType.DMA((6, 3, 3)),
            pltpu.SemaphoreType.DMA((4,)),
        ],
        compiler_params=pltpu.CompilerParams(collective_id=0, has_side_effects=True),
        cost_estimate=pl.CostEstimate(flops=0, bytes_accessed=180000000, transcendentals=0),
        name="gather_weights",
    )(*parts)
    return tuple(o.reshape(D, o.shape[-1]) for o in outs)


def scatter_kernel(*refs):
    grads, small = refs[:2], refs[2]
    outs, small_out = refs[3:9], refs[9]
    ahead, mine = refs[10:16], refs[16:22]
    arrived = (refs[22:28], refs[28:34], refs[34:40])
    small_in, send, recv, own_sem, small_send, small_recv = refs[40:]
    places = ring_places()
    greet_neighbours(places)
    started = []

    def near(axis, by):
        return lax.rem(places[axis] + (by + SIDE), SIDE)

    def block(number, stage, place):
        at, first, width, order, _ = GRAD_STREAMS[number]
        axis = order[stage]
        if stage == 0:
            index = [slice(None)] * 3
            index[axis] = place
            return grads[at].at[(*index, slice(None), pl.ds(first, width))]
        left = [a for a in range(3) if a != order[0]]
        index = [slice(None)] * 2
        if stage == 2:
            index[left.index(order[1])] = places[order[1]]
        index[left.index(axis)] = place
        return mine[number].at[tuple(index)]

    def launch(number, stage, kind, source):
        axis, way = GRAD_STREAMS[number][3][stage], GRAD_STREAMS[number][4]
        copy = remote(
            source,
            arrived[stage][number].at[kind],
            send.at[number, stage, kind],
            recv.at[number, stage, kind],
            ring_step(places, axis, -way if kind == 2 else way),
        )
        copy.start()
        started.append(copy)
        return copy

    def add_into(target, source, stage):
        def one(total, part):
            total[...] = total[...] + part[...]

        if stage == 0:

            def body(k, carry):
                one(target.at[k // 4, k % 4], source.at[k // 4, k % 4])
                return carry

            lax.fori_loop(0, 16, body, 0)
        elif stage == 1:

            def body(k, carry):
                one(target.at[k], source.at[k])
                return carry

            lax.fori_loop(0, 4, body, 0)
        else:
            one(target, source)

    def small_exchange(step):
        axis, odd = step // 2, step % 2
        here = places[axis]
        partner = 3 - here if odd else here + 1 - 2 * lax.rem(here, 2)
        copy = remote(
            small_out,
            small_in.at[step],
            small_send.at[step],
            small_recv.at[step],
            {AXES[axis]: partner},
        )
        copy.start()
        return copy

    def small_finish(copy, step):
        copy.wait_send()
        copy.wait_recv()
        small_out[...] = small_out[...] + small_in[step]

    first, back, local = [], [], []
    for n in range(6):
        axis, way = GRAD_STREAMS[n][3][0], GRAD_STREAMS[n][4]
        first.append(launch(n, 0, 0, block(n, 0, near(axis, 2))))
    for n in range(6):
        axis, way = GRAD_STREAMS[n][3][0], GRAD_STREAMS[n][4]
        pair = (
            pltpu.make_async_copy(block(n, 0, near(axis, way)), ahead[n], own_sem.at[n, 0]),
            pltpu.make_async_copy(block(n, 0, places[axis]), mine[n], own_sem.at[n, 1]),
        )
        for copy in pair:
            copy.start()
        local.append(pair)
        back.append(launch(n, 0, 2, block(n, 0, near(axis, -way))))
    small_out[...] = small[...]
    for stage in range(3):
        if stage:
            first, back = [], []
            for n in range(6):
                axis, way = GRAD_STREAMS[n][3][stage], GRAD_STREAMS[n][4]
                first.append(launch(n, stage, 0, block(n, stage, near(axis, 2))))
                back.append(launch(n, stage, 2, block(n, stage, near(axis, -way))))
        step = small_exchange(2 * stage)
        onward = []
        for n in range(6):
            axis, way = GRAD_STREAMS[n][3][stage], GRAD_STREAMS[n][4]
            if stage == 0:
                local[n][0].wait()
                local[n][1].wait()
                target = ahead[n]
            else:
                target = block(n, stage, near(axis, way))
            first[n].wait_recv()
            add_into(target, arrived[stage][n].at[0], stage)
            onward.append(launch(n, stage, 1, target))
        small_finish(step, 2 * stage)
        step = small_exchange(2 * stage + 1)
        for n in range(6):
            axis = GRAD_STREAMS[n][3][stage]
            target = mine[n] if stage == 0 else block(n, stage, places[axis])
            back[n].wait_recv()
            if stage < 2:
                add_into(target, arrived[stage][n].at[2], stage)
            onward[n].wait_recv()
            if stage < 2:
                add_into(target, arrived[stage][n].at[1], stage)
            else:
                outs[n][...] = target[...].astype(jnp.float32) + (
                    arrived[2][n][1].astype(jnp.float32) + arrived[2][n][2].astype(jnp.float32)
                )
        small_finish(step, 2 * stage + 1)
    for copy in started:
        copy.wait_send()


def scatter_gradients(grads, small):
    widths = [s[2] for s in GRAD_STREAMS]
    vmem = pl.BlockSpec(memory_space=pltpu.VMEM)
    scratch = [pltpu.VMEM((4, 4, ROWS, w), jnp.bfloat16) for w in widths] * 2
    scratch += [pltpu.VMEM((3, 4, 4, ROWS, w), jnp.bfloat16) for w in widths]
    scratch += [pltpu.VMEM((3, 4, ROWS, w), jnp.bfloat16) for w in widths]
    scratch += [pltpu.VMEM((3, ROWS, w), jnp.bfloat16) for w in widths]
    scratch += [
        pltpu.VMEM((6, *small.shape), jnp.float32),
        pltpu.SemaphoreType.DMA((6, 3, 3)),
        pltpu.SemaphoreType.DMA((6, 3, 3)),
        pltpu.SemaphoreType.DMA((6, 2)),
        pltpu.SemaphoreType.DMA((6,)),
        pltpu.SemaphoreType.DMA((6,)),
    ]
    shapes = [jax.ShapeDtypeStruct((ROWS, w), jnp.float32) for w in widths]
    shapes.append(jax.ShapeDtypeStruct(small.shape, jnp.float32))
    views = [g.reshape(4, 4, 4, ROWS, g.shape[-1]) for g in grads]
    outs = pl.pallas_call(
        scatter_kernel,
        out_shape=shapes,
        in_specs=[pl.BlockSpec(memory_space=pl.ANY)] * 2 + [vmem],
        out_specs=[vmem] * 7,
        scratch_shapes=scratch,
        compiler_params=pltpu.CompilerParams(
            collective_id=1, has_side_effects=True, vmem_limit_bytes=28 * 2**20
        ),
        cost_estimate=pl.CostEstimate(flops=0, bytes_accessed=100000000, transcendentals=0),
        name="scatter_gradients",
    )(*views, small)
    return outs


def other_core(value):
    return lax.ppermute(value, "tp", [(0, 1), (1, 0)])


def scan_kernel(
    reverse, parts, out, got, sums, rows, inside, decays, reply, back, send, recv
):
    here, outer = lax.axis_index("ctx_1"), lax.axis_index("ctx_0")
    head = parts.shape[2] - 16
    barrier = pltpu.get_barrier_semaphore()
    for axis, place in (("ctx_1", here), ("ctx_0", outer)):
        for by in range(1, SIDE):
            pl.semaphore_signal(
                barrier,
                inc=1,
                device_id={axis: lax.rem(place + by, SIDE)},
                device_id_type=pl.DeviceIdType.MESH,
            )
    pl.semaphore_wait(barrier, 6)
    started = []

    def spread(stage, axis, place, source, target):
        copies = []
        for by in (2, 1, 3):
            other = lax.rem(place + by, SIDE)
            copy = remote(
                source(other),
                target.at[place],
                send.at[stage, by - 1],
                recv.at[stage, by - 1],
                {axis: other},
            )
            copy.start()
            copies.append(copy)
        started.extend(copies)
        return copies

    def opened(ref, k):
        wide = ref[k].astype(jnp.float32)
        return wide[:, head : head + 1, :], wide[:, :head, :]

    order = range(SIDE - 1, -1, -1) if reverse else range(SIDE)
    copies = spread(0, "ctx_1", here, lambda other: parts.at[other], got)
    got[here] = parts[here]
    for copy in copies:
        copy.wait_recv()
    decay = state = None
    for k in order:
        own_decay, own_state = opened(got, k)
        if decay is None:
            decay, state = own_decay, own_state
        else:
            decays[k] = decay
            inside[k] = state
            decay, state = decay * own_decay, own_decay * state + own_state
    sums[:, :head, :] = state.astype(jnp.bfloat16)
    sums[:, head:, :] = jnp.broadcast_to(decay, (decay.shape[0], 16, decay.shape[2])).astype(
        jnp.bfloat16
    )
    copies = spread(1, "ctx_0", outer, lambda other: sums, rows)
    rows[outer] = sums[...]
    for copy in copies:
        copy.wait_recv()
    before = jnp.zeros_like(state)
    state = None
    for k in order:
        if state is not None:
            before = jnp.where(outer == k, state, before)
        own_decay, own_state = opened(rows, k)
        state = own_state if state is None else own_decay * state + own_state
    for k in order:
        if k == order[0]:
            reply[k] = before.astype(jnp.bfloat16)
        else:
            reply[k] = (decays[k] * before + inside[k]).astype(jnp.bfloat16)
    copies = spread(2, "ctx_1", here, lambda other: reply.at[other], back)
    back[here] = reply[here]
    for copy in copies:
        copy.wait_recv()
    out[...] = back[...].astype(jnp.float32)
    for copy in started:
        copy.wait_send()


def entering(decay, state, reverse):
    heads = decay.shape[0]
    chunk = heads // SIDE
    size, width = state.shape[1:]
    rows = jnp.broadcast_to(decay[:, None, None], (heads, 16, width))
    message = jnp.concatenate([state, rows], axis=1).astype(jnp.bfloat16)
    message = message.reshape(SIDE, chunk, size + 16, width)
    vmem = pl.BlockSpec(memory_space=pltpu.VMEM)
    out = pl.pallas_call(
        functools.partial(scan_kernel, reverse),
        out_shape=jax.ShapeDtypeStruct((SIDE, chunk, size, width), jnp.float32),
        in_specs=[vmem],
        out_specs=vmem,
        scratch_shapes=[
            pltpu.VMEM((SIDE, chunk, size + 16, width), jnp.bfloat16),
            pltpu.VMEM((chunk, size + 16, width), jnp.bfloat16),
            pltpu.VMEM((SIDE, chunk, size + 16, width), jnp.bfloat16),
            pltpu.VMEM((SIDE, chunk, size, width), jnp.float32),
            pltpu.VMEM((SIDE, chunk, 1, width), jnp.float32),
            pltpu.VMEM((SIDE, chunk, size, width), jnp.bfloat16),
            pltpu.VMEM((SIDE, chunk, size, width), jnp.bfloat16),
            pltpu.SemaphoreType.DMA((3, 3)),
            pltpu.SemaphoreType.DMA((3, 3)),
        ],
        compiler_params=pltpu.CompilerParams(
            collective_id=3 if reverse else 2, has_side_effects=True
        ),
        cost_estimate=pl.CostEstimate(flops=0, bytes_accessed=40000000, transcendentals=0),
        name="scan_back" if reverse else "scan_forth",
    )(message)
    return out.reshape(heads, size, width)


def attend_back_kernel(
    kv, keys_t, queries, queries_t, d_att, d_att_t, log_total, delta, lowest, highest_key, d_kv, d_query_t
):
    step = pl.program_id(0)

    @pl.when(step == 0)
    def _():
        d_query_t[...] = jnp.zeros_like(d_query_t)

    at = step * KEY_BLOCK + lax.broadcasted_iota(jnp.int32, (KEY_BLOCK, lowest.shape[1]), 0)
    allowed = (at >= lowest[...]) & (at <= highest_key[...])
    keys, values = kv[:, :HD], kv[:, HD:]
    scale = HD ** (-0.5)
    d_key = jnp.zeros((KEY_BLOCK, HD), jnp.float32)
    d_value = jnp.zeros((KEY_BLOCK, HD), jnp.float32)
    for g in range(queries.shape[0]):
        raw = jnp.dot(keys, queries_t[g], preferred_element_type=jnp.float32)
        logits = jnp.where(allowed, raw * scale, masked_value)
        prob = jnp.exp(logits - log_total[g : g + 1, :])
        d_prob = jnp.dot(values, d_att_t[g], preferred_element_type=jnp.float32)
        d_raw = (prob * (d_prob - delta[g : g + 1, :]) * scale).astype(jnp.bfloat16)
        d_value += jnp.dot(
            prob.astype(jnp.bfloat16), d_att[g], preferred_element_type=jnp.float32
        )
        d_key += jnp.dot(d_raw, queries[g], preferred_element_type=jnp.float32)
        d_query_t[g] += jnp.dot(keys_t[...], d_raw, preferred_element_type=jnp.float32)
    d_kv[...] = jnp.concatenate([d_key, d_value], axis=1).astype(jnp.bfloat16)


def attend_back(key_values, queries_b, d_att_b, log_total, delta, lowest, highest_key):
    count, width = queries_b.shape
    groups = width // HD
    total = key_values.shape[0]
    by_head = queries_b.reshape(count, groups, HD)
    d_by_head = d_att_b.reshape(count, groups, HD)

    def whole(*shape):
        return pl.BlockSpec(shape, lambda s: (0,) * len(shape))

    d_pair, d_query_t = pl.pallas_call(
        attend_back_kernel,
        grid=(total // KEY_BLOCK,),
        out_shape=[
            jax.ShapeDtypeStruct((total, 2 * HD), jnp.bfloat16),
            jax.ShapeDtypeStruct((groups, HD, count), jnp.float32),
        ],
        in_specs=[
            pl.BlockSpec((KEY_BLOCK, 2 * HD), lambda s: (s, 0)),
            pl.BlockSpec((HD, KEY_BLOCK), lambda s: (0, s)),
            whole(groups, count, HD),
            whole(groups, HD, count),
            whole(groups, count, HD),
            whole(groups, HD, count),
            whole(groups, count),
            whole(groups, count),
            whole(1, count),
            whole(1, count),
        ],
        out_specs=[pl.BlockSpec((KEY_BLOCK, 2 * HD), lambda s: (s, 0)), whole(groups, HD, count)],
        compiler_params=pltpu.CompilerParams(vmem_limit_bytes=24 * 2**20),
        cost_estimate=pl.CostEstimate(
            flops=10 * groups * HD * count * total,
            bytes_accessed=8 * total * HD,
            transcendentals=groups * count * total,
        ),
        name="attend_back",
    )(
        key_values,
        key_values[:, :HD].T,
        by_head.transpose(1, 0, 2),
        by_head.transpose(1, 2, 0),
        d_by_head.transpose(1, 0, 2),
        d_by_head.transpose(1, 2, 0),
        log_total,
        delta,
        lowest,
        highest_key,
    )
    return d_pair, d_query_t.transpose(2, 0, 1).reshape(count, width)


def from_everyone(value, axis):
    copies = jnp.broadcast_to(value, (lax.axis_size(axis), *value.shape))
    return lax.all_to_all(copies, axis, split_axis=0, concat_axis=0, tiled=True)


def joined_along(pieces, dim):
    shape = list(pieces.shape[1:])
    shape[dim] *= pieces.shape[0]
    return jnp.moveaxis(pieces, 0, dim).reshape(shape)


def gathered_copies(value, axis, dim):
    pieces = from_everyone(value, axis)
    return joined_along(pieces, dim)


def passed_along(value, axis, by):
    count = lax.axis_size(axis)
    pairs = [(i, i + by) for i in range(count) if 0 <= i + by < count]
    return lax.ppermute(value, axis, pairs)


def split_up(value, dim, count):
    before, after = (value.shape[:dim], value.shape[dim + 1 :])
    return jnp.moveaxis(value.reshape(*before, count, -1, *after), dim, 0)


def summed_on_arrival(value, axis, dim):
    pieces = split_up(value, dim, lax.axis_size(axis))
    arrived = lax.all_to_all(pieces, axis, split_axis=0, concat_axis=0, tiled=True)
    return arrived.astype(jnp.float32).sum(axis=0)


def rms_norm(value, gain):
    return value * lax.rsqrt(jnp.mean(value * value, axis=-1, keepdims=True) + norm_eps) * gain


def silu_slope(value):
    sigma = jax.nn.sigmoid(value)
    return sigma * (1.0 + value * (1.0 - sigma))


def doc_layout(doc_row, start_row, item_count):
    ends = jnp.cumsum(doc_row)
    starts = ends - doc_row
    token_index = start_row + jnp.arange(item_count, dtype=jnp.int32)
    segment = jnp.sum((token_index[:, None] >= ends[None, :]).astype(jnp.int32), axis=1)
    picked = segment[:, None] == jnp.arange(doc_row.shape[0], dtype=jnp.int32)[None, :]
    begin = jnp.sum(jnp.where(picked, starts[None, :], 0), axis=1)
    return (segment, token_index - begin)


def rope_tables(position):
    freq = rope_base ** (-2.0 * jnp.arange(HD // 2, dtype=jnp.float32) / HD)
    angle = position.astype(jnp.float32)[:, None] * freq[None, :]
    return (jnp.cos(angle), jnp.sin(angle))


def rotate(value, cosine, sine):
    shaped = value.reshape(value.shape[0], -1, 2, HD // 2)
    first_half = shaped[:, :, 0]
    second_half = shaped[:, :, 1]
    cos_part = cosine[:, None, :]
    sin_part = sine[:, None, :]
    turned = jnp.stack(
        [
            first_half * cos_part - second_half * sin_part,
            second_half * cos_part + first_half * sin_part,
        ],
        axis=2,
    )
    return turned.reshape(value.shape)


def conv_act(extended, conv_taps, conv_bias, seg_ext):
    item_count = extended.shape[0] - (CONV - 1)
    own_seg = seg_ext[CONV - 1 :]
    total = conv_bias[None, :] + conv_taps[CONV - 1][None, :] * extended[CONV - 1 :]
    for back in range(1, CONV):
        begin = CONV - 1 - back
        same = seg_ext[begin : begin + item_count] == own_seg
        total = total + conv_taps[CONV - 1 - back][None, :] * jnp.where(
            same[:, None], extended[begin : begin + item_count], 0.0
        )
    return jax.nn.silu(total)


def decay_terms(drive_input, dt_bias, a_log):
    dt_step = jax.nn.softplus(drive_input + dt_bias)
    order = jnp.arange(dt_step.shape[0], dtype=jnp.int32)
    upto = (order[None, :] <= order[:, None]).astype(jnp.float32)
    return (dt_step, jnp.dot(upto, -dt_step * jnp.exp(a_log), precision=highest))


def ssd_output(
    inner_input, b_mat, c_mat, drive_input, dt_bias, a_log, d_skip, segment, position, state_in
):
    item_count = inner_input.shape[0]
    head_total = drive_input.shape[1]
    grouped_heads = inner_input.reshape(item_count, head_total, MAMBA_HEAD_SIZE)
    dt_step, log_cum = decay_terms(drive_input, dt_bias, a_log)
    token_order = jnp.arange(item_count, dtype=jnp.int32)
    causal = (token_order[None, :] <= token_order[:, None]) & (segment[None, :] == segment[:, None])
    spread = log_cum.T[:, :, None] - log_cum.T[:, None, :]
    kernel = jnp.where(causal[None], jnp.exp(jnp.where(causal[None], spread, 0.0)), 0.0)
    inner_prod = jnp.dot(c_mat, b_mat.T, precision=state_precision)
    mixing = kernel * inner_prod[None] * dt_step.T[:, None, :]
    final_result = jnp.einsum("hts,shp->thp", mixing, grouped_heads, precision=state_precision)
    carry_on = ((segment == segment[0]) & (position[0] != 0)).astype(jnp.float32)
    carried = jnp.einsum("tn,hpn->thp", c_mat, state_in, precision=state_precision)
    final_result = (
        final_result
        + carried * (jnp.exp(log_cum) * carry_on[:, None])[:, :, None]
        + d_skip[None, :, None] * grouped_heads
    )
    return final_result.reshape(item_count, head_total * MAMBA_HEAD_SIZE)


def ssd_summary(inner_input, b_mat, drive_input, dt_bias, a_log, segment, position):
    item_count = inner_input.shape[0]
    head_total = drive_input.shape[1]
    grouped_heads = inner_input.reshape(item_count, head_total, MAMBA_HEAD_SIZE)
    dt_step, log_cum = decay_terms(drive_input, dt_bias, a_log)
    in_last = (segment == segment[item_count - 1]).astype(jnp.float32)
    weight_last = jnp.exp(log_cum[item_count - 1][None, :] - log_cum) * dt_step * in_last[:, None]
    state = jnp.einsum("sh,shp,sn->hpn", weight_last, grouped_heads, b_mat, precision=state_precision)
    live = ((segment[item_count - 1] == segment[0]) & (position[0] != 0)).astype(jnp.float32)
    return (live * jnp.exp(log_cum[item_count - 1]), state)


def split_vector(vector, widths):
    q_width, k_width, s_width, b_width, h_width = widths
    channels = s_width + b_width
    conv_taps = vector[: CONV * channels].reshape(CONV, channels)
    offset = CONV * channels
    conv_bias = vector[offset : offset + channels]
    offset = offset + channels
    gated_gain = vector[offset : offset + s_width]
    offset = offset + s_width
    return (
        conv_taps,
        conv_bias,
        gated_gain,
        vector[offset : offset + h_width],
        vector[offset + h_width : offset + 2 * h_width],
        vector[offset + 2 * h_width : offset + 3 * h_width],
    )


def feature_sum(value):
    own = value.astype(jnp.bfloat16)
    return own.astype(jnp.float32) + other_core(own).astype(jnp.float32)


def norm_sum(value):
    return value + other_core(value)


def local_matrices(w_in, w_out, w_gu, w_down, layer_at):
    return (
        jnp.pad(w_in[layer_at, :, 0, :], ((0, 0), (0, IN_PAD - IN_COLS))).astype(jnp.bfloat16),
        w_gu[layer_at, :, 0, :].astype(jnp.bfloat16),
        w_out[layer_at, 0].T.astype(jnp.bfloat16),
        w_down[layer_at, 0].T.astype(jnp.bfloat16),
    )


def fetch_layer(w_in, w_out, w_gu, w_down, layer_at, after):
    parts = local_matrices(w_in, w_out, w_gu, w_down, layer_at)
    if after is None:
        return gather_weights(parts)
    parts, _ = lax.optimization_barrier((parts, after[0][:ROWS, :128]))
    filled = lax.all_gather(jnp.concatenate(parts, axis=1), FSDP_CTX, axis=0, tiled=True)
    bounds = [sum(WIDTHS[:k]) for k in range(1, len(WIDTHS))]
    return tuple(jnp.split(filled, bounds, axis=1))


def attention_logits(queries_b, key_values, allowed):
    grouped_heads = queries_b.reshape(queries_b.shape[0], -1, HD)
    raw = jnp.einsum(
        "tgd,sd->gts", grouped_heads, key_values[:, :HD], preferred_element_type=jnp.float32
    )
    return jnp.where(allowed[None], raw * HD ** (-0.5), masked_value)


def layer_forward(state, weights, vector, gains, context, widths):
    w_in_b, w_gu_b, w_out_t, w_down_t = weights
    segment, position, seg_ext, allowed, cosine, sine, lowest, highest_key = context
    q_width, k_width, s_width, b_width, h_width = widths
    conv_taps, conv_bias, gated_gain, a_log, dt_bias, d_skip = split_vector(vector, widths)
    item_count = state.shape[0]
    at_v = q_width + k_width
    at_z = at_v + k_width
    at_x = at_z + s_width
    at_t = at_x + s_width + b_width
    hidden_b = rms_norm(state, gains[0]).astype(jnp.bfloat16)
    proj = jnp.dot(hidden_b, w_in_b, preferred_element_type=jnp.float32)
    queries_b = rotate(proj[:, :q_width], cosine, sine).astype(jnp.bfloat16)
    pair = jnp.concatenate(
        [rotate(proj[:, q_width:at_v], cosine, sine), proj[:, at_v:at_z]], axis=1
    ).astype(jnp.bfloat16)
    key_values = gathered_copies(pair, CTX, 0)
    logits = attention_logits(queries_b, key_values, allowed)
    top = jnp.max(logits, axis=2, keepdims=True)
    log_total = top + jnp.log(jnp.sum(jnp.exp(logits - top), axis=2, keepdims=True))
    prob_b = jnp.exp(logits - log_total).astype(jnp.bfloat16)
    attended = jnp.einsum(
        "gts,sd->tgd", prob_b, key_values[:, HD:], preferred_element_type=jnp.float32
    ).reshape(item_count, q_width)
    mixed_in = proj[:, at_x:at_t]
    halo_rows = passed_along(mixed_in[item_count - (CONV - 1) :], CTX, 1)
    extended = jnp.concatenate([halo_rows, mixed_in], axis=0)
    active = conv_act(extended, conv_taps, conv_bias, seg_ext)
    own_part = active[:, s_width:].astype(jnp.bfloat16)
    other_part = other_core(own_part)
    leads = lax.axis_index("tp") == 0
    both = jnp.concatenate(
        [jnp.where(leads, own_part, other_part), jnp.where(leads, other_part, own_part)], axis=1
    ).astype(jnp.float32)
    inner_input = active[:, :s_width]
    drive_input = proj[:, at_t : at_t + h_width]
    decay_own, state_own = ssd_summary(
        inner_input, both[:, :MAMBA_STATE_SIZE], drive_input, dt_bias, a_log, segment, position
    )
    state_in = entering(decay_own, state_own, False)
    ssm = ssd_output(
        inner_input,
        both[:, :MAMBA_STATE_SIZE],
        both[:, MAMBA_STATE_SIZE:],
        drive_input,
        dt_bias,
        a_log,
        d_skip,
        segment,
        position,
        state_in,
    )
    gated = ssm * jax.nn.silu(proj[:, at_z:at_x])
    inverse = lax.rsqrt(norm_sum(jnp.sum(gated * gated, axis=1)) / DSSM + norm_eps)[:, None]
    features = jnp.concatenate([attended, gated * inverse * gated_gain], axis=1).astype(
        jnp.bfloat16
    )
    middle = state + feature_sum(
        jnp.einsum("tc,dc->td", features, w_out_t, preferred_element_type=jnp.float32)
    )
    hidden2_b = rms_norm(middle, gains[1]).astype(jnp.bfloat16)
    upgate = jnp.dot(hidden2_b, w_gu_b, preferred_element_type=jnp.float32)
    half_width = upgate.shape[1] // 2
    inner_b = (jax.nn.silu(upgate[:, :half_width]) * upgate[:, half_width:]).astype(jnp.bfloat16)
    final_result = middle + feature_sum(
        jnp.einsum("tf,df->td", inner_b, w_down_t, preferred_element_type=jnp.float32)
    )
    kept = (
        state,
        hidden_b,
        proj,
        queries_b,
        key_values,
        log_total,
        extended,
        active,
        both,
        state_in,
        decay_own,
        ssm,
        gated,
        inverse,
        features,
        middle,
        hidden2_b,
        upgate,
        inner_b,
        attended,
    )
    return (final_result, kept)


def layer_backward(grad_out, kept, weights, vector, gains, context, widths):
    w_in_b, w_gu_b, w_out_t, w_down_t = weights
    segment, position, seg_ext, allowed, cosine, sine, lowest, highest_key = context
    q_width, k_width, s_width, b_width, h_width = widths
    conv_taps, conv_bias, gated_gain, a_log, dt_bias, d_skip = split_vector(vector, widths)
    (
        state,
        hidden_b,
        proj,
        queries_b,
        key_values,
        log_total,
        extended,
        active,
        both,
        state_in,
        decay_own,
        ssm,
        gated,
        inverse,
        features,
        middle,
        hidden2_b,
        upgate,
        inner_b,
        attended,
    ) = kept
    item_count = state.shape[0]
    at_v = q_width + k_width
    at_z = at_v + k_width
    at_x = at_z + s_width
    at_t = at_x + s_width + b_width
    grad_b = grad_out.astype(jnp.bfloat16)
    grad_down = jnp.einsum(
        "td,tf->df", grad_b, inner_b, preferred_element_type=jnp.float32
    ).astype(jnp.bfloat16)
    d_inner = jnp.dot(grad_b, w_down_t, preferred_element_type=jnp.float32)
    half_width = upgate.shape[1] // 2
    gate_part = upgate[:, :half_width]
    d_upgate_b = jnp.concatenate(
        [
            d_inner * upgate[:, half_width:] * silu_slope(gate_part),
            d_inner * jax.nn.silu(gate_part),
        ],
        axis=1,
    ).astype(jnp.bfloat16)
    grad_gu = jnp.einsum(
        "td,tf->df", hidden2_b, d_upgate_b, preferred_element_type=jnp.float32
    ).astype(jnp.bfloat16)
    wide_part = jnp.concatenate([grad_gu, grad_down], axis=1)
    for axis in FSDP_CTX:
        wide_part = lax.psum_scatter(wide_part, axis, tiled=True)
    d_hidden2 = feature_sum(
        jnp.einsum("tf,df->td", d_upgate_b, w_gu_b, preferred_element_type=jnp.float32)
    )
    d_middle_norm, d_gain_mlp = jax.vjp(rms_norm, middle, gains[1])[1](d_hidden2)
    d_middle = grad_out + d_middle_norm
    mix_b = d_middle.astype(jnp.bfloat16)
    grad_out_proj = jnp.einsum(
        "td,tc->dc", mix_b, features, preferred_element_type=jnp.float32
    ).astype(jnp.bfloat16)
    d_features = jnp.dot(mix_b, w_out_t, preferred_element_type=jnp.float32)
    d_normed = d_features[:, q_width:]
    weighted = d_normed * gated_gain
    d_gated_gain = jnp.sum(d_normed * gated * inverse, axis=0)
    across = norm_sum(jnp.sum(weighted * gated, axis=1))[:, None]
    d_gated = weighted * inverse - gated * inverse**3 * across / DSSM
    gate_z = proj[:, at_z:at_x]
    d_ssm = d_gated * jax.nn.silu(gate_z)
    d_gate_z = d_gated * ssm * silu_slope(gate_z)
    inner_input = active[:, :s_width]
    drive_input = proj[:, at_t : at_t + h_width]

    def output_part(x_part, b_part, c_part, drive_part, bias_part, log_part, skip_part, carry_part):
        return ssd_output(
            x_part,
            b_part,
            c_part,
            drive_part,
            bias_part,
            log_part,
            skip_part,
            segment,
            position,
            carry_part,
        )

    output_pull = jax.vjp(
        output_part,
        inner_input,
        both[:, :MAMBA_STATE_SIZE],
        both[:, MAMBA_STATE_SIZE:],
        drive_input,
        dt_bias,
        a_log,
        d_skip,
        state_in,
    )[1]
    dx_one, db_one, dc_one, drive_one, bias_one, log_one, skip_grad, d_carry = output_pull(d_ssm)
    later = entering(decay_own, d_carry, True)

    def summary_part(x_part, b_part, drive_part, bias_part, log_part):
        return ssd_summary(x_part, b_part, drive_part, bias_part, log_part, segment, position)

    summary_pull = jax.vjp(
        summary_part, inner_input, both[:, :MAMBA_STATE_SIZE], drive_input, dt_bias, a_log
    )[1]
    dx_two, db_two, drive_two, bias_two, log_two = summary_pull(
        (jnp.sum(later * state_in, axis=(1, 2)), later)
    )
    d_both = jnp.concatenate([db_one + db_two, dc_one], axis=1)
    d_both_b = d_both.astype(jnp.bfloat16)
    leads = lax.axis_index("tp") == 0
    kept_part = jnp.where(leads, d_both_b[:, :b_width], d_both_b[:, b_width:])
    sent_part = jnp.where(leads, d_both_b[:, b_width:], d_both_b[:, :b_width])
    d_own = kept_part.astype(jnp.float32) + other_core(sent_part).astype(jnp.float32)

    def conv_part(ext_part, taps_part, bias_part):
        return conv_act(ext_part, taps_part, bias_part, seg_ext)

    conv_pull = jax.vjp(conv_part, extended, conv_taps, conv_bias)[1]
    d_extended, d_taps, d_bias = conv_pull(jnp.concatenate([dx_one + dx_two, d_own], axis=1))
    spill = passed_along(d_extended[: CONV - 1], CTX, -1)
    d_mixed = jnp.concatenate(
        [d_extended[CONV - 1 : item_count], d_extended[item_count:] + spill], axis=0
    )
    d_att_b = d_features[:, :q_width].astype(jnp.bfloat16)
    delta = jnp.sum(
        (d_att_b.astype(jnp.float32) * attended).reshape(item_count, -1, HD), axis=2
    ).T
    d_pair_all, d_query = attend_back(
        key_values, queries_b, d_att_b, log_total[:, :, 0], delta, lowest, highest_key
    )
    d_pair = summed_on_arrival(d_pair_all, CTX, 0)
    d_proj_b = jnp.concatenate(
        [
            rotate(d_query, cosine, -sine),
            rotate(d_pair[:, :HD], cosine, -sine),
            d_pair[:, HD:],
            d_gate_z,
            d_mixed,
            drive_one + drive_two,
            jnp.zeros((item_count, IN_PAD - IN_COLS), jnp.float32),
        ],
        axis=1,
    ).astype(jnp.bfloat16)
    grad_in = jnp.einsum(
        "td,tc->dc", hidden_b, d_proj_b, preferred_element_type=jnp.float32
    ).astype(jnp.bfloat16)
    d_hidden = feature_sum(
        jnp.einsum("tc,dc->td", d_proj_b, w_in_b, preferred_element_type=jnp.float32)
    )
    d_state_norm, d_gain_mix = jax.vjp(rms_norm, state, gains[0])[1](d_hidden)
    d_vector = jnp.concatenate(
        [
            d_taps.reshape(-1),
            d_bias,
            d_gated_gain,
            log_one + log_two,
            bias_one + bias_two,
            skip_grad,
        ]
    )
    return (
        d_middle + d_state_norm,
        (grad_in, grad_out_proj),
        wide_part.astype(jnp.float32),
        d_vector,
        jnp.stack([d_gain_mix, d_gain_mlp]),
    )


def adamw(weight, first_m, second_m, grad, rate, decay):
    first_new = beta_one * first_m + (1.0 - beta_one) * grad
    second_new = beta_two * second_m + (1.0 - beta_two) * grad * grad
    ratio = (
        first_new
        / (1.0 - beta_one**STEP)
        / (jnp.sqrt(second_new / (1.0 - beta_two**STEP)) + adam_eps)
    )
    return (first_new, second_new, weight - rate * (ratio + decay * weight))


def per_device(
    block_input,
    cotangent,
    lengths,
    w_in,
    w_out,
    w_gu,
    w_down,
    vectors,
    norm_gains,
    first_in,
    first_out,
    first_gu,
    first_down,
    first_vectors,
    first_gains,
    second_in,
    second_out,
    second_gu,
    second_down,
    second_vectors,
    second_gains,
):
    group_count = lax.axis_size("tp")
    widths = (
        HEADS * HD // group_count,
        KV_HEADS * HD // group_count,
        MAMBA_HEADS * MAMBA_HEAD_SIZE // group_count,
        2 * MAMBA_STATE_SIZE // group_count,
        MAMBA_HEADS // group_count,
    )
    item_count = block_input.shape[0]
    start_row = lax.axis_index(CTX) * item_count
    seq_total = item_count * lax.axis_size(CTX)
    doc_row = lengths[0]
    segment, position = doc_layout(doc_row, start_row, item_count)
    seg_ext = doc_layout(doc_row, start_row - (CONV - 1), item_count + CONV - 1)[0]
    key_seg = doc_layout(doc_row, 0, seq_total)[0]
    query_index = start_row + jnp.arange(item_count, dtype=jnp.int32)
    allowed = (jnp.arange(seq_total, dtype=jnp.int32)[None, :] <= query_index[:, None]) & (
        key_seg[None, :] == segment[:, None]
    )
    cosine, sine = rope_tables(position)
    lowest, highest_key = (query_index - position)[None, :], query_index[None, :]
    context = (segment, position, seg_ext, allowed, cosine, sine, lowest, highest_key)
    stored = []
    fetched = []
    state = block_input
    for layer_at in range(LAYERS):
        weights = fetch_layer(
            w_in, w_out, w_gu, w_down, layer_at, fetched[0] if fetched else None
        )
        state, kept = layer_forward(
            state, weights, vectors[layer_at, 0], norm_gains[layer_at], context, widths
        )
        stored.append(kept)
        fetched.append(weights)
    grad_state = cotangent
    shards = [None] * LAYERS
    small_grads = [None] * LAYERS
    vec = vectors.shape[-1]
    for layer_at in reversed(range(LAYERS)):
        grad_state, matrices, wide_part, d_vector, d_gains = layer_backward(
            grad_state,
            stored[layer_at],
            fetched[layer_at],
            vectors[layer_at, 0],
            norm_gains[layer_at],
            context,
            widths,
        )
        small = jnp.concatenate([d_vector, d_gains.reshape(-1)])
        span = -(-small.shape[0] // 1024) * 8
        small = jnp.pad(small, (0, span * 128 - small.shape[0])).reshape(span, 128)
        *pieces, small = scatter_gradients(matrices, small)
        shards[layer_at] = (
            jnp.concatenate(pieces[:4], axis=1)[:, :IN_COLS],
            wide_part[:, : 2 * D],
            jnp.concatenate(pieces[4:], axis=1).T,
            wide_part[:, 2 * D :].T,
        )
        small_grads[layer_at] = small.reshape(-1)
    grad_in_all = jnp.stack([p[0] for p in shards]).reshape(w_in.shape)
    grad_gu_all = jnp.stack([p[1] for p in shards]).reshape(w_gu.shape)
    grad_out_all = jnp.stack([p[2] for p in shards]).reshape(w_out.shape)
    grad_down_all = jnp.stack([p[3] for p in shards]).reshape(w_down.shape)
    vector_total = jnp.stack([v[:vec] for v in small_grads]).reshape(vectors.shape)
    gain_total = jnp.stack([v[vec : vec + 2 * D] for v in small_grads]).reshape(norm_gains.shape)
    up_in = adamw(w_in, first_in, second_in, grad_in_all, rate_matrix, decay_rate)
    up_out = adamw(w_out, first_out, second_out, grad_out_all, rate_matrix, decay_rate)
    up_gu = adamw(w_gu, first_gu, second_gu, grad_gu_all, rate_matrix, decay_rate)
    up_down = adamw(w_down, first_down, second_down, grad_down_all, rate_matrix, decay_rate)
    up_vec = adamw(vectors, first_vectors, second_vectors, vector_total, rate_vector, 0.0)
    up_gain = adamw(norm_gains, first_gains, second_gains, gain_total, rate_vector, 0.0)
    return (
        state,
        grad_state,
        up_in[0],
        up_in[1],
        up_in[2],
        up_out[0],
        up_out[1],
        up_out[2],
        up_gu[0],
        up_gu[1],
        up_gu[2],
        up_down[0],
        up_down[1],
        up_down[2],
        up_vec[0],
        up_vec[1],
        up_vec[2],
        up_gain[0],
        up_gain[1],
        up_gain[2],
    )


def solution(mesh):
    torus = Mesh(
        mesh.devices.reshape(mesh.shape["fsdp"], 4, 4, mesh.shape["tp"]),
        ("fsdp", "ctx_0", "ctx_1", "tp"),
    )
    in_specs = (
        P(FSDP_CTX, None),
        P(FSDP_CTX, None),
        P("fsdp", None),
        P(None, FSDP_CTX, "tp", None),
        P(None, "tp", None, FSDP_CTX),
        P(None, FSDP_CTX, "tp", None),
        P(None, "tp", None, FSDP_CTX),
        P(None, "tp", None),
        P(),
        P(None, FSDP_CTX, "tp", None),
        P(None, "tp", None, FSDP_CTX),
        P(None, FSDP_CTX, "tp", None),
        P(None, "tp", None, FSDP_CTX),
        P(None, "tp", None),
        P(),
        P(None, FSDP_CTX, "tp", None),
        P(None, "tp", None, FSDP_CTX),
        P(None, FSDP_CTX, "tp", None),
        P(None, "tp", None, FSDP_CTX),
        P(None, "tp", None),
        P(),
    )
    out_specs = (
        P(FSDP_CTX, None),
        P(FSDP_CTX, None),
        P(None, FSDP_CTX, "tp", None),
        P(None, FSDP_CTX, "tp", None),
        P(None, FSDP_CTX, "tp", None),
        P(None, "tp", None, FSDP_CTX),
        P(None, "tp", None, FSDP_CTX),
        P(None, "tp", None, FSDP_CTX),
        P(None, FSDP_CTX, "tp", None),
        P(None, FSDP_CTX, "tp", None),
        P(None, FSDP_CTX, "tp", None),
        P(None, "tp", None, FSDP_CTX),
        P(None, "tp", None, FSDP_CTX),
        P(None, "tp", None, FSDP_CTX),
        P(None, "tp", None),
        P(None, "tp", None),
        P(None, "tp", None),
        P(),
        P(),
        P(),
    )
    return jax.shard_map(
        per_device, mesh=torus, in_specs=in_specs, out_specs=out_specs, check_vma=False
    )
```

```python
import functools

import jax
import jax.numpy as jnp
from jax import lax
from jax.experimental import pallas as pl
from jax.experimental.pallas import tpu as pltpu
from jax.sharding import Mesh
from jax.sharding import PartitionSpec as P

HEADS = 8
KV_HEADS = 2
HD = 64
MAMBA_HEADS = 24
MAMBA_HEAD_SIZE = 64
MAMBA_STATE_SIZE = 128
CONV = 4
LAYERS = 2
STEP = 10
DSSM = 1536
FSDP_CTX = ("fsdp", "ctx_0", "ctx_1")
CTX = ("ctx_0", "ctx_1")


highest = lax.Precision.HIGHEST
state_precision = lax.Precision.DEFAULT
D = 1024
IN_COLS = 2060
IN_PAD = 2176
AXES = ("fsdp", "ctx_0", "ctx_1")
SIDE = 4
ROWS = 16
STREAMS = (
    (0, 0, 384, (0, 1, 2), 1),
    (0, 384, 384, (0, 1, 2), -1),
    (0, 768, 384, (1, 2, 0), 1),
    (0, 1152, 384, (1, 2, 0), -1),
    (0, 1536, 384, (2, 0, 1), 1),
    (0, 1920, 256, (2, 0, 1), -1),
)
GRAD_STREAMS = (
    (0, 0, 896, (0, 1, 2), 1),
    (0, 896, 768, (0, 1, 2), -1),
    (0, 1664, 256, (1, 2, 0), 1),
    (0, 1920, 256, (2, 0, 1), -1),
    (1, 0, 2048, (1, 2), 1),
    (1, 2048, 2048, (1, 2), -1),
    (2, 0, 1152, (1, 2), 1),
    (2, 1152, 1024, (2, 1), -1),
    (3, 0, 2048, (2, 1), 1),
    (3, 2048, 2048, (2, 1), -1),
)
GRAD_COUNT = len(GRAD_STREAMS)
KEY_BLOCK = 512
norm_eps = 1e-05
rope_base = 100000000000.0
masked_value = -1e30
beta_one = 0.9
beta_two = 0.95
adam_eps = 1e-08
decay_rate = 0.1
rate_matrix = 0.05
rate_vector = 0.5


def ring_places():
    return tuple(lax.axis_index(a) for a in AXES)


def ring_step(places, axis, by):
    return {AXES[axis]: lax.rem(places[axis] + (by + SIDE), SIDE)}


def greet_neighbours(places):
    barrier = pltpu.get_barrier_semaphore()
    for axis in range(3):
        for by in (1, -1):
            pl.semaphore_signal(
                barrier,
                inc=1,
                device_id=ring_step(places, axis, by),
                device_id_type=pl.DeviceIdType.MESH,
            )
    pl.semaphore_wait(barrier, 6)


def remote(src, dst, send, recv, device):
    return pltpu.make_async_remote_copy(
        src_ref=src,
        dst_ref=dst,
        send_sem=send,
        recv_sem=recv,
        device_id=device,
        device_id_type=pl.DeviceIdType.MESH,
    )


def gather_kernel(shard, full, send, recv, own_sem):
    places = ring_places()
    greet_neighbours(places)
    own = pltpu.make_async_copy(shard, full.at[places[0], places[1], places[2]], own_sem)
    own.start()
    started = []

    def region(number, stage, place):
        _, first, width, order, _ = STREAMS[number]
        order = order[::-1]
        index = list(places)
        for axis in order[:stage]:
            index[axis] = slice(None)
        index[order[stage]] = place
        return full.at[(*index, slice(None), pl.ds(first, width))]

    def launch(number, stage, kind):
        _, first, width, order, way = STREAMS[number]
        axis = order[::-1][stage]
        here = places[axis]
        if kind == 2:
            source = target = region(number, stage, lax.rem(here + (SIDE - way), SIDE))
        else:
            source = target = region(number, stage, here)
            if stage == 0:
                source = shard.at[:, pl.ds(first, width)]
        copy = remote(
            source,
            target,
            send.at[number, stage, kind],
            recv.at[number, stage, kind],
            ring_step(places, axis, -way if kind == 1 else way),
        )
        copy.start()
        started.append(copy)
        return copy

    for stage in range(3):
        if stage == 1:
            own.wait()
        first, back = [], []
        for n in range(6):
            first.append(launch(n, stage, 0))
            back.append(launch(n, stage, 1))
        onward = []
        for n in range(6):
            first[n].wait_recv()
            onward.append(launch(n, stage, 2))
        for n in range(6):
            back[n].wait_recv()
            onward[n].wait_recv()
    for copy in started:
        copy.wait_send()


def gather_weights(part):
    out = pl.pallas_call(
        gather_kernel,
        out_shape=jax.ShapeDtypeStruct((4, 4, 4, *part.shape), part.dtype),
        in_specs=[pl.BlockSpec(memory_space=pl.ANY)],
        out_specs=pl.BlockSpec(memory_space=pl.ANY),
        scratch_shapes=[
            pltpu.SemaphoreType.DMA((6, 3, 3)),
            pltpu.SemaphoreType.DMA((6, 3, 3)),
            pltpu.SemaphoreType.DMA,
        ],
        compiler_params=pltpu.CompilerParams(collective_id=0, has_side_effects=True),
        cost_estimate=pl.CostEstimate(flops=0, bytes_accessed=80000000, transcendentals=0),
        name="gather_weights",
    )(part)
    return out.reshape(D, part.shape[-1])


def scatter_kernel(*refs):
    count = GRAD_COUNT
    grads, small = refs[:4], refs[4]
    refs = refs[5:]
    outs, small_out = refs[:count], refs[count]
    refs = refs[count + 1 :]
    ahead, mine = refs[:count], refs[count : 2 * count]
    refs = refs[2 * count :]
    arrived = (refs[:count], refs[count : 2 * count], refs[2 * count : 2 * count + 4])
    small_in, send, recv, own_sem, small_send, small_recv = refs[2 * count + 4 :]
    places = ring_places()
    greet_neighbours(places)
    started = []

    def near(axis, by):
        return lax.rem(places[axis] + (by + SIDE), SIDE)

    def block(number, stage, place):
        at, first, width, order, _ = GRAD_STREAMS[number]
        axis = order[stage]
        dims = sorted(order)
        if stage == 0:
            index = [slice(None)] * len(dims)
            index[dims.index(axis)] = place
            return grads[at].at[(*index, slice(None), pl.ds(first, width))]
        left = [a for a in dims if a != order[0]]
        index = [slice(None)] * len(left)
        for done in order[1:stage]:
            index[left.index(done)] = places[done]
        index[left.index(axis)] = place
        return mine[number].at[tuple(index)]

    def launch(number, stage, kind, source):
        axis, way = GRAD_STREAMS[number][3][stage], GRAD_STREAMS[number][4]
        copy = remote(
            source,
            arrived[stage][number].at[kind],
            send.at[number, stage, kind],
            recv.at[number, stage, kind],
            ring_step(places, axis, -way if kind == 2 else way),
        )
        copy.start()
        started.append(copy)
        return copy

    def add_into(target, source, lead):
        def one(total, part):
            total[...] = total[...] + part[...]

        if lead == 2:

            def body(k, carry):
                one(target.at[k // 4, k % 4], source.at[k // 4, k % 4])
                return carry

            lax.fori_loop(0, 16, body, 0)
        elif lead == 1:

            def body(k, carry):
                one(target.at[k], source.at[k])
                return carry

            lax.fori_loop(0, 4, body, 0)
        else:
            one(target, source)

    def small_exchange(step):
        axis, odd = step // 2, step % 2
        here = places[axis]
        partner = 3 - here if odd else here + 1 - 2 * lax.rem(here, 2)
        copy = remote(
            small_out,
            small_in.at[step],
            small_send.at[step],
            small_recv.at[step],
            {AXES[axis]: partner},
        )
        copy.start()
        return copy

    def small_finish(copy, step):
        copy.wait_send()
        copy.wait_recv()
        small_out[...] = small_out[...] + small_in[step]

    local = {}
    small_out[...] = small[...]
    for stage in range(3):
        active = [n for n in range(count) if len(GRAD_STREAMS[n][3]) > stage]
        first, back, onward = {}, {}, {}
        for n in active:
            axis, way = GRAD_STREAMS[n][3][stage], GRAD_STREAMS[n][4]
            first[n] = launch(n, stage, 0, block(n, stage, near(axis, 2)))
        for n in active:
            axis, way = GRAD_STREAMS[n][3][stage], GRAD_STREAMS[n][4]
            if stage == 0:
                pair = (
                    pltpu.make_async_copy(block(n, 0, near(axis, way)), ahead[n], own_sem.at[n, 0]),
                    pltpu.make_async_copy(block(n, 0, places[axis]), mine[n], own_sem.at[n, 1]),
                )
                for copy in pair:
                    copy.start()
                local[n] = pair
            back[n] = launch(n, stage, 2, block(n, stage, near(axis, -way)))
        step = small_exchange(2 * stage)
        for n in active:
            axis, way = GRAD_STREAMS[n][3][stage], GRAD_STREAMS[n][4]
            if stage == 0:
                local[n][0].wait()
                local[n][1].wait()
                target = ahead[n]
            else:
                target = block(n, stage, near(axis, way))
            first[n].wait_recv()
            add_into(target, arrived[stage][n].at[0], len(GRAD_STREAMS[n][3]) - 1 - stage)
            onward[n] = launch(n, stage, 1, target)
        small_finish(step, 2 * stage)
        step = small_exchange(2 * stage + 1)
        for n in active:
            order = GRAD_STREAMS[n][3]
            lead = len(order) - 1 - stage
            target = mine[n] if stage == 0 else block(n, stage, places[order[stage]])
            back[n].wait_recv()
            if lead:
                add_into(target, arrived[stage][n].at[2], lead)
            onward[n].wait_recv()
            if lead:
                add_into(target, arrived[stage][n].at[1], lead)
            else:
                outs[n][...] = target[...].astype(jnp.float32) + (
                    arrived[stage][n][1].astype(jnp.float32)
                    + arrived[stage][n][2].astype(jnp.float32)
                )
        small_finish(step, 2 * stage + 1)
    for copy in started:
        copy.wait_send()


def scatter_gradients(full, quarters, small):
    vmem = pl.BlockSpec(memory_space=pltpu.VMEM)

    def held(*lead_less):
        return [
            pltpu.VMEM((*lead, *(4,) * (len(s[3]) - less), ROWS, s[2]), jnp.bfloat16)
            for lead, less in lead_less
            for s in GRAD_STREAMS
            if len(s[3]) >= less
        ]

    scratch = held(((), 1), ((), 1), ((3,), 1), ((3,), 2), ((3,), 3))
    scratch += [
        pltpu.VMEM((6, *small.shape), jnp.float32),
        pltpu.SemaphoreType.DMA((GRAD_COUNT, 3, 3)),
        pltpu.SemaphoreType.DMA((GRAD_COUNT, 3, 3)),
        pltpu.SemaphoreType.DMA((GRAD_COUNT, 2)),
        pltpu.SemaphoreType.DMA((6,)),
        pltpu.SemaphoreType.DMA((6,)),
    ]
    shapes = [jax.ShapeDtypeStruct((ROWS, s[2]), jnp.float32) for s in GRAD_STREAMS]
    shapes.append(jax.ShapeDtypeStruct(small.shape, jnp.float32))
    views = [full.reshape(4, 4, 4, ROWS, full.shape[-1])]
    views += [q.reshape(4, 4, ROWS, q.shape[-1]) for q in quarters]
    return pl.pallas_call(
        scatter_kernel,
        out_shape=shapes,
        in_specs=[pl.BlockSpec(memory_space=pl.ANY)] * 4 + [vmem],
        out_specs=[vmem] * (GRAD_COUNT + 1),
        scratch_shapes=scratch,
        compiler_params=pltpu.CompilerParams(
            collective_id=1, has_side_effects=True, vmem_limit_bytes=28 * 2**20
        ),
        cost_estimate=pl.CostEstimate(flops=0, bytes_accessed=100000000, transcendentals=0),
        name="scatter_gradients",
    )(*views, small)


def other_core(value):
    return lax.ppermute(value, "tp", [(0, 1), (1, 0)])


def scan_kernel(
    reverse, parts, out, got, sums, rows, inside, decays, reply, back, send, recv
):
    here, outer = lax.axis_index("ctx_1"), lax.axis_index("ctx_0")
    head = parts.shape[2] - 16
    barrier = pltpu.get_barrier_semaphore()
    for axis, place in (("ctx_1", here), ("ctx_0", outer)):
        for by in range(1, SIDE):
            pl.semaphore_signal(
                barrier,
                inc=1,
                device_id={axis: lax.rem(place + by, SIDE)},
                device_id_type=pl.DeviceIdType.MESH,
            )
    pl.semaphore_wait(barrier, 6)
    started = []

    def spread(stage, axis, place, source, target):
        copies = []
        for by in (2, 1, 3):
            other = lax.rem(place + by, SIDE)
            copy = remote(
                source(other),
                target.at[place],
                send.at[stage, by - 1],
                recv.at[stage, by - 1],
                {axis: other},
            )
            copy.start()
            copies.append(copy)
        started.extend(copies)
        return copies

    def opened(ref, k):
        wide = ref[k].astype(jnp.float32)
        return wide[:, head : head + 1, :], wide[:, :head, :]

    order = range(SIDE - 1, -1, -1) if reverse else range(SIDE)
    copies = spread(0, "ctx_1", here, lambda other: parts.at[other], got)
    got[here] = parts[here]
    for copy in copies:
        copy.wait_recv()
    decay = state = None
    for k in order:
        own_decay, own_state = opened(got, k)
        if decay is None:
            decay, state = own_decay, own_state
        else:
            decays[k] = decay
            inside[k] = state
            decay, state = decay * own_decay, own_decay * state + own_state
    sums[:, :head, :] = state.astype(jnp.bfloat16)
    sums[:, head:, :] = jnp.broadcast_to(decay, (decay.shape[0], 16, decay.shape[2])).astype(
        jnp.bfloat16
    )
    copies = spread(1, "ctx_0", outer, lambda other: sums, rows)
    rows[outer] = sums[...]
    for copy in copies:
        copy.wait_recv()
    before = jnp.zeros_like(state)
    state = None
    for k in order:
        if state is not None:
            before = jnp.where(outer == k, state, before)
        own_decay, own_state = opened(rows, k)
        state = own_state if state is None else own_decay * state + own_state
    for k in order:
        if k == order[0]:
            reply[k] = before.astype(jnp.bfloat16)
        else:
            reply[k] = (decays[k] * before + inside[k]).astype(jnp.bfloat16)
    copies = spread(2, "ctx_1", here, lambda other: reply.at[other], back)
    back[here] = reply[here]
    for copy in copies:
        copy.wait_recv()
    out[...] = back[...].astype(jnp.float32)
    for copy in started:
        copy.wait_send()


def entering(decay, state, reverse):
    heads = decay.shape[0]
    chunk = heads // SIDE
    size, width = state.shape[1:]
    rows = jnp.broadcast_to(decay[:, None, None], (heads, 16, width))
    message = jnp.concatenate([state, rows], axis=1).astype(jnp.bfloat16)
    message = message.reshape(SIDE, chunk, size + 16, width)
    vmem = pl.BlockSpec(memory_space=pltpu.VMEM)
    out = pl.pallas_call(
        functools.partial(scan_kernel, reverse),
        out_shape=jax.ShapeDtypeStruct((SIDE, chunk, size, width), jnp.float32),
        in_specs=[vmem],
        out_specs=vmem,
        scratch_shapes=[
            pltpu.VMEM((SIDE, chunk, size + 16, width), jnp.bfloat16),
            pltpu.VMEM((chunk, size + 16, width), jnp.bfloat16),
            pltpu.VMEM((SIDE, chunk, size + 16, width), jnp.bfloat16),
            pltpu.VMEM((SIDE, chunk, size, width), jnp.float32),
            pltpu.VMEM((SIDE, chunk, 1, width), jnp.float32),
            pltpu.VMEM((SIDE, chunk, size, width), jnp.bfloat16),
            pltpu.VMEM((SIDE, chunk, size, width), jnp.bfloat16),
            pltpu.SemaphoreType.DMA((3, 3)),
            pltpu.SemaphoreType.DMA((3, 3)),
        ],
        compiler_params=pltpu.CompilerParams(
            collective_id=3 if reverse else 2, has_side_effects=True
        ),
        cost_estimate=pl.CostEstimate(flops=0, bytes_accessed=40000000, transcendentals=0),
        name="scan_back" if reverse else "scan_forth",
    )(message)
    return out.reshape(heads, size, width)


def attend_back_kernel(
    kv, keys_t, queries, queries_t, d_att, d_att_t, log_total, delta, lowest, highest_key, d_kv, d_query_t
):
    step = pl.program_id(0)

    @pl.when(step == 0)
    def _():
        d_query_t[...] = jnp.zeros_like(d_query_t)

    at = step * KEY_BLOCK + lax.broadcasted_iota(jnp.int32, (KEY_BLOCK, lowest.shape[1]), 0)
    allowed = (at >= lowest[...]) & (at <= highest_key[...])
    keys, values = kv[:, :HD], kv[:, HD:]
    scale = HD ** (-0.5)
    d_key = jnp.zeros((KEY_BLOCK, HD), jnp.float32)
    d_value = jnp.zeros((KEY_BLOCK, HD), jnp.float32)
    for g in range(queries.shape[0]):
        raw = jnp.dot(keys, queries_t[g], preferred_element_type=jnp.float32)
        logits = jnp.where(allowed, raw * scale, masked_value)
        prob = jnp.exp(logits - log_total[g : g + 1, :])
        d_prob = jnp.dot(values, d_att_t[g], preferred_element_type=jnp.float32)
        d_raw = (prob * (d_prob - delta[g : g + 1, :]) * scale).astype(jnp.bfloat16)
        d_value += jnp.dot(
            prob.astype(jnp.bfloat16), d_att[g], preferred_element_type=jnp.float32
        )
        d_key += jnp.dot(d_raw, queries[g], preferred_element_type=jnp.float32)
        d_query_t[g] += jnp.dot(keys_t[...], d_raw, preferred_element_type=jnp.float32)
    d_kv[...] = jnp.concatenate([d_key, d_value], axis=1).astype(jnp.bfloat16)


def attend_back(key_values, queries_b, d_att_b, log_total, delta, lowest, highest_key):
    count, width = queries_b.shape
    groups = width // HD
    total = key_values.shape[0]
    by_head = queries_b.reshape(count, groups, HD)
    d_by_head = d_att_b.reshape(count, groups, HD)

    def whole(*shape):
        return pl.BlockSpec(shape, lambda s: (0,) * len(shape))

    d_pair, d_query_t = pl.pallas_call(
        attend_back_kernel,
        grid=(total // KEY_BLOCK,),
        out_shape=[
            jax.ShapeDtypeStruct((total, 2 * HD), jnp.bfloat16),
            jax.ShapeDtypeStruct((groups, HD, count), jnp.float32),
        ],
        in_specs=[
            pl.BlockSpec((KEY_BLOCK, 2 * HD), lambda s: (s, 0)),
            pl.BlockSpec((HD, KEY_BLOCK), lambda s: (0, s)),
            whole(groups, count, HD),
            whole(groups, HD, count),
            whole(groups, count, HD),
            whole(groups, HD, count),
            whole(groups, count),
            whole(groups, count),
            whole(1, count),
            whole(1, count),
        ],
        out_specs=[pl.BlockSpec((KEY_BLOCK, 2 * HD), lambda s: (s, 0)), whole(groups, HD, count)],
        compiler_params=pltpu.CompilerParams(vmem_limit_bytes=24 * 2**20),
        cost_estimate=pl.CostEstimate(
            flops=10 * groups * HD * count * total,
            bytes_accessed=8 * total * HD,
            transcendentals=groups * count * total,
        ),
        name="attend_back",
    )(
        key_values,
        key_values[:, :HD].T,
        by_head.transpose(1, 0, 2),
        by_head.transpose(1, 2, 0),
        d_by_head.transpose(1, 0, 2),
        d_by_head.transpose(1, 2, 0),
        log_total,
        delta,
        lowest,
        highest_key,
    )
    return d_pair, d_query_t.transpose(2, 0, 1).reshape(count, width)


def from_everyone(value, axis):
    copies = jnp.broadcast_to(value, (lax.axis_size(axis), *value.shape))
    return lax.all_to_all(copies, axis, split_axis=0, concat_axis=0, tiled=True)


def joined_along(pieces, dim):
    shape = list(pieces.shape[1:])
    shape[dim] *= pieces.shape[0]
    return jnp.moveaxis(pieces, 0, dim).reshape(shape)


def gathered_copies(value, axis, dim):
    pieces = from_everyone(value, axis)
    return joined_along(pieces, dim)


def passed_along(value, axis, by):
    count = lax.axis_size(axis)
    pairs = [(i, i + by) for i in range(count) if 0 <= i + by < count]
    return lax.ppermute(value, axis, pairs)


def split_up(value, dim, count):
    before, after = (value.shape[:dim], value.shape[dim + 1 :])
    return jnp.moveaxis(value.reshape(*before, count, -1, *after), dim, 0)


def summed_on_arrival(value, axis, dim):
    pieces = split_up(value, dim, lax.axis_size(axis))
    arrived = lax.all_to_all(pieces, axis, split_axis=0, concat_axis=0, tiled=True)
    return arrived.astype(jnp.float32).sum(axis=0)


def rms_norm(value, gain):
    return value * lax.rsqrt(jnp.mean(value * value, axis=-1, keepdims=True) + norm_eps) * gain


def silu_slope(value):
    sigma = jax.nn.sigmoid(value)
    return sigma * (1.0 + value * (1.0 - sigma))


def doc_layout(doc_row, start_row, item_count):
    ends = jnp.cumsum(doc_row)
    starts = ends - doc_row
    token_index = start_row + jnp.arange(item_count, dtype=jnp.int32)
    segment = jnp.sum((token_index[:, None] >= ends[None, :]).astype(jnp.int32), axis=1)
    picked = segment[:, None] == jnp.arange(doc_row.shape[0], dtype=jnp.int32)[None, :]
    begin = jnp.sum(jnp.where(picked, starts[None, :], 0), axis=1)
    return (segment, token_index - begin)


def rope_tables(position):
    freq = rope_base ** (-2.0 * jnp.arange(HD // 2, dtype=jnp.float32) / HD)
    angle = position.astype(jnp.float32)[:, None] * freq[None, :]
    return (jnp.cos(angle), jnp.sin(angle))


def rotate(value, cosine, sine):
    shaped = value.reshape(value.shape[0], -1, 2, HD // 2)
    first_half = shaped[:, :, 0]
    second_half = shaped[:, :, 1]
    cos_part = cosine[:, None, :]
    sin_part = sine[:, None, :]
    turned = jnp.stack(
        [
            first_half * cos_part - second_half * sin_part,
            second_half * cos_part + first_half * sin_part,
        ],
        axis=2,
    )
    return turned.reshape(value.shape)


def conv_act(extended, conv_taps, conv_bias, seg_ext):
    item_count = extended.shape[0] - (CONV - 1)
    own_seg = seg_ext[CONV - 1 :]
    total = conv_bias[None, :] + conv_taps[CONV - 1][None, :] * extended[CONV - 1 :]
    for back in range(1, CONV):
        begin = CONV - 1 - back
        same = seg_ext[begin : begin + item_count] == own_seg
        total = total + conv_taps[CONV - 1 - back][None, :] * jnp.where(
            same[:, None], extended[begin : begin + item_count], 0.0
        )
    return jax.nn.silu(total)


def decay_terms(drive_input, dt_bias, a_log):
    dt_step = jax.nn.softplus(drive_input + dt_bias)
    order = jnp.arange(dt_step.shape[0], dtype=jnp.int32)
    upto = (order[None, :] <= order[:, None]).astype(jnp.float32)
    return (dt_step, jnp.dot(upto, -dt_step * jnp.exp(a_log), precision=highest))


def ssd_output(
    inner_input, b_mat, c_mat, drive_input, dt_bias, a_log, d_skip, segment, position, state_in
):
    item_count = inner_input.shape[0]
    head_total = drive_input.shape[1]
    grouped_heads = inner_input.reshape(item_count, head_total, MAMBA_HEAD_SIZE)
    dt_step, log_cum = decay_terms(drive_input, dt_bias, a_log)
    token_order = jnp.arange(item_count, dtype=jnp.int32)
    causal = (token_order[None, :] <= token_order[:, None]) & (segment[None, :] == segment[:, None])
    spread = log_cum.T[:, :, None] - log_cum.T[:, None, :]
    kernel = jnp.where(causal[None], jnp.exp(jnp.where(causal[None], spread, 0.0)), 0.0)
    inner_prod = jnp.dot(c_mat, b_mat.T, precision=state_precision)
    mixing = kernel * inner_prod[None] * dt_step.T[:, None, :]
    final_result = jnp.einsum("hts,shp->thp", mixing, grouped_heads, precision=state_precision)
    carry_on = ((segment == segment[0]) & (position[0] != 0)).astype(jnp.float32)
    carried = jnp.einsum("tn,hpn->thp", c_mat, state_in, precision=state_precision)
    final_result = (
        final_result
        + carried * (jnp.exp(log_cum) * carry_on[:, None])[:, :, None]
        + d_skip[None, :, None] * grouped_heads
    )
    return final_result.reshape(item_count, head_total * MAMBA_HEAD_SIZE)


def ssd_summary(inner_input, b_mat, drive_input, dt_bias, a_log, segment, position):
    item_count = inner_input.shape[0]
    head_total = drive_input.shape[1]
    grouped_heads = inner_input.reshape(item_count, head_total, MAMBA_HEAD_SIZE)
    dt_step, log_cum = decay_terms(drive_input, dt_bias, a_log)
    in_last = (segment == segment[item_count - 1]).astype(jnp.float32)
    weight_last = jnp.exp(log_cum[item_count - 1][None, :] - log_cum) * dt_step * in_last[:, None]
    state = jnp.einsum("sh,shp,sn->hpn", weight_last, grouped_heads, b_mat, precision=state_precision)
    live = ((segment[item_count - 1] == segment[0]) & (position[0] != 0)).astype(jnp.float32)
    return (live * jnp.exp(log_cum[item_count - 1]), state)


def split_vector(vector, widths):
    q_width, k_width, s_width, b_width, h_width = widths
    channels = s_width + b_width
    conv_taps = vector[: CONV * channels].reshape(CONV, channels)
    offset = CONV * channels
    conv_bias = vector[offset : offset + channels]
    offset = offset + channels
    gated_gain = vector[offset : offset + s_width]
    offset = offset + s_width
    return (
        conv_taps,
        conv_bias,
        gated_gain,
        vector[offset : offset + h_width],
        vector[offset + h_width : offset + 2 * h_width],
        vector[offset + 2 * h_width : offset + 3 * h_width],
    )


def feature_sum(value):
    own = value.astype(jnp.bfloat16)
    return own.astype(jnp.float32) + other_core(own).astype(jnp.float32)


def norm_sum(value):
    return value + other_core(value)


def local_matrices(w_in, w_out, w_gu, w_down, layer_at):
    return (
        jnp.pad(w_in[layer_at, :, 0, :], ((0, 0), (0, IN_PAD - IN_COLS))).astype(jnp.bfloat16),
        w_gu[layer_at, :, 0, :].astype(jnp.bfloat16),
        w_out[layer_at, 0].T.astype(jnp.bfloat16),
        w_down[layer_at, 0].T.astype(jnp.bfloat16),
    )


def fetch_layers(w_in, w_out, w_gu, w_down):
    parts = [local_matrices(w_in, w_out, w_gu, w_down, k) for k in range(LAYERS)]
    rest = (*parts[0][1:], *parts[1])
    filled = lax.all_gather(jnp.concatenate(rest, axis=1), FSDP_CTX, axis=0, tiled=True)
    bounds, at = [], 0
    for part in rest[:-1]:
        at += part.shape[1]
        bounds.append(at)
    pieces = jnp.split(filled, bounds, axis=1)
    return (gather_weights(parts[0][0]), *pieces[:3]), tuple(pieces[3:])


def attention_logits(queries_b, key_values, allowed):
    grouped_heads = queries_b.reshape(queries_b.shape[0], -1, HD)
    raw = jnp.einsum(
        "tgd,sd->gts", grouped_heads, key_values[:, :HD], preferred_element_type=jnp.float32
    )
    return jnp.where(allowed[None], raw * HD ** (-0.5), masked_value)


def layer_forward(state, weights, vector, gains, context, widths):
    w_in_b, w_gu_b, w_out_t, w_down_t = weights
    segment, position, seg_ext, allowed, cosine, sine, lowest, highest_key = context
    q_width, k_width, s_width, b_width, h_width = widths
    conv_taps, conv_bias, gated_gain, a_log, dt_bias, d_skip = split_vector(vector, widths)
    item_count = state.shape[0]
    at_v = q_width + k_width
    at_z = at_v + k_width
    at_x = at_z + s_width
    at_t = at_x + s_width + b_width
    hidden_b = rms_norm(state, gains[0]).astype(jnp.bfloat16)
    proj = jnp.dot(hidden_b, w_in_b, preferred_element_type=jnp.float32)
    queries_b = rotate(proj[:, :q_width], cosine, sine).astype(jnp.bfloat16)
    pair = jnp.concatenate(
        [rotate(proj[:, q_width:at_v], cosine, sine), proj[:, at_v:at_z]], axis=1
    ).astype(jnp.bfloat16)
    key_values = gathered_copies(pair, CTX, 0)
    logits = attention_logits(queries_b, key_values, allowed)
    top = jnp.max(logits, axis=2, keepdims=True)
    log_total = top + jnp.log(jnp.sum(jnp.exp(logits - top), axis=2, keepdims=True))
    prob_b = jnp.exp(logits - log_total).astype(jnp.bfloat16)
    attended = jnp.einsum(
        "gts,sd->tgd", prob_b, key_values[:, HD:], preferred_element_type=jnp.float32
    ).reshape(item_count, q_width)
    mixed_in = proj[:, at_x:at_t]
    halo_rows = passed_along(mixed_in[item_count - (CONV - 1) :], CTX, 1)
    extended = jnp.concatenate([halo_rows, mixed_in], axis=0)
    active = conv_act(extended, conv_taps, conv_bias, seg_ext)
    own_part = active[:, s_width:].astype(jnp.bfloat16)
    other_part = other_core(own_part)
    leads = lax.axis_index("tp") == 0
    both = jnp.concatenate(
        [jnp.where(leads, own_part, other_part), jnp.where(leads, other_part, own_part)], axis=1
    ).astype(jnp.float32)
    inner_input = active[:, :s_width]
    drive_input = proj[:, at_t : at_t + h_width]
    decay_own, state_own = ssd_summary(
        inner_input, both[:, :MAMBA_STATE_SIZE], drive_input, dt_bias, a_log, segment, position
    )
    state_in = entering(decay_own, state_own, False)
    ssm = ssd_output(
        inner_input,
        both[:, :MAMBA_STATE_SIZE],
        both[:, MAMBA_STATE_SIZE:],
        drive_input,
        dt_bias,
        a_log,
        d_skip,
        segment,
        position,
        state_in,
    )
    gated = ssm * jax.nn.silu(proj[:, at_z:at_x])
    inverse = lax.rsqrt(norm_sum(jnp.sum(gated * gated, axis=1)) / DSSM + norm_eps)[:, None]
    features = jnp.concatenate([attended, gated * inverse * gated_gain], axis=1).astype(
        jnp.bfloat16
    )
    middle = state + feature_sum(
        jnp.einsum("tc,dc->td", features, w_out_t, preferred_element_type=jnp.float32)
    )
    hidden2_b = rms_norm(middle, gains[1]).astype(jnp.bfloat16)
    upgate = jnp.dot(hidden2_b, w_gu_b, preferred_element_type=jnp.float32)
    half_width = upgate.shape[1] // 2
    inner_b = (jax.nn.silu(upgate[:, :half_width]) * upgate[:, half_width:]).astype(jnp.bfloat16)
    final_result = middle + feature_sum(
        jnp.einsum("tf,df->td", inner_b, w_down_t, preferred_element_type=jnp.float32)
    )
    kept = (
        state,
        hidden_b,
        proj,
        queries_b,
        key_values,
        log_total,
        extended,
        active,
        both,
        state_in,
        decay_own,
        ssm,
        gated,
        inverse,
        features,
        middle,
        hidden2_b,
        upgate,
        inner_b,
        attended,
    )
    return (final_result, kept)


def layer_backward(grad_out, kept, weights, vector, gains, context, widths):
    w_in_b, w_gu_b, w_out_t, w_down_t = weights
    segment, position, seg_ext, allowed, cosine, sine, lowest, highest_key = context
    q_width, k_width, s_width, b_width, h_width = widths
    conv_taps, conv_bias, gated_gain, a_log, dt_bias, d_skip = split_vector(vector, widths)
    (
        state,
        hidden_b,
        proj,
        queries_b,
        key_values,
        log_total,
        extended,
        active,
        both,
        state_in,
        decay_own,
        ssm,
        gated,
        inverse,
        features,
        middle,
        hidden2_b,
        upgate,
        inner_b,
        attended,
    ) = kept
    item_count = state.shape[0]
    at_v = q_width + k_width
    at_z = at_v + k_width
    at_x = at_z + s_width
    at_t = at_x + s_width + b_width
    grad_b = grad_out.astype(jnp.bfloat16)
    grad_down = jnp.einsum(
        "td,tf->df", grad_b, inner_b, preferred_element_type=jnp.float32
    ).astype(jnp.bfloat16)
    d_inner = jnp.dot(grad_b, w_down_t, preferred_element_type=jnp.float32)
    half_width = upgate.shape[1] // 2
    gate_part = upgate[:, :half_width]
    d_upgate_b = jnp.concatenate(
        [
            d_inner * upgate[:, half_width:] * silu_slope(gate_part),
            d_inner * jax.nn.silu(gate_part),
        ],
        axis=1,
    ).astype(jnp.bfloat16)
    grad_gu = jnp.einsum(
        "td,tf->df", hidden2_b, d_upgate_b, preferred_element_type=jnp.float32
    ).astype(jnp.bfloat16)
    d_hidden2 = feature_sum(
        jnp.einsum("tf,df->td", d_upgate_b, w_gu_b, preferred_element_type=jnp.float32)
    )
    d_middle_norm, d_gain_mlp = jax.vjp(rms_norm, middle, gains[1])[1](d_hidden2)
    d_middle = grad_out + d_middle_norm
    mix_b = d_middle.astype(jnp.bfloat16)
    grad_out_proj = jnp.einsum(
        "td,tc->dc", mix_b, features, preferred_element_type=jnp.float32
    ).astype(jnp.bfloat16)
    early = lax.psum_scatter(
        jnp.concatenate([grad_gu, grad_down, grad_out_proj], axis=1), "fsdp", tiled=True
    )
    d_features = jnp.dot(mix_b, w_out_t, preferred_element_type=jnp.float32)
    d_normed = d_features[:, q_width:]
    weighted = d_normed * gated_gain
    d_gated_gain = jnp.sum(d_normed * gated * inverse, axis=0)
    across = norm_sum(jnp.sum(weighted * gated, axis=1))[:, None]
    d_gated = weighted * inverse - gated * inverse**3 * across / DSSM
    gate_z = proj[:, at_z:at_x]
    d_ssm = d_gated * jax.nn.silu(gate_z)
    d_gate_z = d_gated * ssm * silu_slope(gate_z)
    inner_input = active[:, :s_width]
    drive_input = proj[:, at_t : at_t + h_width]

    def output_part(x_part, b_part, c_part, drive_part, bias_part, log_part, skip_part, carry_part):
        return ssd_output(
            x_part,
            b_part,
            c_part,
            drive_part,
            bias_part,
            log_part,
            skip_part,
            segment,
            position,
            carry_part,
        )

    output_pull = jax.vjp(
        output_part,
        inner_input,
        both[:, :MAMBA_STATE_SIZE],
        both[:, MAMBA_STATE_SIZE:],
        drive_input,
        dt_bias,
        a_log,
        d_skip,
        state_in,
    )[1]
    dx_one, db_one, dc_one, drive_one, bias_one, log_one, skip_grad, d_carry = output_pull(d_ssm)
    later = entering(decay_own, d_carry, True)

    def summary_part(x_part, b_part, drive_part, bias_part, log_part):
        return ssd_summary(x_part, b_part, drive_part, bias_part, log_part, segment, position)

    summary_pull = jax.vjp(
        summary_part, inner_input, both[:, :MAMBA_STATE_SIZE], drive_input, dt_bias, a_log
    )[1]
    dx_two, db_two, drive_two, bias_two, log_two = summary_pull(
        (jnp.sum(later * state_in, axis=(1, 2)), later)
    )
    d_both = jnp.concatenate([db_one + db_two, dc_one], axis=1)
    d_both_b = d_both.astype(jnp.bfloat16)
    leads = lax.axis_index("tp") == 0
    kept_part = jnp.where(leads, d_both_b[:, :b_width], d_both_b[:, b_width:])
    sent_part = jnp.where(leads, d_both_b[:, b_width:], d_both_b[:, :b_width])
    d_own = kept_part.astype(jnp.float32) + other_core(sent_part).astype(jnp.float32)

    def conv_part(ext_part, taps_part, bias_part):
        return conv_act(ext_part, taps_part, bias_part, seg_ext)

    conv_pull = jax.vjp(conv_part, extended, conv_taps, conv_bias)[1]
    d_extended, d_taps, d_bias = conv_pull(jnp.concatenate([dx_one + dx_two, d_own], axis=1))
    spill = passed_along(d_extended[: CONV - 1], CTX, -1)
    d_mixed = jnp.concatenate(
        [d_extended[CONV - 1 : item_count], d_extended[item_count:] + spill], axis=0
    )
    d_att_b = d_features[:, :q_width].astype(jnp.bfloat16)
    delta = jnp.sum(
        (d_att_b.astype(jnp.float32) * attended).reshape(item_count, -1, HD), axis=2
    ).T
    d_pair_all, d_query = attend_back(
        key_values, queries_b, d_att_b, log_total[:, :, 0], delta, lowest, highest_key
    )
    d_pair = summed_on_arrival(d_pair_all, CTX, 0)
    d_proj_b = jnp.concatenate(
        [
            rotate(d_query, cosine, -sine),
            rotate(d_pair[:, :HD], cosine, -sine),
            d_pair[:, HD:],
            d_gate_z,
            d_mixed,
            drive_one + drive_two,
            jnp.zeros((item_count, IN_PAD - IN_COLS), jnp.float32),
        ],
        axis=1,
    ).astype(jnp.bfloat16)
    grad_in = jnp.einsum(
        "td,tc->dc", hidden_b, d_proj_b, preferred_element_type=jnp.float32
    ).astype(jnp.bfloat16)
    d_hidden = feature_sum(
        jnp.einsum("tc,dc->td", d_proj_b, w_in_b, preferred_element_type=jnp.float32)
    )
    d_state_norm, d_gain_mix = jax.vjp(rms_norm, state, gains[0])[1](d_hidden)
    d_vector = jnp.concatenate(
        [
            d_taps.reshape(-1),
            d_bias,
            d_gated_gain,
            log_one + log_two,
            bias_one + bias_two,
            skip_grad,
        ]
    )
    return (
        d_middle + d_state_norm,
        grad_in,
        early,
        d_vector,
        jnp.stack([d_gain_mix, d_gain_mlp]),
    )


def adamw(weight, first_m, second_m, grad, rate, decay):
    first_new = beta_one * first_m + (1.0 - beta_one) * grad
    second_new = beta_two * second_m + (1.0 - beta_two) * grad * grad
    ratio = (
        first_new
        / (1.0 - beta_one**STEP)
        / (jnp.sqrt(second_new / (1.0 - beta_two**STEP)) + adam_eps)
    )
    return (first_new, second_new, weight - rate * (ratio + decay * weight))


def per_device(
    block_input,
    cotangent,
    lengths,
    w_in,
    w_out,
    w_gu,
    w_down,
    vectors,
    norm_gains,
    first_in,
    first_out,
    first_gu,
    first_down,
    first_vectors,
    first_gains,
    second_in,
    second_out,
    second_gu,
    second_down,
    second_vectors,
    second_gains,
):
    group_count = lax.axis_size("tp")
    widths = (
        HEADS * HD // group_count,
        KV_HEADS * HD // group_count,
        MAMBA_HEADS * MAMBA_HEAD_SIZE // group_count,
        2 * MAMBA_STATE_SIZE // group_count,
        MAMBA_HEADS // group_count,
    )
    item_count = block_input.shape[0]
    start_row = lax.axis_index(CTX) * item_count
    seq_total = item_count * lax.axis_size(CTX)
    doc_row = lengths[0]
    segment, position = doc_layout(doc_row, start_row, item_count)
    seg_ext = doc_layout(doc_row, start_row - (CONV - 1), item_count + CONV - 1)[0]
    key_seg = doc_layout(doc_row, 0, seq_total)[0]
    query_index = start_row + jnp.arange(item_count, dtype=jnp.int32)
    allowed = (jnp.arange(seq_total, dtype=jnp.int32)[None, :] <= query_index[:, None]) & (
        key_seg[None, :] == segment[:, None]
    )
    cosine, sine = rope_tables(position)
    lowest, highest_key = (query_index - position)[None, :], query_index[None, :]
    context = (segment, position, seg_ext, allowed, cosine, sine, lowest, highest_key)
    stored = []
    state = block_input
    fetched = fetch_layers(w_in, w_out, w_gu, w_down)
    for layer_at in range(LAYERS):
        weights = fetched[layer_at]
        state, kept = layer_forward(
            state, weights, vectors[layer_at, 0], norm_gains[layer_at], context, widths
        )
        stored.append(kept)
    grad_state = cotangent
    early_parts = [None] * LAYERS
    late_parts = [None] * LAYERS
    small_parts = [None] * LAYERS
    vec = vectors.shape[-1]
    for layer_at in reversed(range(LAYERS)):
        grad_state, late, early, d_vector, d_gains = layer_backward(
            grad_state,
            stored[layer_at],
            fetched[layer_at],
            vectors[layer_at, 0],
            norm_gains[layer_at],
            context,
            widths,
        )
        early_parts[layer_at] = early
        late_parts[layer_at] = lax.psum_scatter(late, "fsdp", tiled=True) if layer_at else late
        small_parts[layer_at] = jnp.concatenate([d_vector, d_gains.reshape(-1)])
    small = jnp.concatenate(small_parts)
    span = -(-small.shape[0] // 1024) * 8
    small = jnp.pad(small, (0, span * 128 - small.shape[0])).reshape(span, 128)
    *pieces, small = scatter_gradients(
        late_parts[0], (early_parts[1], late_parts[1], early_parts[0]), small
    )
    shards = [
        (
            jnp.concatenate(some, axis=1)[:, :IN_COLS],
            wide,
            rest[:, D:].T,
            rest[:, :D].T,
        )
        for some, wide, rest in (
            (pieces[:4], pieces[8], pieces[9]),
            (pieces[6:8], pieces[4], pieces[5]),
        )
    ]
    small_grads = small.reshape(-1)[: LAYERS * (vec + 2 * D)].reshape(LAYERS, vec + 2 * D)
    grad_in_all = jnp.stack([p[0] for p in shards]).reshape(w_in.shape)
    grad_gu_all = jnp.stack([p[1] for p in shards]).reshape(w_gu.shape)
    grad_out_all = jnp.stack([p[2] for p in shards]).reshape(w_out.shape)
    grad_down_all = jnp.stack([p[3] for p in shards]).reshape(w_down.shape)
    vector_total = small_grads[:, :vec].reshape(vectors.shape)
    gain_total = small_grads[:, vec:].reshape(norm_gains.shape)
    up_in = adamw(w_in, first_in, second_in, grad_in_all, rate_matrix, decay_rate)
    up_out = adamw(w_out, first_out, second_out, grad_out_all, rate_matrix, decay_rate)
    up_gu = adamw(w_gu, first_gu, second_gu, grad_gu_all, rate_matrix, decay_rate)
    up_down = adamw(w_down, first_down, second_down, grad_down_all, rate_matrix, decay_rate)
    up_vec = adamw(vectors, first_vectors, second_vectors, vector_total, rate_vector, 0.0)
    up_gain = adamw(norm_gains, first_gains, second_gains, gain_total, rate_vector, 0.0)
    return (
        state,
        grad_state,
        up_in[0],
        up_in[1],
        up_in[2],
        up_out[0],
        up_out[1],
        up_out[2],
        up_gu[0],
        up_gu[1],
        up_gu[2],
        up_down[0],
        up_down[1],
        up_down[2],
        up_vec[0],
        up_vec[1],
        up_vec[2],
        up_gain[0],
        up_gain[1],
        up_gain[2],
    )


def solution(mesh):
    torus = Mesh(
        mesh.devices.reshape(mesh.shape["fsdp"], 4, 4, mesh.shape["tp"]),
        ("fsdp", "ctx_0", "ctx_1", "tp"),
    )
    in_specs = (
        P(FSDP_CTX, None),
        P(FSDP_CTX, None),
        P("fsdp", None),
        P(None, FSDP_CTX, "tp", None),
        P(None, "tp", None, FSDP_CTX),
        P(None, FSDP_CTX, "tp", None),
        P(None, "tp", None, FSDP_CTX),
        P(None, "tp", None),
        P(),
        P(None, FSDP_CTX, "tp", None),
        P(None, "tp", None, FSDP_CTX),
        P(None, FSDP_CTX, "tp", None),
        P(None, "tp", None, FSDP_CTX),
        P(None, "tp", None),
        P(),
        P(None, FSDP_CTX, "tp", None),
        P(None, "tp", None, FSDP_CTX),
        P(None, FSDP_CTX, "tp", None),
        P(None, "tp", None, FSDP_CTX),
        P(None, "tp", None),
        P(),
    )
    out_specs = (
        P(FSDP_CTX, None),
        P(FSDP_CTX, None),
        P(None, FSDP_CTX, "tp", None),
        P(None, FSDP_CTX, "tp", None),
        P(None, FSDP_CTX, "tp", None),
        P(None, "tp", None, FSDP_CTX),
        P(None, "tp", None, FSDP_CTX),
        P(None, "tp", None, FSDP_CTX),
        P(None, FSDP_CTX, "tp", None),
        P(None, FSDP_CTX, "tp", None),
        P(None, FSDP_CTX, "tp", None),
        P(None, "tp", None, FSDP_CTX),
        P(None, "tp", None, FSDP_CTX),
        P(None, "tp", None, FSDP_CTX),
        P(None, "tp", None),
        P(None, "tp", None),
        P(None, "tp", None),
        P(),
        P(),
        P(),
    )
    return jax.shard_map(
        per_device, mesh=torus, in_specs=in_specs, out_specs=out_specs, check_vma=False
    )
```

```python
import functools

import jax
import jax.numpy as jnp
from jax import lax
from jax.experimental import pallas as pl
from jax.experimental.pallas import tpu as pltpu
from jax.sharding import Mesh
from jax.sharding import PartitionSpec as P

HEADS = 8
KV_HEADS = 2
HD = 64
MAMBA_HEADS = 24
MAMBA_HEAD_SIZE = 64
MAMBA_STATE_SIZE = 128
CONV = 4
LAYERS = 2
STEP = 10
DSSM = 1536
FSDP_CTX = ("fsdp", "ctx_0", "ctx_1")
CTX = ("ctx_0", "ctx_1")


highest = lax.Precision.HIGHEST
state_precision = lax.Precision.DEFAULT
D = 1024
IN_COLS = 2060
IN_PAD = 2176
AXES = ("fsdp", "ctx_0", "ctx_1")
SIDE = 4
ROWS = 16
STREAMS = (
    (0, 0, 384, (0, 1, 2), 1),
    (0, 384, 384, (0, 1, 2), -1),
    (0, 768, 384, (1, 2, 0), 1),
    (0, 1152, 384, (1, 2, 0), -1),
    (0, 1536, 384, (2, 0, 1), 1),
    (0, 1920, 256, (2, 0, 1), -1),
)
GRAD_STREAMS = (
    (0, 0, 896, (0, 1, 2), 1),
    (0, 896, 768, (0, 1, 2), -1),
    (0, 1664, 256, (1, 2, 0), 1),
    (0, 1920, 256, (2, 0, 1), -1),
    (1, 0, 2048, (1, 2), 1),
    (1, 2048, 2048, (1, 2), -1),
    (2, 0, 1152, (1, 2), 1),
    (2, 1152, 1024, (2, 1), -1),
    (3, 0, 2048, (2, 1), 1),
    (3, 2048, 2048, (2, 1), -1),
)
GRAD_COUNT = len(GRAD_STREAMS)
KEY_BLOCK = 512
norm_eps = 1e-05
rope_base = 100000000000.0
masked_value = -1e30
beta_one = 0.9
beta_two = 0.95
adam_eps = 1e-08
decay_rate = 0.1
rate_matrix = 0.05
rate_vector = 0.5


def ring_places():
    return tuple(lax.axis_index(a) for a in AXES)


def ring_step(places, axis, by):
    return {AXES[axis]: lax.rem(places[axis] + (by + SIDE), SIDE)}


def greet_neighbours(places):
    barrier = pltpu.get_barrier_semaphore()
    for axis in range(3):
        for by in (1, -1):
            pl.semaphore_signal(
                barrier,
                inc=1,
                device_id=ring_step(places, axis, by),
                device_id_type=pl.DeviceIdType.MESH,
            )
    pl.semaphore_wait(barrier, 6)


def remote(src, dst, send, recv, device):
    return pltpu.make_async_remote_copy(
        src_ref=src,
        dst_ref=dst,
        send_sem=send,
        recv_sem=recv,
        device_id=device,
        device_id_type=pl.DeviceIdType.MESH,
    )


def gather_kernel(shard, full, send, recv, own_sem):
    places = ring_places()
    greet_neighbours(places)
    own = pltpu.make_async_copy(shard, full.at[places[0], places[1], places[2]], own_sem)
    own.start()
    started = []

    def region(number, stage, place):
        _, first, width, order, _ = STREAMS[number]
        order = order[::-1]
        index = list(places)
        for axis in order[:stage]:
            index[axis] = slice(None)
        index[order[stage]] = place
        return full.at[(*index, slice(None), pl.ds(first, width))]

    def launch(number, stage, kind):
        _, first, width, order, way = STREAMS[number]
        axis = order[::-1][stage]
        here = places[axis]
        if kind == 2:
            source = target = region(number, stage, lax.rem(here + (SIDE - way), SIDE))
        else:
            source = target = region(number, stage, here)
            if stage == 0:
                source = shard.at[:, pl.ds(first, width)]
        copy = remote(
            source,
            target,
            send.at[number, stage, kind],
            recv.at[number, stage, kind],
            ring_step(places, axis, -way if kind == 1 else way),
        )
        copy.start()
        started.append(copy)
        return copy

    for stage in range(3):
        if stage == 1:
            own.wait()
        first, back = [], []
        for n in range(6):
            first.append(launch(n, stage, 0))
            back.append(launch(n, stage, 1))
        onward = []
        for n in range(6):
            first[n].wait_recv()
            onward.append(launch(n, stage, 2))
        for n in range(6):
            back[n].wait_recv()
            onward[n].wait_recv()
    for copy in started:
        copy.wait_send()


def gather_weights(part):
    out = pl.pallas_call(
        gather_kernel,
        out_shape=jax.ShapeDtypeStruct((4, 4, 4, *part.shape), part.dtype),
        in_specs=[pl.BlockSpec(memory_space=pl.ANY)],
        out_specs=pl.BlockSpec(memory_space=pl.ANY),
        scratch_shapes=[
            pltpu.SemaphoreType.DMA((6, 3, 3)),
            pltpu.SemaphoreType.DMA((6, 3, 3)),
            pltpu.SemaphoreType.DMA,
        ],
        compiler_params=pltpu.CompilerParams(collective_id=0, has_side_effects=True),
        cost_estimate=pl.CostEstimate(flops=0, bytes_accessed=80000000, transcendentals=0),
        name="gather_weights",
    )(part)
    return out.reshape(D, part.shape[-1])


def scatter_kernel(*refs):
    count = GRAD_COUNT
    grads, small = refs[:4], refs[4]
    refs = refs[5:]
    outs, small_out = refs[:count], refs[count]
    refs = refs[count + 1 :]
    ahead, mine = refs[:count], refs[count : 2 * count]
    refs = refs[2 * count :]
    arrived = (refs[:count], refs[count : 2 * count], refs[2 * count : 2 * count + 4])
    small_in, send, recv, own_sem, small_send, small_recv = refs[2 * count + 4 :]
    places = ring_places()
    greet_neighbours(places)
    started = []

    def near(axis, by):
        return lax.rem(places[axis] + (by + SIDE), SIDE)

    def block(number, stage, place):
        at, first, width, order, _ = GRAD_STREAMS[number]
        axis = order[stage]
        dims = sorted(order)
        if stage == 0:
            index = [slice(None)] * len(dims)
            index[dims.index(axis)] = place
            return grads[at].at[(*index, slice(None), pl.ds(first, width))]
        left = [a for a in dims if a != order[0]]
        index = [slice(None)] * len(left)
        for done in order[1:stage]:
            index[left.index(done)] = places[done]
        index[left.index(axis)] = place
        return mine[number].at[tuple(index)]

    def launch(number, stage, kind, source):
        axis, way = GRAD_STREAMS[number][3][stage], GRAD_STREAMS[number][4]
        copy = remote(
            source,
            arrived[stage][number].at[kind],
            send.at[number, stage, kind],
            recv.at[number, stage, kind],
            ring_step(places, axis, -way if kind == 2 else way),
        )
        copy.start()
        started.append(copy)
        return copy

    def add_into(target, source, lead):
        def one(total, part):
            total[...] = total[...] + part[...]

        if lead == 2:

            def body(k, carry):
                one(target.at[k // 4, k % 4], source.at[k // 4, k % 4])
                return carry

            lax.fori_loop(0, 16, body, 0)
        elif lead == 1:

            def body(k, carry):
                one(target.at[k], source.at[k])
                return carry

            lax.fori_loop(0, 4, body, 0)
        else:
            one(target, source)

    def small_exchange(step):
        axis, odd = step // 2, step % 2
        here = places[axis]
        partner = 3 - here if odd else here + 1 - 2 * lax.rem(here, 2)
        copy = remote(
            small_out,
            small_in.at[step],
            small_send.at[step],
            small_recv.at[step],
            {AXES[axis]: partner},
        )
        copy.start()
        return copy

    def small_finish(copy, step):
        copy.wait_send()
        copy.wait_recv()
        small_out[...] = small_out[...] + small_in[step]

    local = {}
    small_out[...] = small[...]
    for stage in range(3):
        active = [n for n in range(count) if len(GRAD_STREAMS[n][3]) > stage]
        first, back, onward = {}, {}, {}
        for n in active:
            axis, way = GRAD_STREAMS[n][3][stage], GRAD_STREAMS[n][4]
            first[n] = launch(n, stage, 0, block(n, stage, near(axis, 2)))
        for n in active:
            axis, way = GRAD_STREAMS[n][3][stage], GRAD_STREAMS[n][4]
            if stage == 0:
                pair = (
                    pltpu.make_async_copy(block(n, 0, near(axis, way)), ahead[n], own_sem.at[n, 0]),
                    pltpu.make_async_copy(block(n, 0, places[axis]), mine[n], own_sem.at[n, 1]),
                )
                for copy in pair:
                    copy.start()
                local[n] = pair
            back[n] = launch(n, stage, 2, block(n, stage, near(axis, -way)))
        step = small_exchange(2 * stage)
        for n in active:
            axis, way = GRAD_STREAMS[n][3][stage], GRAD_STREAMS[n][4]
            if stage == 0:
                local[n][0].wait()
                local[n][1].wait()
                target = ahead[n]
            else:
                target = block(n, stage, near(axis, way))
            first[n].wait_recv()
            add_into(target, arrived[stage][n].at[0], len(GRAD_STREAMS[n][3]) - 1 - stage)
            onward[n] = launch(n, stage, 1, target)
        small_finish(step, 2 * stage)
        step = small_exchange(2 * stage + 1)
        for n in active:
            order = GRAD_STREAMS[n][3]
            lead = len(order) - 1 - stage
            target = mine[n] if stage == 0 else block(n, stage, places[order[stage]])
            back[n].wait_recv()
            if lead:
                add_into(target, arrived[stage][n].at[2], lead)
            onward[n].wait_recv()
            if lead:
                add_into(target, arrived[stage][n].at[1], lead)
            else:
                outs[n][...] = target[...].astype(jnp.float32) + (
                    arrived[stage][n][1].astype(jnp.float32)
                    + arrived[stage][n][2].astype(jnp.float32)
                )
        small_finish(step, 2 * stage + 1)
    for copy in started:
        copy.wait_send()


def scatter_gradients(full, quarters, small):
    vmem = pl.BlockSpec(memory_space=pltpu.VMEM)

    def held(*lead_less):
        return [
            pltpu.VMEM((*lead, *(4,) * (len(s[3]) - less), ROWS, s[2]), jnp.bfloat16)
            for lead, less in lead_less
            for s in GRAD_STREAMS
            if len(s[3]) >= less
        ]

    scratch = held(((), 1), ((), 1), ((3,), 1), ((3,), 2), ((3,), 3))
    scratch += [
        pltpu.VMEM((6, *small.shape), jnp.float32),
        pltpu.SemaphoreType.DMA((GRAD_COUNT, 3, 3)),
        pltpu.SemaphoreType.DMA((GRAD_COUNT, 3, 3)),
        pltpu.SemaphoreType.DMA((GRAD_COUNT, 2)),
        pltpu.SemaphoreType.DMA((6,)),
        pltpu.SemaphoreType.DMA((6,)),
    ]
    shapes = [jax.ShapeDtypeStruct((ROWS, s[2]), jnp.float32) for s in GRAD_STREAMS]
    shapes.append(jax.ShapeDtypeStruct(small.shape, jnp.float32))
    views = [full.reshape(4, 4, 4, ROWS, full.shape[-1])]
    views += [q.reshape(4, 4, ROWS, q.shape[-1]) for q in quarters]
    return pl.pallas_call(
        scatter_kernel,
        out_shape=shapes,
        in_specs=[pl.BlockSpec(memory_space=pl.ANY)] * 4 + [vmem],
        out_specs=[vmem] * (GRAD_COUNT + 1),
        scratch_shapes=scratch,
        compiler_params=pltpu.CompilerParams(
            collective_id=1, has_side_effects=True, vmem_limit_bytes=28 * 2**20
        ),
        cost_estimate=pl.CostEstimate(flops=0, bytes_accessed=100000000, transcendentals=0),
        name="scatter_gradients",
    )(*views, small)


def other_core(value):
    return lax.ppermute(value, "tp", [(0, 1), (1, 0)])


def scan_kernel(
    reverse, parts, out, got, sums, rows, inside, decays, reply, back, send, recv
):
    here, outer = lax.axis_index("ctx_1"), lax.axis_index("ctx_0")
    head = parts.shape[2] - 16
    barrier = pltpu.get_barrier_semaphore()
    for axis, place in (("ctx_1", here), ("ctx_0", outer)):
        for by in range(1, SIDE):
            pl.semaphore_signal(
                barrier,
                inc=1,
                device_id={axis: lax.rem(place + by, SIDE)},
                device_id_type=pl.DeviceIdType.MESH,
            )
    pl.semaphore_wait(barrier, 6)
    started = []

    def spread(stage, axis, place, source, target):
        copies = []
        for by in (2, 1, 3):
            other = lax.rem(place + by, SIDE)
            copy = remote(
                source(other),
                target.at[place],
                send.at[stage, by - 1],
                recv.at[stage, by - 1],
                {axis: other},
            )
            copy.start()
            copies.append(copy)
        started.extend(copies)
        return copies

    def opened(ref, k):
        wide = ref[k].astype(jnp.float32)
        return wide[:, head : head + 1, :], wide[:, :head, :]

    order = range(SIDE - 1, -1, -1) if reverse else range(SIDE)
    copies = spread(0, "ctx_1", here, lambda other: parts.at[other], got)
    got[here] = parts[here]
    for copy in copies:
        copy.wait_recv()
    decay = state = None
    for k in order:
        own_decay, own_state = opened(got, k)
        if decay is None:
            decay, state = own_decay, own_state
        else:
            decays[k] = decay
            inside[k] = state
            decay, state = decay * own_decay, own_decay * state + own_state
    sums[:, :head, :] = state.astype(jnp.bfloat16)
    sums[:, head:, :] = jnp.broadcast_to(decay, (decay.shape[0], 16, decay.shape[2])).astype(
        jnp.bfloat16
    )
    copies = spread(1, "ctx_0", outer, lambda other: sums, rows)
    rows[outer] = sums[...]
    for copy in copies:
        copy.wait_recv()
    before = jnp.zeros_like(state)
    state = None
    for k in order:
        if state is not None:
            before = jnp.where(outer == k, state, before)
        own_decay, own_state = opened(rows, k)
        state = own_state if state is None else own_decay * state + own_state
    for k in order:
        if k == order[0]:
            reply[k] = before.astype(jnp.bfloat16)
        else:
            reply[k] = (decays[k] * before + inside[k]).astype(jnp.bfloat16)
    copies = spread(2, "ctx_1", here, lambda other: reply.at[other], back)
    back[here] = reply[here]
    for copy in copies:
        copy.wait_recv()
    out[...] = back[...].astype(jnp.float32)
    for copy in started:
        copy.wait_send()


def entering(decay, state, reverse):
    heads = decay.shape[0]
    chunk = heads // SIDE
    size, width = state.shape[1:]
    rows = jnp.broadcast_to(decay[:, None, None], (heads, 16, width))
    message = jnp.concatenate([state, rows], axis=1).astype(jnp.bfloat16)
    message = message.reshape(SIDE, chunk, size + 16, width)
    vmem = pl.BlockSpec(memory_space=pltpu.VMEM)
    out = pl.pallas_call(
        functools.partial(scan_kernel, reverse),
        out_shape=jax.ShapeDtypeStruct((SIDE, chunk, size, width), jnp.float32),
        in_specs=[vmem],
        out_specs=vmem,
        scratch_shapes=[
            pltpu.VMEM((SIDE, chunk, size + 16, width), jnp.bfloat16),
            pltpu.VMEM((chunk, size + 16, width), jnp.bfloat16),
            pltpu.VMEM((SIDE, chunk, size + 16, width), jnp.bfloat16),
            pltpu.VMEM((SIDE, chunk, size, width), jnp.float32),
            pltpu.VMEM((SIDE, chunk, 1, width), jnp.float32),
            pltpu.VMEM((SIDE, chunk, size, width), jnp.bfloat16),
            pltpu.VMEM((SIDE, chunk, size, width), jnp.bfloat16),
            pltpu.SemaphoreType.DMA((3, 3)),
            pltpu.SemaphoreType.DMA((3, 3)),
        ],
        compiler_params=pltpu.CompilerParams(
            collective_id=3 if reverse else 2, has_side_effects=True
        ),
        cost_estimate=pl.CostEstimate(flops=0, bytes_accessed=40000000, transcendentals=0),
        name="scan_back" if reverse else "scan_forth",
    )(message)
    return out.reshape(heads, size, width)


def attend_back_kernel(
    kv, keys_t, queries, queries_t, d_att, d_att_t, log_total, delta, lowest, highest_key, d_kv, d_query_t
):
    step = pl.program_id(0)

    @pl.when(step == 0)
    def _():
        d_query_t[...] = jnp.zeros_like(d_query_t)

    at = step * KEY_BLOCK + lax.broadcasted_iota(jnp.int32, (KEY_BLOCK, lowest.shape[1]), 0)
    allowed = (at >= lowest[...]) & (at <= highest_key[...])
    keys, values = kv[:, :HD], kv[:, HD:]
    scale = HD ** (-0.5)
    d_key = jnp.zeros((KEY_BLOCK, HD), jnp.float32)
    d_value = jnp.zeros((KEY_BLOCK, HD), jnp.float32)
    for g in range(queries.shape[0]):
        raw = jnp.dot(keys, queries_t[g], preferred_element_type=jnp.float32)
        logits = jnp.where(allowed, raw * scale, masked_value)
        prob = jnp.exp(logits - log_total[g : g + 1, :])
        d_prob = jnp.dot(values, d_att_t[g], preferred_element_type=jnp.float32)
        d_raw = (prob * (d_prob - delta[g : g + 1, :]) * scale).astype(jnp.bfloat16)
        d_value += jnp.dot(
            prob.astype(jnp.bfloat16), d_att[g], preferred_element_type=jnp.float32
        )
        d_key += jnp.dot(d_raw, queries[g], preferred_element_type=jnp.float32)
        d_query_t[g] += jnp.dot(keys_t[...], d_raw, preferred_element_type=jnp.float32)
    d_kv[...] = jnp.concatenate([d_key, d_value], axis=1).astype(jnp.bfloat16)


def attend_back(key_values, queries_b, d_att_b, log_total, delta, lowest, highest_key):
    count, width = queries_b.shape
    groups = width // HD
    total = key_values.shape[0]
    by_head = queries_b.reshape(count, groups, HD)
    d_by_head = d_att_b.reshape(count, groups, HD)

    def whole(*shape):
        return pl.BlockSpec(shape, lambda s: (0,) * len(shape))

    d_pair, d_query_t = pl.pallas_call(
        attend_back_kernel,
        grid=(total // KEY_BLOCK,),
        out_shape=[
            jax.ShapeDtypeStruct((total, 2 * HD), jnp.bfloat16),
            jax.ShapeDtypeStruct((groups, HD, count), jnp.float32),
        ],
        in_specs=[
            pl.BlockSpec((KEY_BLOCK, 2 * HD), lambda s: (s, 0)),
            pl.BlockSpec((HD, KEY_BLOCK), lambda s: (0, s)),
            whole(groups, count, HD),
            whole(groups, HD, count),
            whole(groups, count, HD),
            whole(groups, HD, count),
            whole(groups, count),
            whole(groups, count),
            whole(1, count),
            whole(1, count),
        ],
        out_specs=[pl.BlockSpec((KEY_BLOCK, 2 * HD), lambda s: (s, 0)), whole(groups, HD, count)],
        compiler_params=pltpu.CompilerParams(vmem_limit_bytes=24 * 2**20),
        cost_estimate=pl.CostEstimate(
            flops=10 * groups * HD * count * total,
            bytes_accessed=8 * total * HD,
            transcendentals=groups * count * total,
        ),
        name="attend_back",
    )(
        key_values,
        key_values[:, :HD].T,
        by_head.transpose(1, 0, 2),
        by_head.transpose(1, 2, 0),
        d_by_head.transpose(1, 0, 2),
        d_by_head.transpose(1, 2, 0),
        log_total,
        delta,
        lowest,
        highest_key,
    )
    return d_pair, d_query_t.transpose(2, 0, 1).reshape(count, width)


def from_everyone(value, axis):
    copies = jnp.broadcast_to(value, (lax.axis_size(axis), *value.shape))
    return lax.all_to_all(copies, axis, split_axis=0, concat_axis=0, tiled=True)


def joined_along(pieces, dim):
    shape = list(pieces.shape[1:])
    shape[dim] *= pieces.shape[0]
    return jnp.moveaxis(pieces, 0, dim).reshape(shape)


def gathered_copies(value, axis, dim):
    pieces = from_everyone(value, axis)
    return joined_along(pieces, dim)


def passed_along(value, axis, by):
    count = lax.axis_size(axis)
    pairs = [(i, i + by) for i in range(count) if 0 <= i + by < count]
    return lax.ppermute(value, axis, pairs)


def split_up(value, dim, count):
    before, after = (value.shape[:dim], value.shape[dim + 1 :])
    return jnp.moveaxis(value.reshape(*before, count, -1, *after), dim, 0)


def summed_on_arrival(value, axis, dim):
    pieces = split_up(value, dim, lax.axis_size(axis))
    arrived = lax.all_to_all(pieces, axis, split_axis=0, concat_axis=0, tiled=True)
    return arrived.astype(jnp.float32).sum(axis=0)


def rms_norm(value, gain):
    return value * lax.rsqrt(jnp.mean(value * value, axis=-1, keepdims=True) + norm_eps) * gain


def silu_slope(value):
    sigma = jax.nn.sigmoid(value)
    return sigma * (1.0 + value * (1.0 - sigma))


def doc_layout(doc_row, start_row, item_count):
    ends = jnp.cumsum(doc_row)
    starts = ends - doc_row
    token_index = start_row + jnp.arange(item_count, dtype=jnp.int32)
    segment = jnp.sum((token_index[:, None] >= ends[None, :]).astype(jnp.int32), axis=1)
    picked = segment[:, None] == jnp.arange(doc_row.shape[0], dtype=jnp.int32)[None, :]
    begin = jnp.sum(jnp.where(picked, starts[None, :], 0), axis=1)
    return (segment, token_index - begin)


def rope_tables(position):
    freq = rope_base ** (-2.0 * jnp.arange(HD // 2, dtype=jnp.float32) / HD)
    angle = position.astype(jnp.float32)[:, None] * freq[None, :]
    return (jnp.cos(angle), jnp.sin(angle))


def rotate(value, cosine, sine):
    shaped = value.reshape(value.shape[0], -1, 2, HD // 2)
    first_half = shaped[:, :, 0]
    second_half = shaped[:, :, 1]
    cos_part = cosine[:, None, :]
    sin_part = sine[:, None, :]
    turned = jnp.stack(
        [
            first_half * cos_part - second_half * sin_part,
            second_half * cos_part + first_half * sin_part,
        ],
        axis=2,
    )
    return turned.reshape(value.shape)


def conv_act(extended, conv_taps, conv_bias, seg_ext):
    item_count = extended.shape[0] - (CONV - 1)
    own_seg = seg_ext[CONV - 1 :]
    total = conv_bias[None, :] + conv_taps[CONV - 1][None, :] * extended[CONV - 1 :]
    for back in range(1, CONV):
        begin = CONV - 1 - back
        same = seg_ext[begin : begin + item_count] == own_seg
        total = total + conv_taps[CONV - 1 - back][None, :] * jnp.where(
            same[:, None], extended[begin : begin + item_count], 0.0
        )
    return jax.nn.silu(total)


def decay_terms(drive_input, dt_bias, a_log):
    dt_step = jax.nn.softplus(drive_input + dt_bias)
    order = jnp.arange(dt_step.shape[0], dtype=jnp.int32)
    upto = (order[None, :] <= order[:, None]).astype(jnp.float32)
    return (dt_step, jnp.dot(upto, -dt_step * jnp.exp(a_log), precision=highest))


def head_columns(heads):
    column = jnp.arange(heads * MAMBA_HEAD_SIZE, dtype=jnp.int32) // MAMBA_HEAD_SIZE
    return (column[None, :] == jnp.arange(heads, dtype=jnp.int32)[:, None]).astype(jnp.float32)


def spread_heads(value, columns):
    return jnp.dot(value, columns, precision=highest, preferred_element_type=jnp.float32)


def fold_heads(value, columns):
    return lax.dot_general(
        value,
        columns,
        (((1,), (1,)), ((), ())),
        precision=highest,
        preferred_element_type=jnp.float32,
    )


def cross(left, right):
    return lax.dot_general(
        left, right, (((1,), (1,)), ((), ())), preferred_element_type=jnp.float32
    )


def same_document(seg_col, seg_row, flipped):
    count = seg_col.shape[0]
    down = lax.broadcasted_iota(jnp.int32, (count, count), 0)
    over = lax.broadcasted_iota(jnp.int32, (count, count), 1)
    earlier = (down <= over) if flipped else (over <= down)
    return earlier & (seg_col == seg_row)


def state_forth_kernel(
    x, both, log_col, log_row, dt_step, entry, skip, seg_col, seg_row, state, columns, out
):
    b_mat, c_mat = both[:, :MAMBA_STATE_SIZE], both[:, MAMBA_STATE_SIZE:]
    seen = same_document(seg_col[...], seg_row[...], False)
    inner_prod = cross(c_mat, b_mat)
    spreader = columns[...]
    driven = (x[...] * spread_heads(dt_step[...], spreader)).astype(jnp.bfloat16)
    carried = cross(c_mat, state[...].astype(jnp.bfloat16))
    base = carried * spread_heads(entry[...], spreader) + skip[...] * x[...]
    for pair in range(log_row.shape[0] // 2):
        halves = []
        for h in (2 * pair, 2 * pair + 1):
            fade = log_col[:, h : h + 1] - log_row[h : h + 1, :]
            mixing = jnp.exp(jnp.where(seen, fade, masked_value)) * inner_prod
            at = h * MAMBA_HEAD_SIZE
            halves.append(
                jnp.dot(
                    mixing.astype(jnp.bfloat16),
                    driven[:, at : at + MAMBA_HEAD_SIZE],
                    preferred_element_type=jnp.float32,
                )
            )
        at = 2 * pair * MAMBA_HEAD_SIZE
        till = at + 2 * MAMBA_HEAD_SIZE
        out[:, at:till] = base[:, at:till] + jnp.concatenate(halves, axis=1)


def state_back_kernel(
    x,
    y,
    d_y,
    both,
    log_col,
    log_row,
    dt_step,
    fading,
    entry,
    skip,
    seg_col,
    seg_row,
    state,
    later,
    columns,
    d_x,
    d_both,
    by_dt,
    by_log,
    by_skip,
):
    b_mat, c_mat = both[:, :MAMBA_STATE_SIZE], both[:, MAMBA_STATE_SIZE:]
    seen = same_document(seg_col[...], seg_row[...], True)
    inner_prod = cross(b_mat, c_mat)
    spreader = columns[...]
    x_all, d_all = x[...], d_y[...]
    x_b, d_b = x_all.astype(jnp.bfloat16), d_all.astype(jnp.bfloat16)
    later_b, state_b = later[...].astype(jnp.bfloat16), state[...].astype(jnp.bfloat16)
    d_inner_prod = jnp.zeros_like(inner_prod)
    parts = []
    for h in range(log_row.shape[0]):
        at = h * MAMBA_HEAD_SIZE
        fade = log_row[h : h + 1, :] - log_col[:, h : h + 1]
        kernel = jnp.exp(jnp.where(seen, fade, masked_value))
        d_mixing = cross(x_b[:, at : at + MAMBA_HEAD_SIZE], d_b[:, at : at + MAMBA_HEAD_SIZE])
        d_inner_prod += kernel * d_mixing * dt_step[:, h : h + 1]
        parts.append(
            jnp.dot(
                (kernel * inner_prod).astype(jnp.bfloat16),
                d_b[:, at : at + MAMBA_HEAD_SIZE],
                preferred_element_type=jnp.float32,
            )
        )
    fade_all = spread_heads(fading[...], spreader)
    dt_all = spread_heads(dt_step[...], spreader)
    pulled = jnp.concatenate(parts, axis=1) + fade_all * cross(b_mat, later_b)
    d_x[...] = dt_all * pulled + skip[...] * d_all
    by_dt[...] = fold_heads(x_all * pulled, spreader)
    by_log[...] = fold_heads(d_all * (y[...] - skip[...] * x_all), spreader)
    by_skip[...] = fold_heads(d_all * x_all, spreader)
    d_inner_b = d_inner_prod.astype(jnp.bfloat16)
    d_b_mat = jnp.dot(d_inner_b, c_mat, preferred_element_type=jnp.float32) + jnp.dot(
        (x_all * fade_all * dt_all).astype(jnp.bfloat16),
        later_b,
        preferred_element_type=jnp.float32,
    )
    d_c_mat = lax.dot_general(
        d_inner_b, b_mat, (((0,), (0,)), ((), ())), preferred_element_type=jnp.float32
    ) + jnp.dot(
        (d_all * spread_heads(entry[...], spreader)).astype(jnp.bfloat16),
        state_b,
        preferred_element_type=jnp.float32,
    )
    d_both[...] = jnp.concatenate([d_b_mat, d_c_mat], axis=1)


def state_call(kernel, shapes, name, *arrays):
    vmem = pl.BlockSpec(memory_space=pltpu.VMEM)
    return pl.pallas_call(
        kernel,
        out_shape=shapes,
        in_specs=[vmem] * len(arrays),
        out_specs=jax.tree.map(lambda s: vmem, shapes),
        compiler_params=pltpu.CompilerParams(vmem_limit_bytes=32 * 2**20),
        cost_estimate=pl.CostEstimate(
            flops=2000000000, bytes_accessed=8000000, transcendentals=800000
        ),
        name=name,
    )(*arrays)


def decay_parts(drive_input, dt_bias, a_log, segment, position):
    dt_step, log_cum = decay_terms(drive_input, dt_bias, a_log)
    count = log_cum.shape[0]
    last = log_cum[count - 1]
    in_last = (segment == segment[count - 1]).astype(jnp.float32)
    fading = jnp.exp(last[None, :] - log_cum) * in_last[:, None]
    carry_on = ((segment == segment[0]) & (position[0] != 0)).astype(jnp.float32)
    entry = jnp.exp(log_cum) * carry_on[:, None]
    return dt_step, log_cum, fading, entry, carry_on[count - 1] * jnp.exp(last)


def split_vector(vector, widths):
    q_width, k_width, s_width, b_width, h_width = widths
    channels = s_width + b_width
    conv_taps = vector[: CONV * channels].reshape(CONV, channels)
    offset = CONV * channels
    conv_bias = vector[offset : offset + channels]
    offset = offset + channels
    gated_gain = vector[offset : offset + s_width]
    offset = offset + s_width
    return (
        conv_taps,
        conv_bias,
        gated_gain,
        vector[offset : offset + h_width],
        vector[offset + h_width : offset + 2 * h_width],
        vector[offset + 2 * h_width : offset + 3 * h_width],
    )


def feature_sum(value):
    own = value.astype(jnp.bfloat16)
    return own.astype(jnp.float32) + other_core(own).astype(jnp.float32)


def norm_sum(value):
    return value + other_core(value)


def local_matrices(w_in, w_out, w_gu, w_down, layer_at):
    return (
        jnp.pad(w_in[layer_at, :, 0, :], ((0, 0), (0, IN_PAD - IN_COLS))).astype(jnp.bfloat16),
        w_gu[layer_at, :, 0, :].astype(jnp.bfloat16),
        w_out[layer_at, 0].T.astype(jnp.bfloat16),
        w_down[layer_at, 0].T.astype(jnp.bfloat16),
    )


def fetch_layers(w_in, w_out, w_gu, w_down):
    parts = [local_matrices(w_in, w_out, w_gu, w_down, k) for k in range(LAYERS)]
    rest = (*parts[0][1:], *parts[1])
    filled = lax.all_gather(jnp.concatenate(rest, axis=1), FSDP_CTX, axis=0, tiled=True)
    bounds, at = [], 0
    for part in rest[:-1]:
        at += part.shape[1]
        bounds.append(at)
    pieces = jnp.split(filled, bounds, axis=1)
    return (gather_weights(parts[0][0]), *pieces[:3]), tuple(pieces[3:])


def attention_logits(queries_b, key_values, allowed):
    grouped_heads = queries_b.reshape(queries_b.shape[0], -1, HD)
    raw = jnp.einsum(
        "tgd,sd->gts", grouped_heads, key_values[:, :HD], preferred_element_type=jnp.float32
    )
    return jnp.where(allowed[None], raw * HD ** (-0.5), masked_value)


def layer_forward(state, weights, vector, gains, context, widths):
    w_in_b, w_gu_b, w_out_t, w_down_t = weights
    segment, position, seg_ext, allowed, cosine, sine, lowest, highest_key = context
    q_width, k_width, s_width, b_width, h_width = widths
    conv_taps, conv_bias, gated_gain, a_log, dt_bias, d_skip = split_vector(vector, widths)
    item_count = state.shape[0]
    at_v = q_width + k_width
    at_z = at_v + k_width
    at_x = at_z + s_width
    at_t = at_x + s_width + b_width
    hidden_b = rms_norm(state, gains[0]).astype(jnp.bfloat16)
    proj = jnp.dot(hidden_b, w_in_b, preferred_element_type=jnp.float32)
    queries_b = rotate(proj[:, :q_width], cosine, sine).astype(jnp.bfloat16)
    pair = jnp.concatenate(
        [rotate(proj[:, q_width:at_v], cosine, sine), proj[:, at_v:at_z]], axis=1
    ).astype(jnp.bfloat16)
    key_values = gathered_copies(pair, CTX, 0)
    logits = attention_logits(queries_b, key_values, allowed)
    top = jnp.max(logits, axis=2, keepdims=True)
    log_total = top + jnp.log(jnp.sum(jnp.exp(logits - top), axis=2, keepdims=True))
    prob_b = jnp.exp(logits - log_total).astype(jnp.bfloat16)
    attended = jnp.einsum(
        "gts,sd->tgd", prob_b, key_values[:, HD:], preferred_element_type=jnp.float32
    ).reshape(item_count, q_width)
    mixed_in = proj[:, at_x:at_t]
    halo_rows = passed_along(mixed_in[item_count - (CONV - 1) :], CTX, 1)
    extended = jnp.concatenate([halo_rows, mixed_in], axis=0)
    active = conv_act(extended, conv_taps, conv_bias, seg_ext)
    own_part = active[:, s_width:].astype(jnp.bfloat16)
    other_part = other_core(own_part)
    leads = lax.axis_index("tp") == 0
    both = jnp.concatenate(
        [jnp.where(leads, own_part, other_part), jnp.where(leads, other_part, own_part)], axis=1
    )
    inner_input = active[:, :s_width]
    drive_input = proj[:, at_t : at_t + h_width]
    columns = head_columns(h_width)
    timing = decay_parts(drive_input, dt_bias, a_log, segment, position)
    dt_step, log_cum, fading, entry, decay_own = timing
    weighted = inner_input * spread_heads(fading * dt_step, columns)
    state_own = jnp.einsum("sc,sn->cn", weighted, both[:, :MAMBA_STATE_SIZE].astype(jnp.float32))
    state_own = state_own.reshape(h_width, MAMBA_HEAD_SIZE, MAMBA_STATE_SIZE)
    state_in = entering(decay_own, state_own, False)
    ssm = state_call(
        state_forth_kernel,
        jax.ShapeDtypeStruct(inner_input.shape, jnp.float32),
        "state_forth",
        inner_input,
        both,
        log_cum,
        log_cum.T,
        dt_step,
        entry,
        spread_heads(d_skip[None, :], columns),
        segment[:, None],
        segment[None, :],
        state_in.reshape(s_width, MAMBA_STATE_SIZE),
        columns,
    )
    gated = ssm * jax.nn.silu(proj[:, at_z:at_x])
    inverse = lax.rsqrt(norm_sum(jnp.sum(gated * gated, axis=1)) / DSSM + norm_eps)[:, None]
    features = jnp.concatenate([attended, gated * inverse * gated_gain], axis=1).astype(
        jnp.bfloat16
    )
    middle = state + feature_sum(
        jnp.einsum("tc,dc->td", features, w_out_t, preferred_element_type=jnp.float32)
    )
    hidden2_b = rms_norm(middle, gains[1]).astype(jnp.bfloat16)
    upgate = jnp.dot(hidden2_b, w_gu_b, preferred_element_type=jnp.float32)
    half_width = upgate.shape[1] // 2
    inner_b = (jax.nn.silu(upgate[:, :half_width]) * upgate[:, half_width:]).astype(jnp.bfloat16)
    final_result = middle + feature_sum(
        jnp.einsum("tf,df->td", inner_b, w_down_t, preferred_element_type=jnp.float32)
    )
    kept = (
        state,
        hidden_b,
        proj,
        queries_b,
        key_values,
        log_total,
        extended,
        active,
        both,
        state_in,
        state_own,
        timing,
        ssm,
        gated,
        inverse,
        features,
        middle,
        hidden2_b,
        upgate,
        inner_b,
        attended,
    )
    return (final_result, kept)


def layer_backward(grad_out, kept, weights, vector, gains, context, widths, waiting):
    w_in_b, w_gu_b, w_out_t, w_down_t = weights
    segment, position, seg_ext, allowed, cosine, sine, lowest, highest_key = context
    q_width, k_width, s_width, b_width, h_width = widths
    conv_taps, conv_bias, gated_gain, a_log, dt_bias, d_skip = split_vector(vector, widths)
    (
        state,
        hidden_b,
        proj,
        queries_b,
        key_values,
        log_total,
        extended,
        active,
        both,
        state_in,
        state_own,
        timing,
        ssm,
        gated,
        inverse,
        features,
        middle,
        hidden2_b,
        upgate,
        inner_b,
        attended,
    ) = kept
    item_count = state.shape[0]
    at_v = q_width + k_width
    at_z = at_v + k_width
    at_x = at_z + s_width
    at_t = at_x + s_width + b_width
    grad_b = grad_out.astype(jnp.bfloat16)
    grad_down = jnp.einsum(
        "td,tf->df", grad_b, inner_b, preferred_element_type=jnp.float32
    ).astype(jnp.bfloat16)
    d_inner = jnp.dot(grad_b, w_down_t, preferred_element_type=jnp.float32)
    half_width = upgate.shape[1] // 2
    gate_part = upgate[:, :half_width]
    d_upgate_b = jnp.concatenate(
        [
            d_inner * upgate[:, half_width:] * silu_slope(gate_part),
            d_inner * jax.nn.silu(gate_part),
        ],
        axis=1,
    ).astype(jnp.bfloat16)
    grad_gu = jnp.einsum(
        "td,tf->df", hidden2_b, d_upgate_b, preferred_element_type=jnp.float32
    ).astype(jnp.bfloat16)
    d_hidden2 = feature_sum(
        jnp.einsum("tf,df->td", d_upgate_b, w_gu_b, preferred_element_type=jnp.float32)
    )
    d_middle_norm, d_gain_mlp = jax.vjp(rms_norm, middle, gains[1])[1](d_hidden2)
    d_middle = grad_out + d_middle_norm
    mix_b = d_middle.astype(jnp.bfloat16)
    grad_out_proj = jnp.einsum(
        "td,tc->dc", mix_b, features, preferred_element_type=jnp.float32
    ).astype(jnp.bfloat16)
    early = lax.psum_scatter(
        jnp.concatenate([grad_gu, grad_down, grad_out_proj], axis=1), "fsdp", tiled=True
    )
    d_features = jnp.dot(mix_b, w_out_t, preferred_element_type=jnp.float32)
    d_normed = d_features[:, q_width:]
    weighted = d_normed * gated_gain
    d_gated_gain = jnp.sum(d_normed * gated * inverse, axis=0)
    across = norm_sum(jnp.sum(weighted * gated, axis=1))[:, None]
    d_gated = weighted * inverse - gated * inverse**3 * across / DSSM
    gate_z = proj[:, at_z:at_x]
    d_ssm = d_gated * jax.nn.silu(gate_z)
    d_gate_z = d_gated * ssm * silu_slope(gate_z)
    inner_input = active[:, :s_width]
    drive_input = proj[:, at_t : at_t + h_width]

    dt_step, log_cum, fading, entry, decay_own = timing
    columns = head_columns(h_width)
    d_carry = jnp.einsum(
        "tc,tn->cn",
        d_ssm * spread_heads(entry, columns),
        both[:, MAMBA_STATE_SIZE:].astype(jnp.float32),
    ).reshape(state_in.shape)
    later = entering(decay_own, d_carry, True)
    by_head = jax.ShapeDtypeStruct(dt_step.shape, jnp.float32)
    d_inner_input, d_both, by_dt, by_log, by_skip = state_call(
        state_back_kernel,
        [
            jax.ShapeDtypeStruct(inner_input.shape, jnp.float32),
            jax.ShapeDtypeStruct(both.shape, jnp.float32),
            by_head,
            by_head,
            by_head,
        ],
        "state_back",
        inner_input,
        ssm,
        d_ssm,
        both,
        log_cum,
        log_cum.T,
        dt_step,
        fading,
        entry,
        spread_heads(d_skip[None, :], columns),
        segment[:, None],
        segment[None, :],
        state_in.reshape(s_width, MAMBA_STATE_SIZE),
        later.reshape(s_width, MAMBA_STATE_SIZE),
        columns,
    )
    at_end = jnp.sum(later * (state_own + decay_own[:, None, None] * state_in), axis=(1, 2))
    order = jnp.arange(item_count, dtype=jnp.int32)
    d_log_cum = by_log - dt_step * by_dt
    onward = (order[None, :] >= order[:, None]).astype(jnp.float32)
    d_log_decay = jnp.dot(onward, d_log_cum, precision=highest) + at_end[None, :]
    d_dt = by_dt - jnp.exp(a_log) * d_log_decay
    d_drive = d_dt * jax.nn.sigmoid(drive_input + dt_bias)
    d_a_log = -jnp.sum(d_log_decay * dt_step, axis=0) * jnp.exp(a_log)
    d_dt_bias = jnp.sum(d_drive, axis=0)
    d_skip_grad = jnp.sum(by_skip, axis=0)
    d_both_b = d_both.astype(jnp.bfloat16)
    leads = lax.axis_index("tp") == 0
    kept_part = jnp.where(leads, d_both_b[:, :b_width], d_both_b[:, b_width:])
    sent_part = jnp.where(leads, d_both_b[:, b_width:], d_both_b[:, :b_width])
    d_own = kept_part.astype(jnp.float32) + other_core(sent_part).astype(jnp.float32)

    def conv_part(ext_part, taps_part, bias_part):
        return conv_act(ext_part, taps_part, bias_part, seg_ext)

    conv_pull = jax.vjp(conv_part, extended, conv_taps, conv_bias)[1]
    d_extended, d_taps, d_bias = conv_pull(jnp.concatenate([d_inner_input, d_own], axis=1))
    spill = passed_along(d_extended[: CONV - 1], CTX, -1)
    d_mixed = jnp.concatenate(
        [d_extended[CONV - 1 : item_count], d_extended[item_count:] + spill], axis=0
    )
    d_att_b = d_features[:, :q_width].astype(jnp.bfloat16)
    delta = jnp.sum(
        (d_att_b.astype(jnp.float32) * attended).reshape(item_count, -1, HD), axis=2
    ).T
    d_pair_all, d_query = attend_back(
        key_values, queries_b, d_att_b, log_total[:, :, 0], delta, lowest, highest_key
    )
    if waiting is not None:
        d_pair_all, waiting = lax.optimization_barrier((d_pair_all, waiting))
    d_pair = summed_on_arrival(d_pair_all, CTX, 0)
    d_proj_b = jnp.concatenate(
        [
            rotate(d_query, cosine, -sine),
            rotate(d_pair[:, :HD], cosine, -sine),
            d_pair[:, HD:],
            d_gate_z,
            d_mixed,
            d_drive,
            jnp.zeros((item_count, IN_PAD - IN_COLS), jnp.float32),
        ],
        axis=1,
    ).astype(jnp.bfloat16)
    grad_in = jnp.einsum(
        "td,tc->dc", hidden_b, d_proj_b, preferred_element_type=jnp.float32
    ).astype(jnp.bfloat16)
    d_hidden = feature_sum(
        jnp.einsum("tc,dc->td", d_proj_b, w_in_b, preferred_element_type=jnp.float32)
    )
    d_state_norm, d_gain_mix = jax.vjp(rms_norm, state, gains[0])[1](d_hidden)
    d_vector = jnp.concatenate(
        [
            d_taps.reshape(-1),
            d_bias,
            d_gated_gain,
            d_a_log,
            d_dt_bias,
            d_skip_grad,
        ]
    )
    return (
        d_middle + d_state_norm,
        grad_in,
        early,
        waiting,
        d_vector,
        jnp.stack([d_gain_mix, d_gain_mlp]),
    )


def adamw(weight, first_m, second_m, grad, rate, decay):
    first_new = beta_one * first_m + (1.0 - beta_one) * grad
    second_new = beta_two * second_m + (1.0 - beta_two) * grad * grad
    ratio = (
        first_new
        / (1.0 - beta_one**STEP)
        / (jnp.sqrt(second_new / (1.0 - beta_two**STEP)) + adam_eps)
    )
    return (first_new, second_new, weight - rate * (ratio + decay * weight))


def per_device(
    block_input,
    cotangent,
    lengths,
    w_in,
    w_out,
    w_gu,
    w_down,
    vectors,
    norm_gains,
    first_in,
    first_out,
    first_gu,
    first_down,
    first_vectors,
    first_gains,
    second_in,
    second_out,
    second_gu,
    second_down,
    second_vectors,
    second_gains,
):
    group_count = lax.axis_size("tp")
    widths = (
        HEADS * HD // group_count,
        KV_HEADS * HD // group_count,
        MAMBA_HEADS * MAMBA_HEAD_SIZE // group_count,
        2 * MAMBA_STATE_SIZE // group_count,
        MAMBA_HEADS // group_count,
    )
    item_count = block_input.shape[0]
    start_row = lax.axis_index(CTX) * item_count
    seq_total = item_count * lax.axis_size(CTX)
    doc_row = lengths[0]
    segment, position = doc_layout(doc_row, start_row, item_count)
    seg_ext = doc_layout(doc_row, start_row - (CONV - 1), item_count + CONV - 1)[0]
    key_seg = doc_layout(doc_row, 0, seq_total)[0]
    query_index = start_row + jnp.arange(item_count, dtype=jnp.int32)
    allowed = (jnp.arange(seq_total, dtype=jnp.int32)[None, :] <= query_index[:, None]) & (
        key_seg[None, :] == segment[:, None]
    )
    cosine, sine = rope_tables(position)
    lowest, highest_key = (query_index - position)[None, :], query_index[None, :]
    context = (segment, position, seg_ext, allowed, cosine, sine, lowest, highest_key)
    stored = []
    state = block_input
    fetched = fetch_layers(w_in, w_out, w_gu, w_down)
    for layer_at in range(LAYERS):
        weights = fetched[layer_at]
        state, kept = layer_forward(
            state, weights, vectors[layer_at, 0], norm_gains[layer_at], context, widths
        )
        stored.append(kept)
    grad_state = cotangent
    early_parts = [None] * LAYERS
    waiting = None
    small_parts = [None] * LAYERS
    vec = vectors.shape[-1]
    for layer_at in reversed(range(LAYERS)):
        grad_state, late, early, waiting, d_vector, d_gains = layer_backward(
            grad_state,
            stored[layer_at],
            fetched[layer_at],
            vectors[layer_at, 0],
            norm_gains[layer_at],
            context,
            widths,
            waiting,
        )
        if layer_at:
            grad_state, early = lax.optimization_barrier((grad_state, early))
            waiting = lax.psum_scatter(late, "fsdp", tiled=True)
        else:
            late_parts = (late, waiting)
        early_parts[layer_at] = early
        small_parts[layer_at] = jnp.concatenate([d_vector, d_gains.reshape(-1)])
    small = jnp.concatenate(small_parts)
    span = -(-small.shape[0] // 1024) * 8
    small = jnp.pad(small, (0, span * 128 - small.shape[0])).reshape(span, 128)
    *pieces, small = scatter_gradients(
        late_parts[0], (early_parts[1], late_parts[1], early_parts[0]), small
    )
    shards = [
        (
            jnp.concatenate(some, axis=1)[:, :IN_COLS],
            wide,
            rest[:, D:].T,
            rest[:, :D].T,
        )
        for some, wide, rest in (
            (pieces[:4], pieces[8], pieces[9]),
            (pieces[6:8], pieces[4], pieces[5]),
        )
    ]
    small_grads = small.reshape(-1)[: LAYERS * (vec + 2 * D)].reshape(LAYERS, vec + 2 * D)
    grad_in_all = jnp.stack([p[0] for p in shards]).reshape(w_in.shape)
    grad_gu_all = jnp.stack([p[1] for p in shards]).reshape(w_gu.shape)
    grad_out_all = jnp.stack([p[2] for p in shards]).reshape(w_out.shape)
    grad_down_all = jnp.stack([p[3] for p in shards]).reshape(w_down.shape)
    vector_total = small_grads[:, :vec].reshape(vectors.shape)
    gain_total = small_grads[:, vec:].reshape(norm_gains.shape)
    up_in = adamw(w_in, first_in, second_in, grad_in_all, rate_matrix, decay_rate)
    up_out = adamw(w_out, first_out, second_out, grad_out_all, rate_matrix, decay_rate)
    up_gu = adamw(w_gu, first_gu, second_gu, grad_gu_all, rate_matrix, decay_rate)
    up_down = adamw(w_down, first_down, second_down, grad_down_all, rate_matrix, decay_rate)
    up_vec = adamw(vectors, first_vectors, second_vectors, vector_total, rate_vector, 0.0)
    up_gain = adamw(norm_gains, first_gains, second_gains, gain_total, rate_vector, 0.0)
    return (
        state,
        grad_state,
        up_in[0],
        up_in[1],
        up_in[2],
        up_out[0],
        up_out[1],
        up_out[2],
        up_gu[0],
        up_gu[1],
        up_gu[2],
        up_down[0],
        up_down[1],
        up_down[2],
        up_vec[0],
        up_vec[1],
        up_vec[2],
        up_gain[0],
        up_gain[1],
        up_gain[2],
    )


def solution(mesh):
    torus = Mesh(
        mesh.devices.reshape(mesh.shape["fsdp"], 4, 4, mesh.shape["tp"]),
        ("fsdp", "ctx_0", "ctx_1", "tp"),
    )
    in_specs = (
        P(FSDP_CTX, None),
        P(FSDP_CTX, None),
        P("fsdp", None),
        P(None, FSDP_CTX, "tp", None),
        P(None, "tp", None, FSDP_CTX),
        P(None, FSDP_CTX, "tp", None),
        P(None, "tp", None, FSDP_CTX),
        P(None, "tp", None),
        P(),
        P(None, FSDP_CTX, "tp", None),
        P(None, "tp", None, FSDP_CTX),
        P(None, FSDP_CTX, "tp", None),
        P(None, "tp", None, FSDP_CTX),
        P(None, "tp", None),
        P(),
        P(None, FSDP_CTX, "tp", None),
        P(None, "tp", None, FSDP_CTX),
        P(None, FSDP_CTX, "tp", None),
        P(None, "tp", None, FSDP_CTX),
        P(None, "tp", None),
        P(),
    )
    out_specs = (
        P(FSDP_CTX, None),
        P(FSDP_CTX, None),
        P(None, FSDP_CTX, "tp", None),
        P(None, FSDP_CTX, "tp", None),
        P(None, FSDP_CTX, "tp", None),
        P(None, "tp", None, FSDP_CTX),
        P(None, "tp", None, FSDP_CTX),
        P(None, "tp", None, FSDP_CTX),
        P(None, FSDP_CTX, "tp", None),
        P(None, FSDP_CTX, "tp", None),
        P(None, FSDP_CTX, "tp", None),
        P(None, "tp", None, FSDP_CTX),
        P(None, "tp", None, FSDP_CTX),
        P(None, "tp", None, FSDP_CTX),
        P(None, "tp", None),
        P(None, "tp", None),
        P(None, "tp", None),
        P(),
        P(),
        P(),
    )
    return jax.shard_map(
        per_device, mesh=torus, in_specs=in_specs, out_specs=out_specs, check_vma=False
    )
```

```python
import functools

import jax
import jax.numpy as jnp
from jax import lax
from jax.experimental import pallas as pl
from jax.experimental.pallas import tpu as pltpu
from jax.sharding import Mesh
from jax.sharding import PartitionSpec as P

HEADS = 8
KV_HEADS = 2
HD = 64
MAMBA_HEADS = 24
MAMBA_HEAD_SIZE = 64
MAMBA_STATE_SIZE = 128
CONV = 4
LAYERS = 2
STEP = 10
DSSM = 1536
FSDP_CTX = ("fsdp", "ctx_0", "ctx_1")
CTX = ("ctx_0", "ctx_1")


highest = lax.Precision.HIGHEST
state_precision = lax.Precision.DEFAULT
D = 1024
IN_COLS = 2060
IN_PAD = 2176
AXES = ("fsdp", "ctx_0", "ctx_1")
SIDE = 4
ROWS = 16
STREAMS = (
    (0, 0, 384, (0, 1, 2), 1),
    (0, 384, 384, (0, 1, 2), -1),
    (0, 768, 384, (1, 2, 0), 1),
    (0, 1152, 384, (1, 2, 0), -1),
    (0, 1536, 384, (2, 0, 1), 1),
    (0, 1920, 256, (2, 0, 1), -1),
)
GRAD_STREAMS = (
    (0, 0, 896, (0, 1, 2), 1),
    (0, 896, 768, (0, 1, 2), -1),
    (0, 1664, 256, (1, 2, 0), 1),
    (0, 1920, 256, (2, 0, 1), -1),
    (1, 0, 2048, (1, 2), 1),
    (1, 2048, 2048, (1, 2), -1),
    (2, 0, 1152, (1, 2), 1),
    (2, 1152, 1024, (2, 1), -1),
    (3, 0, 2048, (2, 1), 1),
    (3, 2048, 2048, (2, 1), -1),
)
GRAD_COUNT = len(GRAD_STREAMS)
KEY_BLOCK = 512
norm_eps = 1e-05
rope_base = 100000000000.0
masked_value = -1e30
beta_one = 0.9
beta_two = 0.95
adam_eps = 1e-08
decay_rate = 0.1
rate_matrix = 0.05
rate_vector = 0.5


def ring_places():
    return tuple(lax.axis_index(a) for a in AXES)


def ring_step(places, axis, by):
    return {AXES[axis]: lax.rem(places[axis] + (by + SIDE), SIDE)}


def greet_neighbours(places):
    barrier = pltpu.get_barrier_semaphore()
    for axis in range(3):
        for by in (1, -1):
            pl.semaphore_signal(
                barrier,
                inc=1,
                device_id=ring_step(places, axis, by),
                device_id_type=pl.DeviceIdType.MESH,
            )
    pl.semaphore_wait(barrier, 6)


def remote(src, dst, send, recv, device):
    return pltpu.make_async_remote_copy(
        src_ref=src,
        dst_ref=dst,
        send_sem=send,
        recv_sem=recv,
        device_id=device,
        device_id_type=pl.DeviceIdType.MESH,
    )


def gather_kernel(shard, full, send, recv, own_sem):
    places = ring_places()
    greet_neighbours(places)
    own = pltpu.make_async_copy(shard, full.at[places[0], places[1], places[2]], own_sem)
    own.start()
    started = []

    def region(number, stage, place):
        _, first, width, order, _ = STREAMS[number]
        order = order[::-1]
        index = list(places)
        for axis in order[:stage]:
            index[axis] = slice(None)
        index[order[stage]] = place
        return full.at[(*index, slice(None), pl.ds(first, width))]

    def launch(number, stage, kind):
        _, first, width, order, way = STREAMS[number]
        axis = order[::-1][stage]
        here = places[axis]
        if kind == 2:
            source = target = region(number, stage, lax.rem(here + (SIDE - way), SIDE))
        else:
            source = target = region(number, stage, here)
            if stage == 0:
                source = shard.at[:, pl.ds(first, width)]
        copy = remote(
            source,
            target,
            send.at[number, stage, kind],
            recv.at[number, stage, kind],
            ring_step(places, axis, -way if kind == 1 else way),
        )
        copy.start()
        started.append(copy)
        return copy

    for stage in range(3):
        if stage == 1:
            own.wait()
        first, back = [], []
        for n in range(6):
            first.append(launch(n, stage, 0))
            back.append(launch(n, stage, 1))
        onward = []
        for n in range(6):
            first[n].wait_recv()
            onward.append(launch(n, stage, 2))
        for n in range(6):
            back[n].wait_recv()
            onward[n].wait_recv()
    for copy in started:
        copy.wait_send()


def gather_weights(part):
    out = pl.pallas_call(
        gather_kernel,
        out_shape=jax.ShapeDtypeStruct((4, 4, 4, *part.shape), part.dtype),
        in_specs=[pl.BlockSpec(memory_space=pl.ANY)],
        out_specs=pl.BlockSpec(memory_space=pl.ANY),
        scratch_shapes=[
            pltpu.SemaphoreType.DMA((6, 3, 3)),
            pltpu.SemaphoreType.DMA((6, 3, 3)),
            pltpu.SemaphoreType.DMA,
        ],
        compiler_params=pltpu.CompilerParams(collective_id=0, has_side_effects=True),
        cost_estimate=pl.CostEstimate(flops=0, bytes_accessed=80000000, transcendentals=0),
        name="gather_weights",
    )(part)
    return out.reshape(D, part.shape[-1])


def scatter_kernel(*refs):
    count = GRAD_COUNT
    grads, small = refs[:4], refs[4]
    refs = refs[5:]
    outs, small_out = refs[:count], refs[count]
    refs = refs[count + 1 :]
    ahead, mine = refs[:count], refs[count : 2 * count]
    refs = refs[2 * count :]
    arrived = (refs[:count], refs[count : 2 * count], refs[2 * count : 2 * count + 4])
    small_in, send, recv, own_sem, small_send, small_recv = refs[2 * count + 4 :]
    places = ring_places()
    greet_neighbours(places)
    started = []

    def near(axis, by):
        return lax.rem(places[axis] + (by + SIDE), SIDE)

    def block(number, stage, place):
        at, first, width, order, _ = GRAD_STREAMS[number]
        axis = order[stage]
        dims = sorted(order)
        if stage == 0:
            index = [slice(None)] * len(dims)
            index[dims.index(axis)] = place
            return grads[at].at[(*index, slice(None), pl.ds(first, width))]
        left = [a for a in dims if a != order[0]]
        index = [slice(None)] * len(left)
        for done in order[1:stage]:
            index[left.index(done)] = places[done]
        index[left.index(axis)] = place
        return mine[number].at[tuple(index)]

    def launch(number, stage, kind, source):
        axis, way = GRAD_STREAMS[number][3][stage], GRAD_STREAMS[number][4]
        copy = remote(
            source,
            arrived[stage][number].at[kind],
            send.at[number, stage, kind],
            recv.at[number, stage, kind],
            ring_step(places, axis, -way if kind == 2 else way),
        )
        copy.start()
        started.append(copy)
        return copy

    def add_into(target, source, lead):
        def one(total, part):
            total[...] = total[...] + part[...]

        if lead == 2:

            def body(k, carry):
                one(target.at[k // 4, k % 4], source.at[k // 4, k % 4])
                return carry

            lax.fori_loop(0, 16, body, 0)
        elif lead == 1:

            def body(k, carry):
                one(target.at[k], source.at[k])
                return carry

            lax.fori_loop(0, 4, body, 0)
        else:
            one(target, source)

    def small_exchange(step):
        axis, odd = step // 2, step % 2
        here = places[axis]
        partner = 3 - here if odd else here + 1 - 2 * lax.rem(here, 2)
        copy = remote(
            small_out,
            small_in.at[step],
            small_send.at[step],
            small_recv.at[step],
            {AXES[axis]: partner},
        )
        copy.start()
        return copy

    def small_finish(copy, step):
        copy.wait_send()
        copy.wait_recv()
        small_out[...] = small_out[...] + small_in[step]

    local = {}
    small_out[...] = small[...]
    for stage in range(3):
        active = [n for n in range(count) if len(GRAD_STREAMS[n][3]) > stage]
        active.sort(key=lambda n: len(GRAD_STREAMS[n][3]))
        first, back, onward = {}, {}, {}
        for n in active:
            axis, way = GRAD_STREAMS[n][3][stage], GRAD_STREAMS[n][4]
            first[n] = launch(n, stage, 0, block(n, stage, near(axis, 2)))
        for n in active:
            axis, way = GRAD_STREAMS[n][3][stage], GRAD_STREAMS[n][4]
            if stage == 0:
                pair = (
                    pltpu.make_async_copy(block(n, 0, near(axis, way)), ahead[n], own_sem.at[n, 0]),
                    pltpu.make_async_copy(block(n, 0, places[axis]), mine[n], own_sem.at[n, 1]),
                )
                for copy in pair:
                    copy.start()
                local[n] = pair
            back[n] = launch(n, stage, 2, block(n, stage, near(axis, -way)))
        step = small_exchange(2 * stage)
        for n in active:
            axis, way = GRAD_STREAMS[n][3][stage], GRAD_STREAMS[n][4]
            if stage == 0:
                local[n][0].wait()
                local[n][1].wait()
                target = ahead[n]
            else:
                target = block(n, stage, near(axis, way))
            first[n].wait_recv()
            add_into(target, arrived[stage][n].at[0], len(GRAD_STREAMS[n][3]) - 1 - stage)
            onward[n] = launch(n, stage, 1, target)
        small_finish(step, 2 * stage)
        step = small_exchange(2 * stage + 1)
        for n in active:
            order = GRAD_STREAMS[n][3]
            lead = len(order) - 1 - stage
            target = mine[n] if stage == 0 else block(n, stage, places[order[stage]])
            back[n].wait_recv()
            if lead:
                add_into(target, arrived[stage][n].at[2], lead)
            onward[n].wait_recv()
            if lead:
                add_into(target, arrived[stage][n].at[1], lead)
            else:
                outs[n][...] = target[...].astype(jnp.float32) + (
                    arrived[stage][n][1].astype(jnp.float32)
                    + arrived[stage][n][2].astype(jnp.float32)
                )
        small_finish(step, 2 * stage + 1)
    for copy in started:
        copy.wait_send()


def scatter_gradients(full, quarters, small):
    vmem = pl.BlockSpec(memory_space=pltpu.VMEM)

    def held(*lead_less):
        return [
            pltpu.VMEM((*lead, *(4,) * (len(s[3]) - less), ROWS, s[2]), jnp.bfloat16)
            for lead, less in lead_less
            for s in GRAD_STREAMS
            if len(s[3]) >= less
        ]

    scratch = held(((), 1), ((), 1), ((3,), 1), ((3,), 2), ((3,), 3))
    scratch += [
        pltpu.VMEM((6, *small.shape), jnp.float32),
        pltpu.SemaphoreType.DMA((GRAD_COUNT, 3, 3)),
        pltpu.SemaphoreType.DMA((GRAD_COUNT, 3, 3)),
        pltpu.SemaphoreType.DMA((GRAD_COUNT, 2)),
        pltpu.SemaphoreType.DMA((6,)),
        pltpu.SemaphoreType.DMA((6,)),
    ]
    shapes = [jax.ShapeDtypeStruct((ROWS, s[2]), jnp.float32) for s in GRAD_STREAMS]
    shapes.append(jax.ShapeDtypeStruct(small.shape, jnp.float32))
    views = [full.reshape(4, 4, 4, ROWS, full.shape[-1])]
    views += [q.reshape(4, 4, ROWS, q.shape[-1]) for q in quarters]
    return pl.pallas_call(
        scatter_kernel,
        out_shape=shapes,
        in_specs=[pl.BlockSpec(memory_space=pl.ANY)] * 4 + [vmem],
        out_specs=[vmem] * (GRAD_COUNT + 1),
        scratch_shapes=scratch,
        compiler_params=pltpu.CompilerParams(
            collective_id=1, has_side_effects=True, vmem_limit_bytes=28 * 2**20
        ),
        cost_estimate=pl.CostEstimate(flops=0, bytes_accessed=100000000, transcendentals=0),
        name="scatter_gradients",
    )(*views, small)


def other_core(value):
    return lax.ppermute(value, "tp", [(0, 1), (1, 0)])


def state_scan(reverse, work, parts, out, got, sums, rows, inside, decays, reply, back, send, recv):
    here, outer = lax.axis_index("ctx_1"), lax.axis_index("ctx_0")
    head = parts.shape[2] - 16
    barrier = pltpu.get_barrier_semaphore()
    for axis, place in (("ctx_1", here), ("ctx_0", outer)):
        for by in range(1, SIDE):
            pl.semaphore_signal(
                barrier,
                inc=1,
                device_id={axis: lax.rem(place + by, SIDE)},
                device_id_type=pl.DeviceIdType.MESH,
            )
    pl.semaphore_wait(barrier, 6)
    started = []

    def spread(stage, axis, place, source, target):
        copies = []
        for by in (2, 1, 3):
            other = lax.rem(place + by, SIDE)
            copy = remote(
                source(other),
                target.at[place],
                send.at[stage, by - 1],
                recv.at[stage, by - 1],
                {axis: other},
            )
            copy.start()
            copies.append(copy)
        started.extend(copies)
        return copies

    def opened(ref, k):
        wide = ref[k].astype(jnp.float32)
        return wide[:, head : head + 1, :], wide[:, :head, :]

    order = range(SIDE - 1, -1, -1) if reverse else range(SIDE)
    copies = spread(0, "ctx_1", here, lambda other: parts.at[other], got)
    got[here] = parts[here]
    work(0)
    for copy in copies:
        copy.wait_recv()
    decay = state = None
    for k in order:
        own_decay, own_state = opened(got, k)
        if decay is None:
            decay, state = own_decay, own_state
        else:
            decays[k] = decay
            inside[k] = state
            decay, state = decay * own_decay, own_decay * state + own_state
    sums[:, :head, :] = state.astype(jnp.bfloat16)
    sums[:, head:, :] = jnp.broadcast_to(decay, (decay.shape[0], 16, decay.shape[2])).astype(
        jnp.bfloat16
    )
    copies = spread(1, "ctx_0", outer, lambda other: sums, rows)
    rows[outer] = sums[...]
    work(1)
    for copy in copies:
        copy.wait_recv()
    before = jnp.zeros(inside.shape[1:], jnp.float32)
    state = None
    for k in order:
        if state is not None:
            before = jnp.where(outer == k, state, before)
        own_decay, own_state = opened(rows, k)
        state = own_state if state is None else own_decay * state + own_state
    for k in order:
        if k == order[0]:
            reply[k] = before.astype(jnp.bfloat16)
        else:
            reply[k] = (decays[k] * before + inside[k]).astype(jnp.bfloat16)
    copies = spread(2, "ctx_1", here, lambda other: reply.at[other], back)
    back[here] = reply[here]
    work(2)
    for copy in copies:
        copy.wait_recv()
    out[...] = back[...].astype(jnp.float32)
    for copy in started:
        copy.wait_send()


def turned(value):
    return value.astype(jnp.float32).T.astype(value.dtype)


def seen_keys(block, lowest, highest_key):
    at = block * KEY_BLOCK + lax.broadcasted_iota(jnp.int32, (KEY_BLOCK, lowest.shape[1]), 0)
    return (at >= lowest[...]) & (at <= highest_key[...])


def key_block(kv, block):
    return kv[pl.ds(pl.multiple_of(block * KEY_BLOCK, KEY_BLOCK), KEY_BLOCK), :]


def shared_out(total, body):
    bounds = (0, total * 3 // 8, total * 5 // 8, total)

    def work(stage):
        lax.fori_loop(bounds[stage], bounds[stage + 1], body, 0)

    return work


def scan_attend_kernel(
    parts, kv, queries, lowest, highest_key, out, attended, log_total, queries_t, top, total, mix, *rest
):
    scale = HD ** (-0.5)
    queries_t[...] = turned(queries[...])
    top[...] = jnp.full_like(top, masked_value)
    total[...] = jnp.zeros_like(total)
    mix[...] = jnp.zeros_like(mix)

    def body(block, carry):
        pair = key_block(kv, block)
        keys, values_t = pair[:, :HD], turned(pair)[HD:, :]
        seen = seen_keys(block, lowest, highest_key)
        for g in range(queries.shape[1] // HD):
            head = slice(g * HD, (g + 1) * HD)
            raw = jnp.dot(keys, queries_t[head, :], preferred_element_type=jnp.float32)
            logits = jnp.where(seen, raw * scale, masked_value)
            old = top[g : g + 1, :]
            new = jnp.maximum(old, jnp.max(logits, axis=0, keepdims=True))
            shrink = jnp.exp(old - new)
            weight = jnp.exp(logits - new)
            top[g : g + 1, :] = new
            total[g : g + 1, :] = total[g : g + 1, :] * shrink + jnp.sum(
                weight, axis=0, keepdims=True
            )
            mix[head, :] = mix[head, :] * shrink + jnp.dot(
                values_t, weight.astype(jnp.bfloat16), preferred_element_type=jnp.float32
            )
        return carry

    state_scan(False, shared_out(kv.shape[0] // KEY_BLOCK, body), parts, out, *rest)
    log_total[...] = top[...] + jnp.log(total[...])
    for g in range(queries.shape[1] // HD):
        head = slice(g * HD, (g + 1) * HD)
        mix[head, :] = mix[head, :] / total[g : g + 1, :]
    attended[...] = mix[...].T


def scan_attend_back_kernel(
    parts,
    kv,
    queries,
    d_att,
    attended,
    log_total,
    lowest,
    highest_key,
    out,
    d_kv,
    d_query,
    queries_t,
    d_att_t,
    delta,
    d_query_t,
    *rest,
):
    scale = HD ** (-0.5)
    groups = queries.shape[1] // HD
    queries_t[...] = turned(queries[...])
    d_att_t[...] = turned(d_att[...])
    product = d_att_t[...].astype(jnp.float32) * attended[...].T
    for g in range(groups):
        delta[g : g + 1, :] = jnp.sum(product[g * HD : (g + 1) * HD, :], axis=0, keepdims=True)
    d_query_t[...] = jnp.zeros_like(d_query_t)

    def body(block, carry):
        pair = key_block(kv, block)
        keys, values, keys_t = pair[:, :HD], pair[:, HD:], turned(pair)[:HD, :]
        seen = seen_keys(block, lowest, highest_key)
        d_key = jnp.zeros((KEY_BLOCK, HD), jnp.float32)
        d_value = jnp.zeros((KEY_BLOCK, HD), jnp.float32)
        for g in range(groups):
            head = slice(g * HD, (g + 1) * HD)
            raw = jnp.dot(keys, queries_t[head, :], preferred_element_type=jnp.float32)
            logits = jnp.where(seen, raw * scale, masked_value)
            prob = jnp.exp(logits - log_total[g : g + 1, :])
            d_prob = jnp.dot(values, d_att_t[head, :], preferred_element_type=jnp.float32)
            d_raw = (prob * (d_prob - delta[g : g + 1, :]) * scale).astype(jnp.bfloat16)
            d_value += jnp.dot(
                prob.astype(jnp.bfloat16), d_att[:, head], preferred_element_type=jnp.float32
            )
            d_key += jnp.dot(d_raw, queries[:, head], preferred_element_type=jnp.float32)
            d_query_t[head, :] += jnp.dot(keys_t, d_raw, preferred_element_type=jnp.float32)
        both = jnp.concatenate([d_key, d_value], axis=1).astype(jnp.bfloat16)
        d_kv[pl.ds(pl.multiple_of(block * KEY_BLOCK, KEY_BLOCK), KEY_BLOCK), :] = both
        return carry

    state_scan(True, shared_out(kv.shape[0] // KEY_BLOCK, body), parts, out, *rest)
    d_query[...] = d_query_t[...].T


def entering(decay, state, reverse, shapes, scratch, *arrays):
    heads = decay.shape[0]
    chunk = heads // SIDE
    size, width = state.shape[1:]
    rows = jnp.broadcast_to(decay[:, None, None], (heads, 16, width))
    message = jnp.concatenate([state, rows], axis=1).astype(jnp.bfloat16)
    message = message.reshape(SIDE, chunk, size + 16, width)
    vmem = pl.BlockSpec(memory_space=pltpu.VMEM)
    out, *others = pl.pallas_call(
        scan_attend_back_kernel if reverse else scan_attend_kernel,
        out_shape=[jax.ShapeDtypeStruct((SIDE, chunk, size, width), jnp.float32), *shapes],
        in_specs=[vmem] * (1 + len(arrays)),
        out_specs=[vmem] * (1 + len(shapes)),
        scratch_shapes=[
            *scratch,
            pltpu.VMEM((SIDE, chunk, size + 16, width), jnp.bfloat16),
            pltpu.VMEM((chunk, size + 16, width), jnp.bfloat16),
            pltpu.VMEM((SIDE, chunk, size + 16, width), jnp.bfloat16),
            pltpu.VMEM((SIDE, chunk, size, width), jnp.float32),
            pltpu.VMEM((SIDE, chunk, 1, width), jnp.float32),
            pltpu.VMEM((SIDE, chunk, size, width), jnp.bfloat16),
            pltpu.VMEM((SIDE, chunk, size, width), jnp.bfloat16),
            pltpu.SemaphoreType.DMA((3, 3)),
            pltpu.SemaphoreType.DMA((3, 3)),
        ],
        compiler_params=pltpu.CompilerParams(
            collective_id=3 if reverse else 2,
            has_side_effects=True,
            vmem_limit_bytes=32 * 2**20,
        ),
        cost_estimate=pl.CostEstimate(
            flops=3000000000, bytes_accessed=40000000, transcendentals=4000000
        ),
        name="scan_attend_back" if reverse else "scan_attend",
    )(message, *arrays)
    return out.reshape(heads, size, width), *others


def from_everyone(value, axis):
    copies = jnp.broadcast_to(value, (lax.axis_size(axis), *value.shape))
    return lax.all_to_all(copies, axis, split_axis=0, concat_axis=0, tiled=True)


def joined_along(pieces, dim):
    shape = list(pieces.shape[1:])
    shape[dim] *= pieces.shape[0]
    return jnp.moveaxis(pieces, 0, dim).reshape(shape)


def gathered_copies(value, axis, dim):
    pieces = from_everyone(value, axis)
    return joined_along(pieces, dim)


def passed_along(value, axis, by):
    count = lax.axis_size(axis)
    pairs = [(i, i + by) for i in range(count) if 0 <= i + by < count]
    return lax.ppermute(value, axis, pairs)


def split_up(value, dim, count):
    before, after = (value.shape[:dim], value.shape[dim + 1 :])
    return jnp.moveaxis(value.reshape(*before, count, -1, *after), dim, 0)


def summed_on_arrival(value, axis, dim):
    pieces = split_up(value, dim, lax.axis_size(axis))
    arrived = lax.all_to_all(pieces, axis, split_axis=0, concat_axis=0, tiled=True)
    return arrived.astype(jnp.float32).sum(axis=0)


def rms_norm(value, gain):
    return value * lax.rsqrt(jnp.mean(value * value, axis=-1, keepdims=True) + norm_eps) * gain


def silu_slope(value):
    sigma = jax.nn.sigmoid(value)
    return sigma * (1.0 + value * (1.0 - sigma))


def doc_layout(doc_row, start_row, item_count):
    ends = jnp.cumsum(doc_row)
    starts = ends - doc_row
    token_index = start_row + jnp.arange(item_count, dtype=jnp.int32)
    segment = jnp.sum((token_index[:, None] >= ends[None, :]).astype(jnp.int32), axis=1)
    picked = segment[:, None] == jnp.arange(doc_row.shape[0], dtype=jnp.int32)[None, :]
    begin = jnp.sum(jnp.where(picked, starts[None, :], 0), axis=1)
    return (segment, token_index - begin)


def rope_tables(position):
    freq = rope_base ** (-2.0 * jnp.arange(HD // 2, dtype=jnp.float32) / HD)
    angle = position.astype(jnp.float32)[:, None] * freq[None, :]
    return (jnp.cos(angle), jnp.sin(angle))


def rotate(value, cosine, sine):
    shaped = value.reshape(value.shape[0], -1, 2, HD // 2)
    first_half = shaped[:, :, 0]
    second_half = shaped[:, :, 1]
    cos_part = cosine[:, None, :]
    sin_part = sine[:, None, :]
    turned = jnp.stack(
        [
            first_half * cos_part - second_half * sin_part,
            second_half * cos_part + first_half * sin_part,
        ],
        axis=2,
    )
    return turned.reshape(value.shape)


def conv_act(extended, conv_taps, conv_bias, seg_ext):
    item_count = extended.shape[0] - (CONV - 1)
    own_seg = seg_ext[CONV - 1 :]
    total = conv_bias[None, :] + conv_taps[CONV - 1][None, :] * extended[CONV - 1 :]
    for back in range(1, CONV):
        begin = CONV - 1 - back
        same = seg_ext[begin : begin + item_count] == own_seg
        total = total + conv_taps[CONV - 1 - back][None, :] * jnp.where(
            same[:, None], extended[begin : begin + item_count], 0.0
        )
    return jax.nn.silu(total)


def decay_terms(drive_input, dt_bias, a_log):
    dt_step = jax.nn.softplus(drive_input + dt_bias)
    order = jnp.arange(dt_step.shape[0], dtype=jnp.int32)
    upto = (order[None, :] <= order[:, None]).astype(jnp.float32)
    return (dt_step, jnp.dot(upto, -dt_step * jnp.exp(a_log), precision=highest))


def head_columns(heads):
    column = jnp.arange(heads * MAMBA_HEAD_SIZE, dtype=jnp.int32) // MAMBA_HEAD_SIZE
    return (column[None, :] == jnp.arange(heads, dtype=jnp.int32)[:, None]).astype(jnp.float32)


def spread_heads(value, columns):
    return jnp.dot(value, columns, precision=highest, preferred_element_type=jnp.float32)


def fold_heads(value, columns):
    return lax.dot_general(
        value,
        columns,
        (((1,), (1,)), ((), ())),
        precision=highest,
        preferred_element_type=jnp.float32,
    )


def cross(left, right):
    return lax.dot_general(
        left, right, (((1,), (1,)), ((), ())), preferred_element_type=jnp.float32
    )


def same_document(seg_col, seg_row, flipped):
    count = seg_col.shape[0]
    down = lax.broadcasted_iota(jnp.int32, (count, count), 0)
    over = lax.broadcasted_iota(jnp.int32, (count, count), 1)
    earlier = (down <= over) if flipped else (over <= down)
    return earlier & (seg_col == seg_row)


def state_forth_kernel(
    x, both, log_col, log_row, dt_step, entry, skip, seg_col, seg_row, state, columns, out
):
    b_mat, c_mat = both[:, :MAMBA_STATE_SIZE], both[:, MAMBA_STATE_SIZE:]
    seen = same_document(seg_col[...], seg_row[...], False)
    inner_prod = cross(c_mat, b_mat)
    spreader = columns[...]
    driven = (x[...] * spread_heads(dt_step[...], spreader)).astype(jnp.bfloat16)
    carried = cross(c_mat, state[...].astype(jnp.bfloat16))
    base = carried * spread_heads(entry[...], spreader) + skip[...] * x[...]
    for pair in range(log_row.shape[0] // 2):
        halves = []
        for h in (2 * pair, 2 * pair + 1):
            fade = log_col[:, h : h + 1] - log_row[h : h + 1, :]
            mixing = jnp.exp(jnp.where(seen, fade, masked_value)) * inner_prod
            at = h * MAMBA_HEAD_SIZE
            halves.append(
                jnp.dot(
                    mixing.astype(jnp.bfloat16),
                    driven[:, at : at + MAMBA_HEAD_SIZE],
                    preferred_element_type=jnp.float32,
                )
            )
        at = 2 * pair * MAMBA_HEAD_SIZE
        till = at + 2 * MAMBA_HEAD_SIZE
        out[:, at:till] = base[:, at:till] + jnp.concatenate(halves, axis=1)


def state_back_kernel(
    x,
    y,
    d_y,
    both,
    log_col,
    log_row,
    dt_step,
    fading,
    entry,
    skip,
    seg_col,
    seg_row,
    state,
    later,
    columns,
    d_x,
    d_both,
    by_dt,
    by_log,
    by_skip,
):
    b_mat, c_mat = both[:, :MAMBA_STATE_SIZE], both[:, MAMBA_STATE_SIZE:]
    seen = same_document(seg_col[...], seg_row[...], True)
    inner_prod = cross(b_mat, c_mat)
    spreader = columns[...]
    x_all, d_all = x[...], d_y[...]
    x_b, d_b = x_all.astype(jnp.bfloat16), d_all.astype(jnp.bfloat16)
    later_b, state_b = later[...].astype(jnp.bfloat16), state[...].astype(jnp.bfloat16)
    d_inner_prod = jnp.zeros_like(inner_prod)
    parts = []
    for h in range(log_row.shape[0]):
        at = h * MAMBA_HEAD_SIZE
        fade = log_row[h : h + 1, :] - log_col[:, h : h + 1]
        kernel = jnp.exp(jnp.where(seen, fade, masked_value))
        d_mixing = cross(x_b[:, at : at + MAMBA_HEAD_SIZE], d_b[:, at : at + MAMBA_HEAD_SIZE])
        d_inner_prod += kernel * d_mixing * dt_step[:, h : h + 1]
        parts.append(
            jnp.dot(
                (kernel * inner_prod).astype(jnp.bfloat16),
                d_b[:, at : at + MAMBA_HEAD_SIZE],
                preferred_element_type=jnp.float32,
            )
        )
    fade_all = spread_heads(fading[...], spreader)
    dt_all = spread_heads(dt_step[...], spreader)
    pulled = jnp.concatenate(parts, axis=1) + fade_all * cross(b_mat, later_b)
    d_x[...] = dt_all * pulled + skip[...] * d_all
    by_dt[...] = fold_heads(x_all * pulled, spreader)
    by_log[...] = fold_heads(d_all * (y[...] - skip[...] * x_all), spreader)
    by_skip[...] = fold_heads(d_all * x_all, spreader)
    d_inner_b = d_inner_prod.astype(jnp.bfloat16)
    d_b_mat = jnp.dot(d_inner_b, c_mat, preferred_element_type=jnp.float32) + jnp.dot(
        (x_all * fade_all * dt_all).astype(jnp.bfloat16),
        later_b,
        preferred_element_type=jnp.float32,
    )
    d_c_mat = lax.dot_general(
        d_inner_b, b_mat, (((0,), (0,)), ((), ())), preferred_element_type=jnp.float32
    ) + jnp.dot(
        (d_all * spread_heads(entry[...], spreader)).astype(jnp.bfloat16),
        state_b,
        preferred_element_type=jnp.float32,
    )
    d_both[...] = jnp.concatenate([d_b_mat, d_c_mat], axis=1)


def state_call(kernel, shapes, name, *arrays):
    vmem = pl.BlockSpec(memory_space=pltpu.VMEM)
    return pl.pallas_call(
        kernel,
        out_shape=shapes,
        in_specs=[vmem] * len(arrays),
        out_specs=jax.tree.map(lambda s: vmem, shapes),
        compiler_params=pltpu.CompilerParams(vmem_limit_bytes=32 * 2**20),
        cost_estimate=pl.CostEstimate(
            flops=2000000000, bytes_accessed=8000000, transcendentals=800000
        ),
        name=name,
    )(*arrays)


def decay_parts(drive_input, dt_bias, a_log, segment, position):
    dt_step, log_cum = decay_terms(drive_input, dt_bias, a_log)
    count = log_cum.shape[0]
    last = log_cum[count - 1]
    in_last = (segment == segment[count - 1]).astype(jnp.float32)
    fading = jnp.exp(last[None, :] - log_cum) * in_last[:, None]
    carry_on = ((segment == segment[0]) & (position[0] != 0)).astype(jnp.float32)
    entry = jnp.exp(log_cum) * carry_on[:, None]
    return dt_step, log_cum, fading, entry, carry_on[count - 1] * jnp.exp(last)


def split_vector(vector, widths):
    q_width, k_width, s_width, b_width, h_width = widths
    channels = s_width + b_width
    conv_taps = vector[: CONV * channels].reshape(CONV, channels)
    offset = CONV * channels
    conv_bias = vector[offset : offset + channels]
    offset = offset + channels
    gated_gain = vector[offset : offset + s_width]
    offset = offset + s_width
    return (
        conv_taps,
        conv_bias,
        gated_gain,
        vector[offset : offset + h_width],
        vector[offset + h_width : offset + 2 * h_width],
        vector[offset + 2 * h_width : offset + 3 * h_width],
    )


def feature_sum(value):
    own = value.astype(jnp.bfloat16)
    return own.astype(jnp.float32) + other_core(own).astype(jnp.float32)


def norm_sum(value):
    return value + other_core(value)


def local_matrices(w_in, w_out, w_gu, w_down, layer_at):
    return (
        jnp.pad(w_in[layer_at, :, 0, :], ((0, 0), (0, IN_PAD - IN_COLS))).astype(jnp.bfloat16),
        w_gu[layer_at, :, 0, :].astype(jnp.bfloat16),
        w_out[layer_at, 0].T.astype(jnp.bfloat16),
        w_down[layer_at, 0].T.astype(jnp.bfloat16),
    )


def fetch_layers(w_in, w_out, w_gu, w_down):
    parts = [local_matrices(w_in, w_out, w_gu, w_down, k) for k in range(LAYERS)]
    rest = (*parts[0][1:], *parts[1])
    filled = lax.all_gather(jnp.concatenate(rest, axis=1), FSDP_CTX, axis=0, tiled=True)
    bounds, at = [], 0
    for part in rest[:-1]:
        at += part.shape[1]
        bounds.append(at)
    pieces = jnp.split(filled, bounds, axis=1)
    return (gather_weights(parts[0][0]), *pieces[:3]), tuple(pieces[3:])


def layer_forward(state, weights, vector, gains, context, widths):
    w_in_b, w_gu_b, w_out_t, w_down_t = weights
    segment, position, seg_ext, cosine, sine, lowest, highest_key = context
    q_width, k_width, s_width, b_width, h_width = widths
    conv_taps, conv_bias, gated_gain, a_log, dt_bias, d_skip = split_vector(vector, widths)
    item_count = state.shape[0]
    at_v = q_width + k_width
    at_z = at_v + k_width
    at_x = at_z + s_width
    at_t = at_x + s_width + b_width
    hidden_b = rms_norm(state, gains[0]).astype(jnp.bfloat16)
    proj = jnp.dot(hidden_b, w_in_b, preferred_element_type=jnp.float32)
    queries_b = rotate(proj[:, :q_width], cosine, sine).astype(jnp.bfloat16)
    pair = jnp.concatenate(
        [rotate(proj[:, q_width:at_v], cosine, sine), proj[:, at_v:at_z]], axis=1
    ).astype(jnp.bfloat16)
    key_values = gathered_copies(pair, CTX, 0)
    mixed_in = proj[:, at_x:at_t]
    halo_rows = passed_along(mixed_in[item_count - (CONV - 1) :], CTX, 1)
    extended = jnp.concatenate([halo_rows, mixed_in], axis=0)
    active = conv_act(extended, conv_taps, conv_bias, seg_ext)
    own_part = active[:, s_width:].astype(jnp.bfloat16)
    other_part = other_core(own_part)
    leads = lax.axis_index("tp") == 0
    both = jnp.concatenate(
        [jnp.where(leads, own_part, other_part), jnp.where(leads, other_part, own_part)], axis=1
    )
    inner_input = active[:, :s_width]
    drive_input = proj[:, at_t : at_t + h_width]
    columns = head_columns(h_width)
    timing = decay_parts(drive_input, dt_bias, a_log, segment, position)
    dt_step, log_cum, fading, entry, decay_own = timing
    weighted = inner_input * spread_heads(fading * dt_step, columns)
    state_own = jnp.einsum("sc,sn->cn", weighted, both[:, :MAMBA_STATE_SIZE].astype(jnp.float32))
    state_own = state_own.reshape(h_width, MAMBA_HEAD_SIZE, MAMBA_STATE_SIZE)
    groups = q_width // HD
    by_query = jax.ShapeDtypeStruct((groups, item_count), jnp.float32)
    state_in, attended, log_total = entering(
        decay_own,
        state_own,
        False,
        [jax.ShapeDtypeStruct((item_count, q_width), jnp.float32), by_query],
        [
            pltpu.VMEM((q_width, item_count), jnp.bfloat16),
            pltpu.VMEM((groups, item_count), jnp.float32),
            pltpu.VMEM((groups, item_count), jnp.float32),
            pltpu.VMEM((q_width, item_count), jnp.float32),
        ],
        key_values,
        queries_b,
        lowest,
        highest_key,
    )
    ssm = state_call(
        state_forth_kernel,
        jax.ShapeDtypeStruct(inner_input.shape, jnp.float32),
        "state_forth",
        inner_input,
        both,
        log_cum,
        log_cum.T,
        dt_step,
        entry,
        spread_heads(d_skip[None, :], columns),
        segment[:, None],
        segment[None, :],
        state_in.reshape(s_width, MAMBA_STATE_SIZE),
        columns,
    )
    gated = ssm * jax.nn.silu(proj[:, at_z:at_x])
    inverse = lax.rsqrt(norm_sum(jnp.sum(gated * gated, axis=1)) / DSSM + norm_eps)[:, None]
    features = jnp.concatenate([attended, gated * inverse * gated_gain], axis=1).astype(
        jnp.bfloat16
    )
    middle = state + feature_sum(
        jnp.einsum("tc,dc->td", features, w_out_t, preferred_element_type=jnp.float32)
    )
    hidden2_b = rms_norm(middle, gains[1]).astype(jnp.bfloat16)
    upgate = jnp.dot(hidden2_b, w_gu_b, preferred_element_type=jnp.float32)
    half_width = upgate.shape[1] // 2
    inner_b = (jax.nn.silu(upgate[:, :half_width]) * upgate[:, half_width:]).astype(jnp.bfloat16)
    final_result = middle + feature_sum(
        jnp.einsum("tf,df->td", inner_b, w_down_t, preferred_element_type=jnp.float32)
    )
    kept = (
        state,
        hidden_b,
        proj,
        queries_b,
        key_values,
        log_total,
        extended,
        active,
        both,
        state_in,
        state_own,
        timing,
        ssm,
        gated,
        inverse,
        features,
        middle,
        hidden2_b,
        upgate,
        inner_b,
        attended,
    )
    return (final_result, kept)


def layer_backward(grad_out, kept, weights, vector, gains, context, widths, waiting):
    w_in_b, w_gu_b, w_out_t, w_down_t = weights
    segment, position, seg_ext, cosine, sine, lowest, highest_key = context
    q_width, k_width, s_width, b_width, h_width = widths
    conv_taps, conv_bias, gated_gain, a_log, dt_bias, d_skip = split_vector(vector, widths)
    (
        state,
        hidden_b,
        proj,
        queries_b,
        key_values,
        log_total,
        extended,
        active,
        both,
        state_in,
        state_own,
        timing,
        ssm,
        gated,
        inverse,
        features,
        middle,
        hidden2_b,
        upgate,
        inner_b,
        attended,
    ) = kept
    item_count = state.shape[0]
    at_v = q_width + k_width
    at_z = at_v + k_width
    at_x = at_z + s_width
    at_t = at_x + s_width + b_width
    grad_b = grad_out.astype(jnp.bfloat16)
    grad_down = jnp.einsum(
        "td,tf->df", grad_b, inner_b, preferred_element_type=jnp.float32
    ).astype(jnp.bfloat16)
    d_inner = jnp.dot(grad_b, w_down_t, preferred_element_type=jnp.float32)
    half_width = upgate.shape[1] // 2
    gate_part = upgate[:, :half_width]
    d_upgate_b = jnp.concatenate(
        [
            d_inner * upgate[:, half_width:] * silu_slope(gate_part),
            d_inner * jax.nn.silu(gate_part),
        ],
        axis=1,
    ).astype(jnp.bfloat16)
    grad_gu = jnp.einsum(
        "td,tf->df", hidden2_b, d_upgate_b, preferred_element_type=jnp.float32
    ).astype(jnp.bfloat16)
    d_hidden2 = feature_sum(
        jnp.einsum("tf,df->td", d_upgate_b, w_gu_b, preferred_element_type=jnp.float32)
    )
    d_middle_norm, d_gain_mlp = jax.vjp(rms_norm, middle, gains[1])[1](d_hidden2)
    d_middle = grad_out + d_middle_norm
    mix_b = d_middle.astype(jnp.bfloat16)
    grad_out_proj = jnp.einsum(
        "td,tc->dc", mix_b, features, preferred_element_type=jnp.float32
    ).astype(jnp.bfloat16)
    early = lax.psum_scatter(
        jnp.concatenate([grad_gu, grad_down, grad_out_proj], axis=1), "fsdp", tiled=True
    )
    d_features = jnp.dot(mix_b, w_out_t, preferred_element_type=jnp.float32)
    d_normed = d_features[:, q_width:]
    weighted = d_normed * gated_gain
    d_gated_gain = jnp.sum(d_normed * gated * inverse, axis=0)
    across = norm_sum(jnp.sum(weighted * gated, axis=1))[:, None]
    d_gated = weighted * inverse - gated * inverse**3 * across / DSSM
    gate_z = proj[:, at_z:at_x]
    d_ssm = d_gated * jax.nn.silu(gate_z)
    d_gate_z = d_gated * ssm * silu_slope(gate_z)
    inner_input = active[:, :s_width]
    drive_input = proj[:, at_t : at_t + h_width]

    dt_step, log_cum, fading, entry, decay_own = timing
    columns = head_columns(h_width)
    d_carry = jnp.einsum(
        "tc,tn->cn",
        d_ssm * spread_heads(entry, columns),
        both[:, MAMBA_STATE_SIZE:].astype(jnp.float32),
    ).reshape(state_in.shape)
    later, d_pair_all, d_query = entering(
        decay_own,
        d_carry,
        True,
        [
            jax.ShapeDtypeStruct(key_values.shape, jnp.bfloat16),
            jax.ShapeDtypeStruct((item_count, q_width), jnp.float32),
        ],
        [
            pltpu.VMEM((q_width, item_count), jnp.bfloat16),
            pltpu.VMEM((q_width, item_count), jnp.bfloat16),
            pltpu.VMEM((q_width // HD, item_count), jnp.float32),
            pltpu.VMEM((q_width, item_count), jnp.float32),
        ],
        key_values,
        queries_b,
        d_features[:, :q_width].astype(jnp.bfloat16),
        attended,
        log_total,
        lowest,
        highest_key,
    )
    if waiting is not None:
        d_pair_all, waiting = lax.optimization_barrier((d_pair_all, waiting))
    d_pair = summed_on_arrival(d_pair_all, CTX, 0)
    by_head = jax.ShapeDtypeStruct(dt_step.shape, jnp.float32)
    d_inner_input, d_both, by_dt, by_log, by_skip = state_call(
        state_back_kernel,
        [
            jax.ShapeDtypeStruct(inner_input.shape, jnp.float32),
            jax.ShapeDtypeStruct(both.shape, jnp.float32),
            by_head,
            by_head,
            by_head,
        ],
        "state_back",
        inner_input,
        ssm,
        d_ssm,
        both,
        log_cum,
        log_cum.T,
        dt_step,
        fading,
        entry,
        spread_heads(d_skip[None, :], columns),
        segment[:, None],
        segment[None, :],
        state_in.reshape(s_width, MAMBA_STATE_SIZE),
        later.reshape(s_width, MAMBA_STATE_SIZE),
        columns,
    )
    at_end = jnp.sum(later * (state_own + decay_own[:, None, None] * state_in), axis=(1, 2))
    order = jnp.arange(item_count, dtype=jnp.int32)
    d_log_cum = by_log - dt_step * by_dt
    onward = (order[None, :] >= order[:, None]).astype(jnp.float32)
    d_log_decay = jnp.dot(onward, d_log_cum, precision=highest) + at_end[None, :]
    d_dt = by_dt - jnp.exp(a_log) * d_log_decay
    d_drive = d_dt * jax.nn.sigmoid(drive_input + dt_bias)
    d_a_log = -jnp.sum(d_log_decay * dt_step, axis=0) * jnp.exp(a_log)
    d_dt_bias = jnp.sum(d_drive, axis=0)
    d_skip_grad = jnp.sum(by_skip, axis=0)
    d_both_b = d_both.astype(jnp.bfloat16)
    leads = lax.axis_index("tp") == 0
    kept_part = jnp.where(leads, d_both_b[:, :b_width], d_both_b[:, b_width:])
    sent_part = jnp.where(leads, d_both_b[:, b_width:], d_both_b[:, :b_width])
    d_own = kept_part.astype(jnp.float32) + other_core(sent_part).astype(jnp.float32)

    def conv_part(ext_part, taps_part, bias_part):
        return conv_act(ext_part, taps_part, bias_part, seg_ext)

    conv_pull = jax.vjp(conv_part, extended, conv_taps, conv_bias)[1]
    d_extended, d_taps, d_bias = conv_pull(jnp.concatenate([d_inner_input, d_own], axis=1))
    spill = passed_along(d_extended[: CONV - 1], CTX, -1)
    d_mixed = jnp.concatenate(
        [d_extended[CONV - 1 : item_count], d_extended[item_count:] + spill], axis=0
    )
    d_proj_b = jnp.concatenate(
        [
            rotate(d_query, cosine, -sine),
            rotate(d_pair[:, :HD], cosine, -sine),
            d_pair[:, HD:],
            d_gate_z,
            d_mixed,
            d_drive,
            jnp.zeros((item_count, IN_PAD - IN_COLS), jnp.float32),
        ],
        axis=1,
    ).astype(jnp.bfloat16)
    grad_in = jnp.einsum(
        "td,tc->dc", hidden_b, d_proj_b, preferred_element_type=jnp.float32
    ).astype(jnp.bfloat16)
    d_hidden = feature_sum(
        jnp.einsum("tc,dc->td", d_proj_b, w_in_b, preferred_element_type=jnp.float32)
    )
    d_state_norm, d_gain_mix = jax.vjp(rms_norm, state, gains[0])[1](d_hidden)
    d_vector = jnp.concatenate(
        [
            d_taps.reshape(-1),
            d_bias,
            d_gated_gain,
            d_a_log,
            d_dt_bias,
            d_skip_grad,
        ]
    )
    return (
        d_middle + d_state_norm,
        grad_in,
        early,
        waiting,
        d_vector,
        jnp.stack([d_gain_mix, d_gain_mlp]),
    )


def adamw(weight, first_m, second_m, grad, rate, decay):
    first_new = beta_one * first_m + (1.0 - beta_one) * grad
    second_new = beta_two * second_m + (1.0 - beta_two) * grad * grad
    ratio = (
        first_new
        / (1.0 - beta_one**STEP)
        / (jnp.sqrt(second_new / (1.0 - beta_two**STEP)) + adam_eps)
    )
    return (first_new, second_new, weight - rate * (ratio + decay * weight))


def per_device(
    block_input,
    cotangent,
    lengths,
    w_in,
    w_out,
    w_gu,
    w_down,
    vectors,
    norm_gains,
    first_in,
    first_out,
    first_gu,
    first_down,
    first_vectors,
    first_gains,
    second_in,
    second_out,
    second_gu,
    second_down,
    second_vectors,
    second_gains,
):
    group_count = lax.axis_size("tp")
    widths = (
        HEADS * HD // group_count,
        KV_HEADS * HD // group_count,
        MAMBA_HEADS * MAMBA_HEAD_SIZE // group_count,
        2 * MAMBA_STATE_SIZE // group_count,
        MAMBA_HEADS // group_count,
    )
    item_count = block_input.shape[0]
    start_row = lax.axis_index(CTX) * item_count
    doc_row = lengths[0]
    segment, position = doc_layout(doc_row, start_row, item_count)
    seg_ext = doc_layout(doc_row, start_row - (CONV - 1), item_count + CONV - 1)[0]
    query_index = start_row + jnp.arange(item_count, dtype=jnp.int32)
    cosine, sine = rope_tables(position)
    lowest, highest_key = (query_index - position)[None, :], query_index[None, :]
    context = (segment, position, seg_ext, cosine, sine, lowest, highest_key)
    stored = []
    state = block_input
    fetched = fetch_layers(w_in, w_out, w_gu, w_down)
    for layer_at in range(LAYERS):
        weights = fetched[layer_at]
        state, kept = layer_forward(
            state, weights, vectors[layer_at, 0], norm_gains[layer_at], context, widths
        )
        stored.append(kept)
    grad_state = cotangent
    early_parts = [None] * LAYERS
    waiting = None
    small_parts = [None] * LAYERS
    vec = vectors.shape[-1]
    for layer_at in reversed(range(LAYERS)):
        grad_state, late, early, waiting, d_vector, d_gains = layer_backward(
            grad_state,
            stored[layer_at],
            fetched[layer_at],
            vectors[layer_at, 0],
            norm_gains[layer_at],
            context,
            widths,
            waiting,
        )
        if layer_at:
            grad_state, early = lax.optimization_barrier((grad_state, early))
            waiting = lax.psum_scatter(late, "fsdp", tiled=True)
        else:
            late_parts = (late, waiting)
        early_parts[layer_at] = early
        small_parts[layer_at] = jnp.concatenate([d_vector, d_gains.reshape(-1)])
    small = jnp.concatenate(small_parts)
    span = -(-small.shape[0] // 1024) * 8
    small = jnp.pad(small, (0, span * 128 - small.shape[0])).reshape(span, 128)
    *pieces, small = scatter_gradients(
        late_parts[0], (early_parts[1], late_parts[1], early_parts[0]), small
    )
    shards = [
        (
            jnp.concatenate(some, axis=1)[:, :IN_COLS],
            wide,
            rest[:, D:].T,
            rest[:, :D].T,
        )
        for some, wide, rest in (
            (pieces[:4], pieces[8], pieces[9]),
            (pieces[6:8], pieces[4], pieces[5]),
        )
    ]
    small_grads = small.reshape(-1)[: LAYERS * (vec + 2 * D)].reshape(LAYERS, vec + 2 * D)
    grad_in_all = jnp.stack([p[0] for p in shards]).reshape(w_in.shape)
    grad_gu_all = jnp.stack([p[1] for p in shards]).reshape(w_gu.shape)
    grad_out_all = jnp.stack([p[2] for p in shards]).reshape(w_out.shape)
    grad_down_all = jnp.stack([p[3] for p in shards]).reshape(w_down.shape)
    vector_total = small_grads[:, :vec].reshape(vectors.shape)
    gain_total = small_grads[:, vec:].reshape(norm_gains.shape)
    up_in = adamw(w_in, first_in, second_in, grad_in_all, rate_matrix, decay_rate)
    up_out = adamw(w_out, first_out, second_out, grad_out_all, rate_matrix, decay_rate)
    up_gu = adamw(w_gu, first_gu, second_gu, grad_gu_all, rate_matrix, decay_rate)
    up_down = adamw(w_down, first_down, second_down, grad_down_all, rate_matrix, decay_rate)
    up_vec = adamw(vectors, first_vectors, second_vectors, vector_total, rate_vector, 0.0)
    up_gain = adamw(norm_gains, first_gains, second_gains, gain_total, rate_vector, 0.0)
    return (
        state,
        grad_state,
        up_in[0],
        up_in[1],
        up_in[2],
        up_out[0],
        up_out[1],
        up_out[2],
        up_gu[0],
        up_gu[1],
        up_gu[2],
        up_down[0],
        up_down[1],
        up_down[2],
        up_vec[0],
        up_vec[1],
        up_vec[2],
        up_gain[0],
        up_gain[1],
        up_gain[2],
    )


def solution(mesh):
    torus = Mesh(
        mesh.devices.reshape(mesh.shape["fsdp"], 4, 4, mesh.shape["tp"]),
        ("fsdp", "ctx_0", "ctx_1", "tp"),
    )
    in_specs = (
        P(FSDP_CTX, None),
        P(FSDP_CTX, None),
        P("fsdp", None),
        P(None, FSDP_CTX, "tp", None),
        P(None, "tp", None, FSDP_CTX),
        P(None, FSDP_CTX, "tp", None),
        P(None, "tp", None, FSDP_CTX),
        P(None, "tp", None),
        P(),
        P(None, FSDP_CTX, "tp", None),
        P(None, "tp", None, FSDP_CTX),
        P(None, FSDP_CTX, "tp", None),
        P(None, "tp", None, FSDP_CTX),
        P(None, "tp", None),
        P(),
        P(None, FSDP_CTX, "tp", None),
        P(None, "tp", None, FSDP_CTX),
        P(None, FSDP_CTX, "tp", None),
        P(None, "tp", None, FSDP_CTX),
        P(None, "tp", None),
        P(),
    )
    out_specs = (
        P(FSDP_CTX, None),
        P(FSDP_CTX, None),
        P(None, FSDP_CTX, "tp", None),
        P(None, FSDP_CTX, "tp", None),
        P(None, FSDP_CTX, "tp", None),
        P(None, "tp", None, FSDP_CTX),
        P(None, "tp", None, FSDP_CTX),
        P(None, "tp", None, FSDP_CTX),
        P(None, FSDP_CTX, "tp", None),
        P(None, FSDP_CTX, "tp", None),
        P(None, FSDP_CTX, "tp", None),
        P(None, "tp", None, FSDP_CTX),
        P(None, "tp", None, FSDP_CTX),
        P(None, "tp", None, FSDP_CTX),
        P(None, "tp", None),
        P(None, "tp", None),
        P(None, "tp", None),
        P(),
        P(),
        P(),
    )
    return jax.shard_map(
        per_device, mesh=torus, in_specs=in_specs, out_specs=out_specs, check_vma=False
    )
```

```python
import functools

import jax
import jax.numpy as jnp
from jax import lax
from jax.experimental import pallas as pl
from jax.experimental.pallas import tpu as pltpu
from jax.sharding import Mesh
from jax.sharding import PartitionSpec as P

HEADS = 8
KV_HEADS = 2
HD = 64
MAMBA_HEADS = 24
MAMBA_HEAD_SIZE = 64
MAMBA_STATE_SIZE = 128
CONV = 4
LAYERS = 2
STEP = 10
DSSM = 1536
FSDP_CTX = ("fsdp", "ctx_0", "ctx_1")
CTX = ("ctx_0", "ctx_1")


highest = lax.Precision.HIGHEST
state_precision = lax.Precision.DEFAULT
D = 1024
IN_COLS = 2060
IN_PAD = 2176
AXES = ("fsdp", "ctx_0", "ctx_1")
SIDE = 4
ROWS = 16
STREAMS = (
    (0, 0, 384, (0, 1, 2), 1),
    (0, 384, 384, (0, 1, 2), -1),
    (0, 768, 384, (1, 2, 0), 1),
    (0, 1152, 384, (1, 2, 0), -1),
    (0, 1536, 384, (2, 0, 1), 1),
    (0, 1920, 256, (2, 0, 1), -1),
)
GRAD_STREAMS = (
    (0, 0, 896, (0, 1, 2), 1),
    (0, 896, 768, (0, 1, 2), -1),
    (0, 1664, 512, (1, 2, 0), 1),
    (1, 768, 256, (1, 2, 0), -1),
    (1, 0, 384, (2, 0, 1), 1),
    (1, 384, 384, (2, 0, 1), -1),
    (2, 0, 2048, (1, 2), 1),
    (2, 2048, 2048, (1, 2), -1),
    (3, 0, 1152, (1, 2), 1),
    (3, 1152, 1024, (2, 1), -1),
    (4, 0, 1536, (2, 1), 1),
    (4, 1536, 1536, (2, 1), -1),
)
GRAD_COUNT = len(GRAD_STREAMS)
FULL_COUNT = 6
KEY_BLOCK = 512
norm_eps = 1e-05
rope_base = 100000000000.0
masked_value = -1e30
beta_one = 0.9
beta_two = 0.95
adam_eps = 1e-08
decay_rate = 0.1
rate_matrix = 0.05
rate_vector = 0.5


def ring_places():
    return tuple(lax.axis_index(a) for a in AXES)


def ring_step(places, axis, by):
    return {AXES[axis]: lax.rem(places[axis] + (by + SIDE), SIDE)}


def greet_neighbours(places):
    barrier = pltpu.get_barrier_semaphore()
    for axis in range(3):
        for by in (1, -1):
            pl.semaphore_signal(
                barrier,
                inc=1,
                device_id=ring_step(places, axis, by),
                device_id_type=pl.DeviceIdType.MESH,
            )
    pl.semaphore_wait(barrier, 6)


def remote(src, dst, send, recv, device):
    return pltpu.make_async_remote_copy(
        src_ref=src,
        dst_ref=dst,
        send_sem=send,
        recv_sem=recv,
        device_id=device,
        device_id_type=pl.DeviceIdType.MESH,
    )


def gather_kernel(shard, full, send, recv, own_sem):
    places = ring_places()
    greet_neighbours(places)
    own = pltpu.make_async_copy(shard, full.at[places[0], places[1], places[2]], own_sem)
    own.start()
    started = []

    def region(number, stage, place):
        _, first, width, order, _ = STREAMS[number]
        order = order[::-1]
        index = list(places)
        for axis in order[:stage]:
            index[axis] = slice(None)
        index[order[stage]] = place
        return full.at[(*index, slice(None), pl.ds(first, width))]

    def launch(number, stage, kind):
        _, first, width, order, way = STREAMS[number]
        axis = order[::-1][stage]
        here = places[axis]
        if kind == 2:
            source = target = region(number, stage, lax.rem(here + (SIDE - way), SIDE))
        else:
            source = target = region(number, stage, here)
            if stage == 0:
                source = shard.at[:, pl.ds(first, width)]
        copy = remote(
            source,
            target,
            send.at[number, stage, kind],
            recv.at[number, stage, kind],
            ring_step(places, axis, -way if kind == 1 else way),
        )
        copy.start()
        started.append(copy)
        return copy

    for stage in range(3):
        if stage == 1:
            own.wait()
        first, back = [], []
        for n in range(6):
            first.append(launch(n, stage, 0))
            back.append(launch(n, stage, 1))
        onward = []
        for n in range(6):
            first[n].wait_recv()
            onward.append(launch(n, stage, 2))
        for n in range(6):
            back[n].wait_recv()
            onward[n].wait_recv()
    for copy in started:
        copy.wait_send()


def gather_weights(part):
    out = pl.pallas_call(
        gather_kernel,
        out_shape=jax.ShapeDtypeStruct((4, 4, 4, *part.shape), part.dtype),
        in_specs=[pl.BlockSpec(memory_space=pl.ANY)],
        out_specs=pl.BlockSpec(memory_space=pl.ANY),
        scratch_shapes=[
            pltpu.SemaphoreType.DMA((6, 3, 3)),
            pltpu.SemaphoreType.DMA((6, 3, 3)),
            pltpu.SemaphoreType.DMA,
        ],
        compiler_params=pltpu.CompilerParams(collective_id=0, has_side_effects=True),
        cost_estimate=pl.CostEstimate(flops=0, bytes_accessed=80000000, transcendentals=0),
        name="gather_weights",
    )(part)
    return out.reshape(D, part.shape[-1])


def scatter_kernel(*refs):
    count = GRAD_COUNT
    grads, small = refs[:5], refs[5]
    refs = refs[6:]
    outs, small_out = refs[:count], refs[count]
    refs = refs[count + 1 :]
    ahead, mine = refs[:count], refs[count : 2 * count]
    refs = refs[2 * count :]
    arrived = (refs[:count], refs[count : 2 * count], refs[2 * count : 2 * count + FULL_COUNT])
    small_in, send, recv, own_sem, small_send, small_recv = refs[2 * count + FULL_COUNT :]
    places = ring_places()
    greet_neighbours(places)
    started = []

    def near(axis, by):
        return lax.rem(places[axis] + (by + SIDE), SIDE)

    def block(number, stage, place):
        at, first, width, order, _ = GRAD_STREAMS[number]
        axis = order[stage]
        dims = sorted(order)
        if stage == 0:
            index = [slice(None)] * len(dims)
            index[dims.index(axis)] = place
            return grads[at].at[(*index, slice(None), pl.ds(first, width))]
        left = [a for a in dims if a != order[0]]
        index = [slice(None)] * len(left)
        for done in order[1:stage]:
            index[left.index(done)] = places[done]
        index[left.index(axis)] = place
        return mine[number].at[tuple(index)]

    def launch(number, stage, kind, source):
        axis, way = GRAD_STREAMS[number][3][stage], GRAD_STREAMS[number][4]
        copy = remote(
            source,
            arrived[stage][number].at[kind],
            send.at[number, stage, kind],
            recv.at[number, stage, kind],
            ring_step(places, axis, -way if kind == 2 else way),
        )
        copy.start()
        started.append(copy)
        return copy

    def add_into(target, source, lead):
        def one(total, part):
            total[...] = total[...] + part[...]

        if lead == 2:

            def body(k, carry):
                one(target.at[k // 4, k % 4], source.at[k // 4, k % 4])
                return carry

            lax.fori_loop(0, 16, body, 0)
        elif lead == 1:

            def body(k, carry):
                one(target.at[k], source.at[k])
                return carry

            lax.fori_loop(0, 4, body, 0)
        else:
            one(target, source)

    def small_exchange(step):
        axis, odd = step // 2, step % 2
        here = places[axis]
        partner = 3 - here if odd else here + 1 - 2 * lax.rem(here, 2)
        copy = remote(
            small_out,
            small_in.at[step],
            small_send.at[step],
            small_recv.at[step],
            {AXES[axis]: partner},
        )
        copy.start()
        return copy

    def small_finish(copy, step):
        copy.wait_send()
        copy.wait_recv()
        small_out[...] = small_out[...] + small_in[step]

    local = {}
    small_out[...] = small[...]
    for stage in range(3):
        active = [n for n in range(count) if len(GRAD_STREAMS[n][3]) > stage]
        active.sort(key=lambda n: len(GRAD_STREAMS[n][3]))
        first, back, onward = {}, {}, {}
        for n in active:
            axis, way = GRAD_STREAMS[n][3][stage], GRAD_STREAMS[n][4]
            first[n] = launch(n, stage, 0, block(n, stage, near(axis, 2)))
        for n in active:
            axis, way = GRAD_STREAMS[n][3][stage], GRAD_STREAMS[n][4]
            if stage == 0:
                pair = (
                    pltpu.make_async_copy(block(n, 0, near(axis, way)), ahead[n], own_sem.at[n, 0]),
                    pltpu.make_async_copy(block(n, 0, places[axis]), mine[n], own_sem.at[n, 1]),
                )
                for copy in pair:
                    copy.start()
                local[n] = pair
            back[n] = launch(n, stage, 2, block(n, stage, near(axis, -way)))
        step = small_exchange(2 * stage)
        for n in active:
            axis, way = GRAD_STREAMS[n][3][stage], GRAD_STREAMS[n][4]
            if stage == 0:
                local[n][0].wait()
                local[n][1].wait()
                target = ahead[n]
            else:
                target = block(n, stage, near(axis, way))
            first[n].wait_recv()
            add_into(target, arrived[stage][n].at[0], len(GRAD_STREAMS[n][3]) - 1 - stage)
            onward[n] = launch(n, stage, 1, target)
        small_finish(step, 2 * stage)
        step = small_exchange(2 * stage + 1)
        for n in active:
            order = GRAD_STREAMS[n][3]
            lead = len(order) - 1 - stage
            target = mine[n] if stage == 0 else block(n, stage, places[order[stage]])
            back[n].wait_recv()
            if lead:
                add_into(target, arrived[stage][n].at[2], lead)
            onward[n].wait_recv()
            if lead:
                add_into(target, arrived[stage][n].at[1], lead)
            else:
                outs[n][...] = target[...].astype(jnp.float32) + (
                    arrived[stage][n][1].astype(jnp.float32)
                    + arrived[stage][n][2].astype(jnp.float32)
                )
        small_finish(step, 2 * stage + 1)
    for copy in started:
        copy.wait_send()


def scatter_gradients(full, quarters, small):
    vmem = pl.BlockSpec(memory_space=pltpu.VMEM)

    def held(*lead_less):
        return [
            pltpu.VMEM((*lead, *(4,) * (len(s[3]) - less), ROWS, s[2]), jnp.bfloat16)
            for lead, less in lead_less
            for s in GRAD_STREAMS
            if len(s[3]) >= less
        ]

    scratch = held(((), 1), ((), 1), ((3,), 1), ((3,), 2), ((3,), 3))
    scratch += [
        pltpu.VMEM((6, *small.shape), jnp.float32),
        pltpu.SemaphoreType.DMA((GRAD_COUNT, 3, 3)),
        pltpu.SemaphoreType.DMA((GRAD_COUNT, 3, 3)),
        pltpu.SemaphoreType.DMA((GRAD_COUNT, 2)),
        pltpu.SemaphoreType.DMA((6,)),
        pltpu.SemaphoreType.DMA((6,)),
    ]
    shapes = [jax.ShapeDtypeStruct((ROWS, s[2]), jnp.float32) for s in GRAD_STREAMS]
    shapes.append(jax.ShapeDtypeStruct(small.shape, jnp.float32))
    views = [f.reshape(4, 4, 4, ROWS, f.shape[-1]) for f in full]
    views += [q.reshape(4, 4, ROWS, q.shape[-1]) for q in quarters]
    return pl.pallas_call(
        scatter_kernel,
        out_shape=shapes,
        in_specs=[pl.BlockSpec(memory_space=pl.ANY)] * 5 + [vmem],
        out_specs=[vmem] * (GRAD_COUNT + 1),
        scratch_shapes=scratch,
        compiler_params=pltpu.CompilerParams(
            collective_id=1, has_side_effects=True, vmem_limit_bytes=28 * 2**20
        ),
        cost_estimate=pl.CostEstimate(flops=0, bytes_accessed=100000000, transcendentals=0),
        name="scatter_gradients",
    )(*views, small)


def other_core(value):
    return lax.ppermute(value, "tp", [(0, 1), (1, 0)])


def state_scan(reverse, work, parts, out, got, sums, rows, inside, decays, reply, back, send, recv):
    here, outer = lax.axis_index("ctx_1"), lax.axis_index("ctx_0")
    head = parts.shape[2] - 16
    barrier = pltpu.get_barrier_semaphore()
    for axis, place in (("ctx_1", here), ("ctx_0", outer)):
        for by in range(1, SIDE):
            pl.semaphore_signal(
                barrier,
                inc=1,
                device_id={axis: lax.rem(place + by, SIDE)},
                device_id_type=pl.DeviceIdType.MESH,
            )
    pl.semaphore_wait(barrier, 6)
    started = []

    def spread(stage, axis, place, source, target):
        copies = []
        for by in (2, 1, 3):
            other = lax.rem(place + by, SIDE)
            copy = remote(
                source(other),
                target.at[place],
                send.at[stage, by - 1],
                recv.at[stage, by - 1],
                {axis: other},
            )
            copy.start()
            copies.append(copy)
        started.extend(copies)
        return copies

    def opened(ref, k):
        wide = ref[k].astype(jnp.float32)
        return wide[:, head : head + 1, :], wide[:, :head, :]

    order = range(SIDE - 1, -1, -1) if reverse else range(SIDE)
    copies = spread(0, "ctx_1", here, lambda other: parts.at[other], got)
    got[here] = parts[here]
    work(0)
    for copy in copies:
        copy.wait_recv()
    decay = state = None
    for k in order:
        own_decay, own_state = opened(got, k)
        if decay is None:
            decay, state = own_decay, own_state
        else:
            decays[k] = decay
            inside[k] = state
            decay, state = decay * own_decay, own_decay * state + own_state
    sums[:, :head, :] = state.astype(jnp.bfloat16)
    sums[:, head:, :] = jnp.broadcast_to(decay, (decay.shape[0], 16, decay.shape[2])).astype(
        jnp.bfloat16
    )
    copies = spread(1, "ctx_0", outer, lambda other: sums, rows)
    rows[outer] = sums[...]
    work(1)
    for copy in copies:
        copy.wait_recv()
    before = jnp.zeros(inside.shape[1:], jnp.float32)
    state = None
    for k in order:
        if state is not None:
            before = jnp.where(outer == k, state, before)
        own_decay, own_state = opened(rows, k)
        state = own_state if state is None else own_decay * state + own_state
    for k in order:
        if k == order[0]:
            reply[k] = before.astype(jnp.bfloat16)
        else:
            reply[k] = (decays[k] * before + inside[k]).astype(jnp.bfloat16)
    copies = spread(2, "ctx_1", here, lambda other: reply.at[other], back)
    back[here] = reply[here]
    work(2)
    for copy in copies:
        copy.wait_recv()
    out[...] = back[...].astype(jnp.float32)
    for copy in started:
        copy.wait_send()


def turned(value):
    return value.astype(jnp.float32).T.astype(value.dtype)


def seen_keys(block, lowest, highest_key):
    at = block * KEY_BLOCK + lax.broadcasted_iota(jnp.int32, (KEY_BLOCK, lowest.shape[1]), 0)
    return (at >= lowest[...]) & (at <= highest_key[...])


def key_block(kv, block):
    return kv[pl.ds(pl.multiple_of(block * KEY_BLOCK, KEY_BLOCK), KEY_BLOCK), :]


def shared_out(total, body):
    bounds = (0, total * 3 // 8, total * 5 // 8, total)

    def work(stage):
        lax.fori_loop(bounds[stage], bounds[stage + 1], body, 0)

    return work


def scan_attend_kernel(
    parts, kv, queries, lowest, highest_key, out, attended, log_total, queries_t, top, total, mix, *rest
):
    scale = HD ** (-0.5)
    queries_t[...] = turned(queries[...])
    top[...] = jnp.full_like(top, masked_value)
    total[...] = jnp.zeros_like(total)
    mix[...] = jnp.zeros_like(mix)

    def body(block, carry):
        pair = key_block(kv, block)
        keys, values_t = pair[:, :HD], turned(pair)[HD:, :]
        seen = seen_keys(block, lowest, highest_key)
        for g in range(queries.shape[1] // HD):
            head = slice(g * HD, (g + 1) * HD)
            raw = jnp.dot(keys, queries_t[head, :], preferred_element_type=jnp.float32)
            logits = jnp.where(seen, raw * scale, masked_value)
            old = top[g : g + 1, :]
            new = jnp.maximum(old, jnp.max(logits, axis=0, keepdims=True))
            shrink = jnp.exp(old - new)
            weight = jnp.exp(logits - new)
            top[g : g + 1, :] = new
            total[g : g + 1, :] = total[g : g + 1, :] * shrink + jnp.sum(
                weight, axis=0, keepdims=True
            )
            mix[head, :] = mix[head, :] * shrink + jnp.dot(
                values_t, weight.astype(jnp.bfloat16), preferred_element_type=jnp.float32
            )
        return carry

    state_scan(False, shared_out(kv.shape[0] // KEY_BLOCK, body), parts, out, *rest)
    log_total[...] = top[...] + jnp.log(total[...])
    for g in range(queries.shape[1] // HD):
        head = slice(g * HD, (g + 1) * HD)
        mix[head, :] = mix[head, :] / total[g : g + 1, :]
    attended[...] = mix[...].T


def scan_attend_back_kernel(
    parts,
    kv,
    queries,
    d_att,
    attended,
    log_total,
    lowest,
    highest_key,
    out,
    d_kv,
    d_query,
    queries_t,
    d_att_t,
    delta,
    d_query_t,
    *rest,
):
    scale = HD ** (-0.5)
    groups = queries.shape[1] // HD
    queries_t[...] = turned(queries[...])
    d_att_t[...] = turned(d_att[...])
    product = d_att_t[...].astype(jnp.float32) * attended[...].T
    for g in range(groups):
        delta[g : g + 1, :] = jnp.sum(product[g * HD : (g + 1) * HD, :], axis=0, keepdims=True)
    d_query_t[...] = jnp.zeros_like(d_query_t)

    def body(block, carry):
        pair = key_block(kv, block)
        keys, values, keys_t = pair[:, :HD], pair[:, HD:], turned(pair)[:HD, :]
        seen = seen_keys(block, lowest, highest_key)
        d_key = jnp.zeros((KEY_BLOCK, HD), jnp.float32)
        d_value = jnp.zeros((KEY_BLOCK, HD), jnp.float32)
        for g in range(groups):
            head = slice(g * HD, (g + 1) * HD)
            raw = jnp.dot(keys, queries_t[head, :], preferred_element_type=jnp.float32)
            logits = jnp.where(seen, raw * scale, masked_value)
            prob = jnp.exp(logits - log_total[g : g + 1, :])
            d_prob = jnp.dot(values, d_att_t[head, :], preferred_element_type=jnp.float32)
            d_raw = (prob * (d_prob - delta[g : g + 1, :]) * scale).astype(jnp.bfloat16)
            d_value += jnp.dot(
                prob.astype(jnp.bfloat16), d_att[:, head], preferred_element_type=jnp.float32
            )
            d_key += jnp.dot(d_raw, queries[:, head], preferred_element_type=jnp.float32)
            d_query_t[head, :] += jnp.dot(keys_t, d_raw, preferred_element_type=jnp.float32)
        both = jnp.concatenate([d_key, d_value], axis=1).astype(jnp.bfloat16)
        d_kv[pl.ds(pl.multiple_of(block * KEY_BLOCK, KEY_BLOCK), KEY_BLOCK), :] = both
        return carry

    state_scan(True, shared_out(kv.shape[0] // KEY_BLOCK, body), parts, out, *rest)
    d_query[...] = d_query_t[...].T


def entering(decay, state, reverse, shapes, scratch, *arrays):
    heads = decay.shape[0]
    chunk = heads // SIDE
    size, width = state.shape[1:]
    rows = jnp.broadcast_to(decay[:, None, None], (heads, 16, width))
    message = jnp.concatenate([state, rows], axis=1).astype(jnp.bfloat16)
    message = message.reshape(SIDE, chunk, size + 16, width)
    vmem = pl.BlockSpec(memory_space=pltpu.VMEM)
    out, *others = pl.pallas_call(
        scan_attend_back_kernel if reverse else scan_attend_kernel,
        out_shape=[jax.ShapeDtypeStruct((SIDE, chunk, size, width), jnp.float32), *shapes],
        in_specs=[vmem] * (1 + len(arrays)),
        out_specs=[vmem] * (1 + len(shapes)),
        scratch_shapes=[
            *scratch,
            pltpu.VMEM((SIDE, chunk, size + 16, width), jnp.bfloat16),
            pltpu.VMEM((chunk, size + 16, width), jnp.bfloat16),
            pltpu.VMEM((SIDE, chunk, size + 16, width), jnp.bfloat16),
            pltpu.VMEM((SIDE, chunk, size, width), jnp.float32),
            pltpu.VMEM((SIDE, chunk, 1, width), jnp.float32),
            pltpu.VMEM((SIDE, chunk, size, width), jnp.bfloat16),
            pltpu.VMEM((SIDE, chunk, size, width), jnp.bfloat16),
            pltpu.SemaphoreType.DMA((3, 3)),
            pltpu.SemaphoreType.DMA((3, 3)),
        ],
        compiler_params=pltpu.CompilerParams(
            collective_id=3 if reverse else 2,
            has_side_effects=True,
            vmem_limit_bytes=14 * 2**20,
        ),
        cost_estimate=pl.CostEstimate(
            flops=3000000000, bytes_accessed=40000000, transcendentals=4000000
        ),
        name="scan_attend_back" if reverse else "scan_attend",
    )(message, *arrays)
    return out.reshape(heads, size, width), *others


def from_everyone(value, axis):
    copies = jnp.broadcast_to(value, (lax.axis_size(axis), *value.shape))
    return lax.all_to_all(copies, axis, split_axis=0, concat_axis=0, tiled=True)


def joined_along(pieces, dim):
    shape = list(pieces.shape[1:])
    shape[dim] *= pieces.shape[0]
    return jnp.moveaxis(pieces, 0, dim).reshape(shape)


def gathered_copies(value, axis, dim):
    pieces = from_everyone(value, axis)
    return joined_along(pieces, dim)


def passed_along(value, axis, by):
    count = lax.axis_size(axis)
    pairs = [(i, i + by) for i in range(count) if 0 <= i + by < count]
    return lax.ppermute(value, axis, pairs)


def split_up(value, dim, count):
    before, after = (value.shape[:dim], value.shape[dim + 1 :])
    return jnp.moveaxis(value.reshape(*before, count, -1, *after), dim, 0)


def summed_on_arrival(value, axis, dim):
    pieces = split_up(value, dim, lax.axis_size(axis))
    arrived = lax.all_to_all(pieces, axis, split_axis=0, concat_axis=0, tiled=True)
    return arrived.astype(jnp.float32).sum(axis=0)


def rms_norm(value, gain):
    return value * lax.rsqrt(jnp.mean(value * value, axis=-1, keepdims=True) + norm_eps) * gain


def silu_slope(value):
    sigma = jax.nn.sigmoid(value)
    return sigma * (1.0 + value * (1.0 - sigma))


def doc_layout(doc_row, start_row, item_count):
    ends = jnp.cumsum(doc_row)
    starts = ends - doc_row
    token_index = start_row + jnp.arange(item_count, dtype=jnp.int32)
    segment = jnp.sum((token_index[:, None] >= ends[None, :]).astype(jnp.int32), axis=1)
    picked = segment[:, None] == jnp.arange(doc_row.shape[0], dtype=jnp.int32)[None, :]
    begin = jnp.sum(jnp.where(picked, starts[None, :], 0), axis=1)
    return (segment, token_index - begin)


def rope_tables(position):
    freq = rope_base ** (-2.0 * jnp.arange(HD // 2, dtype=jnp.float32) / HD)
    angle = position.astype(jnp.float32)[:, None] * freq[None, :]
    return (jnp.cos(angle), jnp.sin(angle))


def rotate(value, cosine, sine):
    shaped = value.reshape(value.shape[0], -1, 2, HD // 2)
    first_half = shaped[:, :, 0]
    second_half = shaped[:, :, 1]
    cos_part = cosine[:, None, :]
    sin_part = sine[:, None, :]
    turned = jnp.stack(
        [
            first_half * cos_part - second_half * sin_part,
            second_half * cos_part + first_half * sin_part,
        ],
        axis=2,
    )
    return turned.reshape(value.shape)


def conv_act(extended, conv_taps, conv_bias, seg_ext):
    item_count = extended.shape[0] - (CONV - 1)
    own_seg = seg_ext[CONV - 1 :]
    total = conv_bias[None, :] + conv_taps[CONV - 1][None, :] * extended[CONV - 1 :]
    for back in range(1, CONV):
        begin = CONV - 1 - back
        same = seg_ext[begin : begin + item_count] == own_seg
        total = total + conv_taps[CONV - 1 - back][None, :] * jnp.where(
            same[:, None], extended[begin : begin + item_count], 0.0
        )
    return jax.nn.silu(total)


def decay_terms(drive_input, dt_bias, a_log):
    dt_step = jax.nn.softplus(drive_input + dt_bias)
    order = jnp.arange(dt_step.shape[0], dtype=jnp.int32)
    upto = (order[None, :] <= order[:, None]).astype(jnp.float32)
    return (dt_step, jnp.dot(upto, -dt_step * jnp.exp(a_log), precision=highest))


def head_columns(heads):
    column = jnp.arange(heads * MAMBA_HEAD_SIZE, dtype=jnp.int32) // MAMBA_HEAD_SIZE
    return (column[None, :] == jnp.arange(heads, dtype=jnp.int32)[:, None]).astype(jnp.float32)


def spread_heads(value, columns):
    return jnp.dot(value, columns, precision=highest, preferred_element_type=jnp.float32)


def fold_heads(value, columns):
    return lax.dot_general(
        value,
        columns,
        (((1,), (1,)), ((), ())),
        precision=highest,
        preferred_element_type=jnp.float32,
    )


def cross(left, right):
    return lax.dot_general(
        left, right, (((1,), (1,)), ((), ())), preferred_element_type=jnp.float32
    )


def same_document(seg_col, seg_row, flipped):
    count = seg_col.shape[0]
    down = lax.broadcasted_iota(jnp.int32, (count, count), 0)
    over = lax.broadcasted_iota(jnp.int32, (count, count), 1)
    earlier = (down <= over) if flipped else (over <= down)
    return earlier & (seg_col == seg_row)


def state_forth_kernel(
    x, both, log_col, log_row, dt_step, entry, skip, seg_col, seg_row, state, columns, out
):
    b_mat, c_mat = both[:, :MAMBA_STATE_SIZE], both[:, MAMBA_STATE_SIZE:]
    seen = same_document(seg_col[...], seg_row[...], False)
    inner_prod = cross(c_mat, b_mat)
    spreader = columns[...]
    driven = (x[...] * spread_heads(dt_step[...], spreader)).astype(jnp.bfloat16)
    carried = cross(c_mat, state[...].astype(jnp.bfloat16))
    base = carried * spread_heads(entry[...], spreader) + skip[...] * x[...]
    for pair in range(log_row.shape[0] // 2):
        halves = []
        for h in (2 * pair, 2 * pair + 1):
            fade = log_col[:, h : h + 1] - log_row[h : h + 1, :]
            mixing = jnp.exp(jnp.where(seen, fade, masked_value)) * inner_prod
            at = h * MAMBA_HEAD_SIZE
            halves.append(
                jnp.dot(
                    mixing.astype(jnp.bfloat16),
                    driven[:, at : at + MAMBA_HEAD_SIZE],
                    preferred_element_type=jnp.float32,
                )
            )
        at = 2 * pair * MAMBA_HEAD_SIZE
        till = at + 2 * MAMBA_HEAD_SIZE
        out[:, at:till] = base[:, at:till] + jnp.concatenate(halves, axis=1)


def state_back_kernel(
    x,
    y,
    d_y,
    both,
    log_col,
    log_row,
    dt_step,
    fading,
    entry,
    skip,
    seg_col,
    seg_row,
    state,
    later,
    columns,
    d_x,
    d_both,
    by_dt,
    by_log,
    by_skip,
):
    b_mat, c_mat = both[:, :MAMBA_STATE_SIZE], both[:, MAMBA_STATE_SIZE:]
    seen = same_document(seg_col[...], seg_row[...], True)
    inner_prod = cross(b_mat, c_mat)
    spreader = columns[...]
    x_all, d_all = x[...], d_y[...]
    x_b, d_b = x_all.astype(jnp.bfloat16), d_all.astype(jnp.bfloat16)
    later_b, state_b = later[...].astype(jnp.bfloat16), state[...].astype(jnp.bfloat16)
    d_inner_prod = jnp.zeros_like(inner_prod)
    parts = []
    for h in range(log_row.shape[0]):
        at = h * MAMBA_HEAD_SIZE
        fade = log_row[h : h + 1, :] - log_col[:, h : h + 1]
        kernel = jnp.exp(jnp.where(seen, fade, masked_value))
        d_mixing = cross(x_b[:, at : at + MAMBA_HEAD_SIZE], d_b[:, at : at + MAMBA_HEAD_SIZE])
        d_inner_prod += kernel * d_mixing * dt_step[:, h : h + 1]
        parts.append(
            jnp.dot(
                (kernel * inner_prod).astype(jnp.bfloat16),
                d_b[:, at : at + MAMBA_HEAD_SIZE],
                preferred_element_type=jnp.float32,
            )
        )
    fade_all = spread_heads(fading[...], spreader)
    dt_all = spread_heads(dt_step[...], spreader)
    pulled = jnp.concatenate(parts, axis=1) + fade_all * cross(b_mat, later_b)
    d_x[...] = dt_all * pulled + skip[...] * d_all
    by_dt[...] = fold_heads(x_all * pulled, spreader)
    by_log[...] = fold_heads(d_all * (y[...] - skip[...] * x_all), spreader)
    by_skip[...] = fold_heads(d_all * x_all, spreader)
    d_inner_b = d_inner_prod.astype(jnp.bfloat16)
    d_b_mat = jnp.dot(d_inner_b, c_mat, preferred_element_type=jnp.float32) + jnp.dot(
        (x_all * fade_all * dt_all).astype(jnp.bfloat16),
        later_b,
        preferred_element_type=jnp.float32,
    )
    d_c_mat = lax.dot_general(
        d_inner_b, b_mat, (((0,), (0,)), ((), ())), preferred_element_type=jnp.float32
    ) + jnp.dot(
        (d_all * spread_heads(entry[...], spreader)).astype(jnp.bfloat16),
        state_b,
        preferred_element_type=jnp.float32,
    )
    d_both[...] = jnp.concatenate([d_b_mat, d_c_mat], axis=1)


def state_call(kernel, shapes, name, *arrays):
    vmem = pl.BlockSpec(memory_space=pltpu.VMEM)
    return pl.pallas_call(
        kernel,
        out_shape=shapes,
        in_specs=[vmem] * len(arrays),
        out_specs=jax.tree.map(lambda s: vmem, shapes),
        compiler_params=pltpu.CompilerParams(vmem_limit_bytes=16 * 2**20),
        cost_estimate=pl.CostEstimate(
            flops=2000000000, bytes_accessed=8000000, transcendentals=800000
        ),
        name=name,
    )(*arrays)


def decay_parts(drive_input, dt_bias, a_log, segment, position):
    dt_step, log_cum = decay_terms(drive_input, dt_bias, a_log)
    count = log_cum.shape[0]
    last = log_cum[count - 1]
    in_last = (segment == segment[count - 1]).astype(jnp.float32)
    fading = jnp.exp(last[None, :] - log_cum) * in_last[:, None]
    carry_on = ((segment == segment[0]) & (position[0] != 0)).astype(jnp.float32)
    entry = jnp.exp(log_cum) * carry_on[:, None]
    return dt_step, log_cum, fading, entry, carry_on[count - 1] * jnp.exp(last)


def split_vector(vector, widths):
    q_width, k_width, s_width, b_width, h_width = widths
    channels = s_width + b_width
    conv_taps = vector[: CONV * channels].reshape(CONV, channels)
    offset = CONV * channels
    conv_bias = vector[offset : offset + channels]
    offset = offset + channels
    gated_gain = vector[offset : offset + s_width]
    offset = offset + s_width
    return (
        conv_taps,
        conv_bias,
        gated_gain,
        vector[offset : offset + h_width],
        vector[offset + h_width : offset + 2 * h_width],
        vector[offset + 2 * h_width : offset + 3 * h_width],
    )


def feature_sum(value):
    own = value.astype(jnp.bfloat16)
    return own.astype(jnp.float32) + other_core(own).astype(jnp.float32)


def norm_sum(value):
    return value + other_core(value)


def local_matrices(w_in, w_out, w_gu, w_down, layer_at):
    return (
        jnp.pad(w_in[layer_at, :, 0, :], ((0, 0), (0, IN_PAD - IN_COLS))).astype(jnp.bfloat16),
        w_gu[layer_at, :, 0, :].astype(jnp.bfloat16),
        w_out[layer_at, 0].T.astype(jnp.bfloat16),
        w_down[layer_at, 0].T.astype(jnp.bfloat16),
    )


def gathered_columns(parts):
    filled = lax.all_gather(jnp.concatenate(parts, axis=1), FSDP_CTX, axis=0, tiled=True)
    bounds, at = [], 0
    for part in parts[:-1]:
        at += part.shape[1]
        bounds.append(at)
    return jnp.split(filled, bounds, axis=1)


def fetch_layers(w_in, w_out, w_gu, w_down):
    zero, one = (local_matrices(w_in, w_out, w_gu, w_down, k) for k in range(LAYERS))
    sooner = gathered_columns((*zero[1:], one[0]))
    first_in, rest = lax.optimization_barrier((gather_weights(zero[0]), one[1:]))
    later = gathered_columns(rest)
    return (first_in, *sooner[:3]), (sooner[3], *later)


def layer_forward(state, weights, vector, gains, context, widths):
    w_in_b, w_gu_b, w_out_t, w_down_t = weights
    segment, position, seg_ext, cosine, sine, lowest, highest_key = context
    q_width, k_width, s_width, b_width, h_width = widths
    conv_taps, conv_bias, gated_gain, a_log, dt_bias, d_skip = split_vector(vector, widths)
    item_count = state.shape[0]
    at_v = q_width + k_width
    at_z = at_v + k_width
    at_x = at_z + s_width
    at_t = at_x + s_width + b_width
    hidden_b = rms_norm(state, gains[0]).astype(jnp.bfloat16)
    proj = jnp.dot(hidden_b, w_in_b, preferred_element_type=jnp.float32)
    queries_b = rotate(proj[:, :q_width], cosine, sine).astype(jnp.bfloat16)
    pair = jnp.concatenate(
        [rotate(proj[:, q_width:at_v], cosine, sine), proj[:, at_v:at_z]], axis=1
    ).astype(jnp.bfloat16)
    key_values = gathered_copies(pair, CTX, 0)
    mixed_in = proj[:, at_x:at_t]
    halo_rows = passed_along(mixed_in[item_count - (CONV - 1) :], CTX, 1)
    extended = jnp.concatenate([halo_rows, mixed_in], axis=0)
    active = conv_act(extended, conv_taps, conv_bias, seg_ext)
    own_part = active[:, s_width:].astype(jnp.bfloat16)
    other_part = other_core(own_part)
    leads = lax.axis_index("tp") == 0
    both = jnp.concatenate(
        [jnp.where(leads, own_part, other_part), jnp.where(leads, other_part, own_part)], axis=1
    )
    inner_input = active[:, :s_width]
    drive_input = proj[:, at_t : at_t + h_width]
    columns = head_columns(h_width)
    timing = decay_parts(drive_input, dt_bias, a_log, segment, position)
    dt_step, log_cum, fading, entry, decay_own = timing
    weighted = inner_input * spread_heads(fading * dt_step, columns)
    state_own = jnp.einsum("sc,sn->cn", weighted, both[:, :MAMBA_STATE_SIZE].astype(jnp.float32))
    state_own = state_own.reshape(h_width, MAMBA_HEAD_SIZE, MAMBA_STATE_SIZE)
    groups = q_width // HD
    by_query = jax.ShapeDtypeStruct((groups, item_count), jnp.float32)
    state_in, attended, log_total = entering(
        decay_own,
        state_own,
        False,
        [jax.ShapeDtypeStruct((item_count, q_width), jnp.float32), by_query],
        [
            pltpu.VMEM((q_width, item_count), jnp.bfloat16),
            pltpu.VMEM((groups, item_count), jnp.float32),
            pltpu.VMEM((groups, item_count), jnp.float32),
            pltpu.VMEM((q_width, item_count), jnp.float32),
        ],
        key_values,
        queries_b,
        lowest,
        highest_key,
    )
    ssm = state_call(
        state_forth_kernel,
        jax.ShapeDtypeStruct(inner_input.shape, jnp.float32),
        "state_forth",
        inner_input,
        both,
        log_cum,
        log_cum.T,
        dt_step,
        entry,
        spread_heads(d_skip[None, :], columns),
        segment[:, None],
        segment[None, :],
        state_in.reshape(s_width, MAMBA_STATE_SIZE),
        columns,
    )
    gated = ssm * jax.nn.silu(proj[:, at_z:at_x])
    inverse = lax.rsqrt(norm_sum(jnp.sum(gated * gated, axis=1)) / DSSM + norm_eps)[:, None]
    features = jnp.concatenate([attended, gated * inverse * gated_gain], axis=1).astype(
        jnp.bfloat16
    )
    middle = state + feature_sum(
        jnp.einsum("tc,dc->td", features, w_out_t, preferred_element_type=jnp.float32)
    )
    hidden2_b = rms_norm(middle, gains[1]).astype(jnp.bfloat16)
    upgate = jnp.dot(hidden2_b, w_gu_b, preferred_element_type=jnp.float32)
    half_width = upgate.shape[1] // 2
    inner_b = (jax.nn.silu(upgate[:, :half_width]) * upgate[:, half_width:]).astype(jnp.bfloat16)
    final_result = middle + feature_sum(
        jnp.einsum("tf,df->td", inner_b, w_down_t, preferred_element_type=jnp.float32)
    )
    kept = (
        state,
        hidden_b,
        proj,
        queries_b,
        key_values,
        log_total,
        extended,
        active,
        both,
        state_in,
        state_own,
        timing,
        ssm,
        gated,
        inverse,
        features,
        middle,
        hidden2_b,
        upgate,
        inner_b,
        attended,
    )
    return (final_result, kept)


def layer_backward(grad_out, kept, weights, vector, gains, context, widths, waiting):
    w_in_b, w_gu_b, w_out_t, w_down_t = weights
    segment, position, seg_ext, cosine, sine, lowest, highest_key = context
    q_width, k_width, s_width, b_width, h_width = widths
    conv_taps, conv_bias, gated_gain, a_log, dt_bias, d_skip = split_vector(vector, widths)
    (
        state,
        hidden_b,
        proj,
        queries_b,
        key_values,
        log_total,
        extended,
        active,
        both,
        state_in,
        state_own,
        timing,
        ssm,
        gated,
        inverse,
        features,
        middle,
        hidden2_b,
        upgate,
        inner_b,
        attended,
    ) = kept
    item_count = state.shape[0]
    at_v = q_width + k_width
    at_z = at_v + k_width
    at_x = at_z + s_width
    at_t = at_x + s_width + b_width
    grad_b = grad_out.astype(jnp.bfloat16)
    grad_down = jnp.einsum(
        "td,tf->df", grad_b, inner_b, preferred_element_type=jnp.float32
    ).astype(jnp.bfloat16)
    d_inner = jnp.dot(grad_b, w_down_t, preferred_element_type=jnp.float32)
    half_width = upgate.shape[1] // 2
    gate_part = upgate[:, :half_width]
    d_upgate_b = jnp.concatenate(
        [
            d_inner * upgate[:, half_width:] * silu_slope(gate_part),
            d_inner * jax.nn.silu(gate_part),
        ],
        axis=1,
    ).astype(jnp.bfloat16)
    grad_gu = jnp.einsum(
        "td,tf->df", hidden2_b, d_upgate_b, preferred_element_type=jnp.float32
    ).astype(jnp.bfloat16)
    d_hidden2 = feature_sum(
        jnp.einsum("tf,df->td", d_upgate_b, w_gu_b, preferred_element_type=jnp.float32)
    )
    d_middle_norm, d_gain_mlp = jax.vjp(rms_norm, middle, gains[1])[1](d_hidden2)
    d_middle = grad_out + d_middle_norm
    mix_b = d_middle.astype(jnp.bfloat16)
    grad_out_proj = jnp.einsum(
        "td,tc->dc", mix_b, features, preferred_element_type=jnp.float32
    ).astype(jnp.bfloat16)
    wide = [grad_gu, grad_down] + ([grad_out_proj] if waiting is None else [])
    early = lax.psum_scatter(jnp.concatenate(wide, axis=1), "fsdp", tiled=True)
    d_features = jnp.dot(mix_b, w_out_t, preferred_element_type=jnp.float32)
    d_normed = d_features[:, q_width:]
    weighted = d_normed * gated_gain
    d_gated_gain = jnp.sum(d_normed * gated * inverse, axis=0)
    across = norm_sum(jnp.sum(weighted * gated, axis=1))[:, None]
    d_gated = weighted * inverse - gated * inverse**3 * across / DSSM
    gate_z = proj[:, at_z:at_x]
    d_ssm = d_gated * jax.nn.silu(gate_z)
    d_gate_z = d_gated * ssm * silu_slope(gate_z)
    inner_input = active[:, :s_width]
    drive_input = proj[:, at_t : at_t + h_width]

    dt_step, log_cum, fading, entry, decay_own = timing
    columns = head_columns(h_width)
    d_carry = jnp.einsum(
        "tc,tn->cn",
        d_ssm * spread_heads(entry, columns),
        both[:, MAMBA_STATE_SIZE:].astype(jnp.float32),
    ).reshape(state_in.shape)
    later, d_pair_all, d_query = entering(
        decay_own,
        d_carry,
        True,
        [
            jax.ShapeDtypeStruct(key_values.shape, jnp.bfloat16),
            jax.ShapeDtypeStruct((item_count, q_width), jnp.float32),
        ],
        [
            pltpu.VMEM((q_width, item_count), jnp.bfloat16),
            pltpu.VMEM((q_width, item_count), jnp.bfloat16),
            pltpu.VMEM((q_width // HD, item_count), jnp.float32),
            pltpu.VMEM((q_width, item_count), jnp.float32),
        ],
        key_values,
        queries_b,
        d_features[:, :q_width].astype(jnp.bfloat16),
        attended,
        log_total,
        lowest,
        highest_key,
    )
    if waiting is not None:
        d_pair_all, waiting = lax.optimization_barrier((d_pair_all, waiting))
    d_pair = summed_on_arrival(d_pair_all, CTX, 0)
    by_head = jax.ShapeDtypeStruct(dt_step.shape, jnp.float32)
    d_inner_input, d_both, by_dt, by_log, by_skip = state_call(
        state_back_kernel,
        [
            jax.ShapeDtypeStruct(inner_input.shape, jnp.float32),
            jax.ShapeDtypeStruct(both.shape, jnp.float32),
            by_head,
            by_head,
            by_head,
        ],
        "state_back",
        inner_input,
        ssm,
        d_ssm,
        both,
        log_cum,
        log_cum.T,
        dt_step,
        fading,
        entry,
        spread_heads(d_skip[None, :], columns),
        segment[:, None],
        segment[None, :],
        state_in.reshape(s_width, MAMBA_STATE_SIZE),
        later.reshape(s_width, MAMBA_STATE_SIZE),
        columns,
    )
    at_end = jnp.sum(later * (state_own + decay_own[:, None, None] * state_in), axis=(1, 2))
    order = jnp.arange(item_count, dtype=jnp.int32)
    d_log_cum = by_log - dt_step * by_dt
    onward = (order[None, :] >= order[:, None]).astype(jnp.float32)
    d_log_decay = jnp.dot(onward, d_log_cum, precision=highest) + at_end[None, :]
    d_dt = by_dt - jnp.exp(a_log) * d_log_decay
    d_drive = d_dt * jax.nn.sigmoid(drive_input + dt_bias)
    d_a_log = -jnp.sum(d_log_decay * dt_step, axis=0) * jnp.exp(a_log)
    d_dt_bias = jnp.sum(d_drive, axis=0)
    d_skip_grad = jnp.sum(by_skip, axis=0)
    d_both_b = d_both.astype(jnp.bfloat16)
    leads = lax.axis_index("tp") == 0
    kept_part = jnp.where(leads, d_both_b[:, :b_width], d_both_b[:, b_width:])
    sent_part = jnp.where(leads, d_both_b[:, b_width:], d_both_b[:, :b_width])
    d_own = kept_part.astype(jnp.float32) + other_core(sent_part).astype(jnp.float32)

    def conv_part(ext_part, taps_part, bias_part):
        return conv_act(ext_part, taps_part, bias_part, seg_ext)

    conv_pull = jax.vjp(conv_part, extended, conv_taps, conv_bias)[1]
    d_extended, d_taps, d_bias = conv_pull(jnp.concatenate([d_inner_input, d_own], axis=1))
    spill = passed_along(d_extended[: CONV - 1], CTX, -1)
    d_mixed = jnp.concatenate(
        [d_extended[CONV - 1 : item_count], d_extended[item_count:] + spill], axis=0
    )
    d_proj_b = jnp.concatenate(
        [
            rotate(d_query, cosine, -sine),
            rotate(d_pair[:, :HD], cosine, -sine),
            d_pair[:, HD:],
            d_gate_z,
            d_mixed,
            d_drive,
            jnp.zeros((item_count, IN_PAD - IN_COLS), jnp.float32),
        ],
        axis=1,
    ).astype(jnp.bfloat16)
    grad_in = jnp.einsum(
        "td,tc->dc", hidden_b, d_proj_b, preferred_element_type=jnp.float32
    ).astype(jnp.bfloat16)
    d_hidden = feature_sum(
        jnp.einsum("tc,dc->td", d_proj_b, w_in_b, preferred_element_type=jnp.float32)
    )
    d_state_norm, d_gain_mix = jax.vjp(rms_norm, state, gains[0])[1](d_hidden)
    d_vector = jnp.concatenate(
        [
            d_taps.reshape(-1),
            d_bias,
            d_gated_gain,
            d_a_log,
            d_dt_bias,
            d_skip_grad,
        ]
    )
    return (
        d_middle + d_state_norm,
        (grad_in, grad_out_proj),
        early,
        waiting,
        d_vector,
        jnp.stack([d_gain_mix, d_gain_mlp]),
    )


def adamw(weight, first_m, second_m, grad, rate, decay):
    first_new = beta_one * first_m + (1.0 - beta_one) * grad
    second_new = beta_two * second_m + (1.0 - beta_two) * grad * grad
    ratio = (
        first_new
        / (1.0 - beta_one**STEP)
        / (jnp.sqrt(second_new / (1.0 - beta_two**STEP)) + adam_eps)
    )
    return (first_new, second_new, weight - rate * (ratio + decay * weight))


def per_device(
    block_input,
    cotangent,
    lengths,
    w_in,
    w_out,
    w_gu,
    w_down,
    vectors,
    norm_gains,
    first_in,
    first_out,
    first_gu,
    first_down,
    first_vectors,
    first_gains,
    second_in,
    second_out,
    second_gu,
    second_down,
    second_vectors,
    second_gains,
):
    group_count = lax.axis_size("tp")
    widths = (
        HEADS * HD // group_count,
        KV_HEADS * HD // group_count,
        MAMBA_HEADS * MAMBA_HEAD_SIZE // group_count,
        2 * MAMBA_STATE_SIZE // group_count,
        MAMBA_HEADS // group_count,
    )
    item_count = block_input.shape[0]
    start_row = lax.axis_index(CTX) * item_count
    doc_row = lengths[0]
    segment, position = doc_layout(doc_row, start_row, item_count)
    seg_ext = doc_layout(doc_row, start_row - (CONV - 1), item_count + CONV - 1)[0]
    query_index = start_row + jnp.arange(item_count, dtype=jnp.int32)
    cosine, sine = rope_tables(position)
    lowest, highest_key = (query_index - position)[None, :], query_index[None, :]
    context = (segment, position, seg_ext, cosine, sine, lowest, highest_key)
    stored = []
    state = block_input
    fetched = fetch_layers(w_in, w_out, w_gu, w_down)
    for layer_at in range(LAYERS):
        weights = fetched[layer_at]
        state, kept = layer_forward(
            state, weights, vectors[layer_at, 0], norm_gains[layer_at], context, widths
        )
        stored.append(kept)
    grad_state = cotangent
    early_parts = [None] * LAYERS
    waiting = None
    small_parts = [None] * LAYERS
    vec = vectors.shape[-1]
    for layer_at in reversed(range(LAYERS)):
        grad_state, late, early, waiting, d_vector, d_gains = layer_backward(
            grad_state,
            stored[layer_at],
            fetched[layer_at],
            vectors[layer_at, 0],
            norm_gains[layer_at],
            context,
            widths,
            waiting,
        )
        if layer_at:
            grad_state, early = lax.optimization_barrier((grad_state, early))
            waiting = lax.psum_scatter(late[0], "fsdp", tiled=True)
        else:
            late_parts = (late, waiting)
        early_parts[layer_at] = early
        small_parts[layer_at] = jnp.concatenate([d_vector, d_gains.reshape(-1)])
    small = jnp.concatenate(small_parts)
    span = -(-small.shape[0] // 1024) * 8
    small = jnp.pad(small, (0, span * 128 - small.shape[0])).reshape(span, 128)
    *pieces, small = scatter_gradients(
        late_parts[0], (early_parts[1], late_parts[1], early_parts[0]), small
    )
    joined = jnp.concatenate(pieces[10:], axis=1)
    shards = [
        (
            jnp.concatenate(pieces[:3], axis=1)[:, :IN_COLS],
            joined[:, : 2 * D],
            jnp.concatenate([pieces[4], pieces[5], pieces[3]], axis=1).T,
            joined[:, 2 * D :].T,
        ),
        (
            jnp.concatenate(pieces[8:10], axis=1)[:, :IN_COLS],
            pieces[6],
            pieces[7][:, D:].T,
            pieces[7][:, :D].T,
        ),
    ]
    small_grads = small.reshape(-1)[: LAYERS * (vec + 2 * D)].reshape(LAYERS, vec + 2 * D)
    grad_in_all = jnp.stack([p[0] for p in shards]).reshape(w_in.shape)
    grad_gu_all = jnp.stack([p[1] for p in shards]).reshape(w_gu.shape)
    grad_out_all = jnp.stack([p[2] for p in shards]).reshape(w_out.shape)
    grad_down_all = jnp.stack([p[3] for p in shards]).reshape(w_down.shape)
    vector_total = small_grads[:, :vec].reshape(vectors.shape)
    gain_total = small_grads[:, vec:].reshape(norm_gains.shape)
    up_in = adamw(w_in, first_in, second_in, grad_in_all, rate_matrix, decay_rate)
    up_out = adamw(w_out, first_out, second_out, grad_out_all, rate_matrix, decay_rate)
    up_gu = adamw(w_gu, first_gu, second_gu, grad_gu_all, rate_matrix, decay_rate)
    up_down = adamw(w_down, first_down, second_down, grad_down_all, rate_matrix, decay_rate)
    up_vec = adamw(vectors, first_vectors, second_vectors, vector_total, rate_vector, 0.0)
    up_gain = adamw(norm_gains, first_gains, second_gains, gain_total, rate_vector, 0.0)
    return (
        state,
        grad_state,
        up_in[0],
        up_in[1],
        up_in[2],
        up_out[0],
        up_out[1],
        up_out[2],
        up_gu[0],
        up_gu[1],
        up_gu[2],
        up_down[0],
        up_down[1],
        up_down[2],
        up_vec[0],
        up_vec[1],
        up_vec[2],
        up_gain[0],
        up_gain[1],
        up_gain[2],
    )


def solution(mesh):
    torus = Mesh(
        mesh.devices.reshape(mesh.shape["fsdp"], 4, 4, mesh.shape["tp"]),
        ("fsdp", "ctx_0", "ctx_1", "tp"),
    )
    in_specs = (
        P(FSDP_CTX, None),
        P(FSDP_CTX, None),
        P("fsdp", None),
        P(None, FSDP_CTX, "tp", None),
        P(None, "tp", None, FSDP_CTX),
        P(None, FSDP_CTX, "tp", None),
        P(None, "tp", None, FSDP_CTX),
        P(None, "tp", None),
        P(),
        P(None, FSDP_CTX, "tp", None),
        P(None, "tp", None, FSDP_CTX),
        P(None, FSDP_CTX, "tp", None),
        P(None, "tp", None, FSDP_CTX),
        P(None, "tp", None),
        P(),
        P(None, FSDP_CTX, "tp", None),
        P(None, "tp", None, FSDP_CTX),
        P(None, FSDP_CTX, "tp", None),
        P(None, "tp", None, FSDP_CTX),
        P(None, "tp", None),
        P(),
    )
    out_specs = (
        P(FSDP_CTX, None),
        P(FSDP_CTX, None),
        P(None, FSDP_CTX, "tp", None),
        P(None, FSDP_CTX, "tp", None),
        P(None, FSDP_CTX, "tp", None),
        P(None, "tp", None, FSDP_CTX),
        P(None, "tp", None, FSDP_CTX),
        P(None, "tp", None, FSDP_CTX),
        P(None, FSDP_CTX, "tp", None),
        P(None, FSDP_CTX, "tp", None),
        P(None, FSDP_CTX, "tp", None),
        P(None, "tp", None, FSDP_CTX),
        P(None, "tp", None, FSDP_CTX),
        P(None, "tp", None, FSDP_CTX),
        P(None, "tp", None),
        P(None, "tp", None),
        P(None, "tp", None),
        P(),
        P(),
        P(),
    )
    return jax.shard_map(
        per_device, mesh=torus, in_specs=in_specs, out_specs=out_specs, check_vma=False
    )
```
